32 devices in a mesh: dp: 4 (over z), seq: 8 (over y, x, core).
Axes of the slice: x: 2, y: 2, z: 4, core: 2. Of those that a mesh axis runs over, the one named last changes fastest.
Arguments:
- hidden_in: bfloat16 [4, 1024, 2048], P('dp', 'seq'), may hold values from -6 to 6
- segments: int32 [4, 1024], P('dp', 'seq'), may hold values from 0 to 254, as said below
- attn_weights: bfloat16 [2048, 8192], P(('dp', 'seq')), may hold values from -0.125 to 0.125
- q_gain: bfloat16 [2048], P(('dp', 'seq')), may hold values from 0.25 to 1.75
- k_gain: bfloat16 [2048], P(('dp', 'seq')), may hold values from 0.25 to 1.75
- attn_gain: bfloat16 [2048], P(('dp', 'seq')), may hold values from 0.25 to 1.75
- ffn_gain: bfloat16 [2048], P(('dp', 'seq')), may hold values from 0.25 to 1.75
- gate_up_weights: bfloat16 [2048, 16384], P(('dp', 'seq')), may hold values from -0.125 to 0.125
- down_weights: bfloat16 [8192, 2048], P(('dp', 'seq')), may hold values from -0.0625 to 0.0625
- cotangent: bfloat16 [4, 1024, 2048], P('dp', 'seq'), may hold values from -6 to 6
Outputs:
- output: bfloat16 [4, 1024, 2048], P('dp', 'seq')
- input_grad: float32 [4, 1024, 2048], P('dp', 'seq')
- grad_attn_weights: float32 [2048, 8192], P(('dp', 'seq'))
- grad_gate_up: float32 [2048, 16384], P(('dp', 'seq'))
- grad_down: float32 [8192, 2048], P(('dp', 'seq'))
- grad_q_gain: float32 [2048], P(('dp', 'seq'))
- grad_k_gain: float32 [2048], P(('dp', 'seq'))
- grad_attn_gain: float32 [2048], P(('dp', 'seq'))
- grad_ffn_gain: float32 [2048], P(('dp', 'seq'))
The draws below stay inside these ranges and needn't reach their ends.
Inputs may be any that keep to these rules, and one draw needn't show every extreme that they name: `segments`: segment numbers start at 0 in each sequence and never fall. In each sequence one document begins at a position between 1 and 127 and ends at a position between 896 and 1022; every other document is shorter than 128 tokens.
All inputs are finite; a program needn't handle non-finite values.
Results may differ from the reference program's by a relative error of at most 0.03.
Values may be sent and summed in bfloat16 or wider, within the bound.
A program may use at most 512 MiB of HBM per device.

```python
import jax
import jax.numpy as jnp
from jax import lax

D = 2048
FF = 8192
HEAD = 128
TOK_DEV = 128
SEQS = 4
SEQ_LEN = 1024


def draw_segments(key, part):
    key = jax.random.fold_in(key, 11)
    key_first, key_last, key_extra, key_pick = jax.random.split(key, 4)
    chosen = jax.random.randint(key_pick, (), 0, SEQS)
    fullest = jnp.arange(SEQS, dtype=jnp.int32)[:, None] == chosen
    opening = jax.random.randint(key_first, (SEQS, 1), 1, TOK_DEV)
    closing = SEQ_LEN - jax.random.randint(key_last, (SEQS, 1), 1, TOK_DEV)
    opening = jnp.where(fullest, TOK_DEV - 1, opening)
    closing = jnp.where(fullest, SEQ_LEN - TOK_DEV + 1, closing)
    places = jnp.arange(SEQ_LEN, dtype=jnp.int32)[None, :]
    extra = (jax.random.randint(key_extra, (SEQS, SEQ_LEN), 0, 4) == 0) | fullest
    outside = (places < opening) | (places > closing)
    starts = (places == opening) | (places == closing) | extra & outside
    starts = starts & (places > 0)
    return jnp.cumsum(starts.astype(jnp.int32), axis=1).astype(jnp.int32)


def shard_levels(own_key, extent, shards, least, largest):
    loudness, own = 1.0, jax.random.fold_in(own_key, 6)
    for dim, blocks in shards:
        heights = jnp.exp(jax.random.uniform(jax.random.fold_in(own, dim), (blocks,), jnp.float32, least / len(shards), largest / len(shards)))
        loudness = loudness * jnp.repeat(heights, extent[dim] // blocks).reshape([-1 if axis == dim else 1 for axis in range(len(extent))])
    return loudness


def normal_values(rng, dims, scale, bound, shards=(), held_as=jnp.bfloat16):
    array = jax.random.normal(rng, dims, jnp.float32) * scale
    if len(shards) > 0:
        array = shard_levels(rng, dims, shards, -0.22, 0.18) * array
    return jnp.clip(array, min=-bound, max=bound).astype(held_as)


def setup_inputs(seed: int = 0) -> dict:
    splits = jax.random.split(jax.random.key(seed), 11)
    return {
        "hidden_in": normal_values(splits[0], (SEQS, SEQ_LEN, D), 1.0, 6.0, ((0, 4), (1, 8))),
        "segments": draw_segments(jax.random.fold_in(splits[10], 71), 0),
        "attn_weights": normal_values(splits[2], (D, 4 * D), D ** -0.5, 0.125, ((0, 32),)),
        "q_gain": jnp.clip(1.0 + 0.15 * jax.random.normal(splits[3], (D,), jnp.float32), 0.25, 1.75).astype(jnp.bfloat16),
        "k_gain": jnp.clip(1.0 + 0.15 * jax.random.normal(splits[4], (D,), jnp.float32), 0.25, 1.75).astype(jnp.bfloat16),
        "attn_gain": jnp.clip(1.0 + 0.15 * jax.random.normal(splits[5], (D,), jnp.float32), 0.25, 1.75).astype(jnp.bfloat16),
        "ffn_gain": jnp.clip(1.0 + 0.15 * jax.random.normal(splits[6], (D,), jnp.float32), 0.25, 1.75).astype(jnp.bfloat16),
        "gate_up_weights": normal_values(splits[7], (D, 2 * FF), D ** -0.5, 0.125, ((0, 32),)),
        "down_weights": normal_values(splits[8], (FF, D), FF ** -0.5, 0.0625, ((0, 32),)),
        "cotangent": normal_values(splits[9], (SEQS, SEQ_LEN, D), 1.0, 6.0, ((0, 4), (1, 8))),
    }


epsilon = 1e-06
rope_base = 500000.0

@jax.custom_vjp
def low(v):
    return lax.optimization_barrier(v.astype(jnp.bfloat16)).astype(jnp.float32)

@jax.custom_vjp
def low_back(v):
    return v

def low_keep(v):
    return (low(v), None)

def low_pass(kept, grad):
    return (grad,)

def back_keep(v):
    return (v, None)

def back_low(kept, grad):
    return (low(grad),)
low.defvjp(low_keep, low_pass)
low_back.defvjp(back_keep, back_low)

def rms_gain(values, gain):
    return values * lax.rsqrt(lax.optimization_barrier(jnp.mean(values * values, axis=-1, keepdims=True)) + epsilon) * gain

def rotate(values, positions):
    num_rows = values.shape[0]
    heads = values.shape[1] // HEAD
    half_dim = HEAD // 2
    frequency = rope_base ** (-2.0 * jnp.arange(half_dim, dtype=jnp.float32) / HEAD)
    angles = positions[:, None] * frequency[None, :]
    cosine = jnp.cos(angles)[:, None, :]
    sines = jnp.sin(angles)[:, None, :]
    pieces = values.reshape(num_rows, heads, HEAD)
    leading = pieces[..., :half_dim]
    trailing = pieces[..., half_dim:]
    turned = jnp.concatenate([leading * cosine - trailing * sines, trailing * cosine + leading * sines], axis=-1)
    return turned.reshape(num_rows, heads * HEAD)

def attend(queries, keys, values_in, doc_ids):
    highest = lax.Precision.HIGHEST
    length = queries.shape[0]
    width = queries.shape[1]
    heads = width // HEAD
    q_block = min(512, length)
    key_heads = keys.reshape(length, heads, HEAD)
    value_heads = values_in.reshape(length, heads, HEAD)
    key_index = jnp.arange(length, dtype=jnp.int32)

    def one_block(query_rows, row_start):
        query_heads = query_rows.reshape(q_block, heads, HEAD)
        scores = jnp.einsum('qhd,khd->hqk', query_heads, key_heads, precision=highest) * HEAD ** (-0.5)
        scores = low_back(scores)
        query_index = row_start + jnp.arange(q_block, dtype=jnp.int32)
        query_docs = lax.dynamic_slice_in_dim(doc_ids, row_start, q_block)
        allowed = (key_index[None, :] <= query_index[:, None]) & (doc_ids[None, :] == query_docs[:, None])
        masked = jnp.where(allowed[None], scores, -1e+30)
        weights = low(jax.nn.softmax(masked, axis=-1))
        mixed = jnp.einsum('hqk,khd->qhd', weights, value_heads, precision=highest)
        return mixed.reshape(q_block, width)
    checked = jax.checkpoint(one_block)
    starts = jnp.arange(length // q_block, dtype=jnp.int32) * q_block
    blocks = queries.reshape(length // q_block, q_block, width)
    result = lax.map(lambda pair: checked(pair[0], pair[1]), (blocks, starts))
    return result.reshape(length, width)

def forward(inputs, attn_w, q_g, k_g, attn_g, ffn_g, gu_w, down_w, doc_ids):
    highest = lax.Precision.HIGHEST
    seqs, length, width = inputs.shape
    flat = inputs.reshape(seqs * length, width)
    projected = low_back(jnp.dot(flat, attn_w[:, :3 * width], precision=highest))
    positions = jnp.tile(jnp.arange(length, dtype=jnp.float32), seqs)
    queries = low(rotate(rms_gain(projected[:, :width], q_g), positions))
    keys = low(rotate(rms_gain(projected[:, width:2 * width], k_g), positions))
    values_in = low(projected[:, 2 * width:])
    mixed = lax.map(lambda group: attend(group[0], group[1], group[2], group[3]), (queries.reshape(seqs, length, width), keys.reshape(seqs, length, width), values_in.reshape(seqs, length, width), doc_ids))
    mixed = low_back(low(mixed.reshape(seqs * length, width)))
    branch = low_back(jnp.dot(mixed, attn_w[:, 3 * width:], precision=highest))
    hidden = flat + rms_gain(branch, attn_g)
    gate_up = low_back(jnp.dot(low(hidden), gu_w, precision=highest))
    inner = gu_w.shape[1] // 2
    activated = low(jax.nn.silu(gate_up[:, :inner]) * gate_up[:, inner:])
    down = low_back(jnp.dot(activated, down_w, precision=highest))
    result = hidden + rms_gain(down, ffn_g)
    return result.reshape(seqs, length, width)

def reference(hidden_in, segments, attn_weights, q_gain, k_gain, attn_gain, ffn_gain, gate_up_weights, down_weights, cotangent):

    def closed(inputs, attn_w, q_g, k_g, attn_g, ffn_g, gu_w, down_w):
        return forward(inputs, attn_w, q_g, k_g, attn_g, ffn_g, gu_w, down_w, segments)
    output, pullback = jax.vjp(closed, hidden_in.astype(jnp.float32), attn_weights.astype(jnp.float32), q_gain.astype(jnp.float32), k_gain.astype(jnp.float32), attn_gain.astype(jnp.float32), ffn_gain.astype(jnp.float32), gate_up_weights.astype(jnp.float32), down_weights.astype(jnp.float32))
    grads = pullback(cotangent.astype(jnp.float32))
    return (output.astype(jnp.bfloat16), grads[0], grads[1], grads[6], grads[7], grads[2], grads[3], grads[4], grads[5])
```

```python
import functools

import jax
import jax.numpy as jnp
from jax import lax
from jax.experimental import pallas as pl
from jax.experimental.pallas import tpu as pltpu
from jax.sharding import PartitionSpec as P

HEAD = 128
epsilon = 1e-06
rope_base = 500000.0
MESH = pl.DeviceIdType.MESH
BF = jnp.bfloat16
F32 = jnp.float32
ANY = pl.BlockSpec(memory_space=pl.ANY)
VM = pl.BlockSpec(memory_space=pltpu.VMEM)
DMA = pltpu.SemaphoreType.DMA


class Plan:
    def __init__(self, mesh, heads):
        self.dp = mesh.shape["dp"]
        self.seq = mesh.shape["seq"]
        self.size = heads
        self.low = heads // self.seq
        self.groups = self.dp // self.low
        self.devices = self.dp * self.seq

    def here(self):
        dp = lax.axis_index("dp")
        seq = lax.axis_index("seq")
        return dp, seq, (dp % self.low) * self.seq + seq

    def member(self, dp, index):
        return (dp // self.low) * self.low + index // self.seq, index % self.seq

    def across(self, dp, seq, bit):
        if bit < self.seq:
            return dp, flip(seq, bit)
        return flip(dp, bit // self.seq), seq


def flip(value, bit):
    return value + bit * (1 - 2 * ((value // bit) % 2))


def flips(value, mask):
    bit = 1
    while bit <= mask:
        if mask & bit:
            value = flip(value, bit)
        bit *= 2
    return value


def greet(devices):
    barrier = pltpu.get_barrier_semaphore()
    for device in devices:
        pl.semaphore_signal(barrier, inc=1, device_id=device, device_id_type=MESH)
    pl.semaphore_wait(barrier, len(devices))


def greet_all(plan, dp, seq):
    barrier = pltpu.get_barrier_semaphore()
    me = dp * plan.seq + seq

    def hello(step, carry):
        other = (me + step) % plan.devices
        pl.semaphore_signal(
            barrier, inc=1, device_id=(other // plan.seq, other % plan.seq), device_id_type=MESH
        )
        return carry

    lax.fori_loop(1, plan.devices, hello, 0)
    pl.semaphore_wait(barrier, plan.devices - 1)


def greet_group(plan, dp, index):
    barrier = pltpu.get_barrier_semaphore()

    def hello(step, carry):
        other = plan.member(dp, (index + step) % plan.size)
        pl.semaphore_signal(barrier, inc=1, device_id=other, device_id_type=MESH)
        return carry

    lax.fori_loop(1, plan.size, hello, 0)
    pl.semaphore_wait(barrier, plan.size - 1)


def send(src, dst, send_sem, recv_sem, device):
    copy = pltpu.make_async_remote_copy(
        src_ref=src,
        dst_ref=dst,
        send_sem=send_sem,
        recv_sem=recv_sem,
        device_id=device,
        device_id_type=MESH,
    )
    copy.start()
    return copy


def wait_bytes(ref, sem):
    pltpu.make_async_copy(ref, ref, sem).wait()


def rows_of(rows):
    third = rows // 3 // 16 * 16
    first = (rows - third) // 2 // 16 * 16
    return ((0, first), (first, rows - third - first), (rows - third, third))


ORDERS = ((2, 4, 8), (4, 8, 2), (8, 2, 4))


def subsets(bits):
    masks = [0]
    for bit in bits:
        masks = masks + [mask | bit for mask in masks]
    return masks


def gather_steps(plan, x, out, dp, seq, index, sems):
    ici_send, ici_recv, core_send, core_recv, local = sems
    rows = x.shape[0]
    parts = rows_of(rows)
    copies = []

    def place(mask, part):
        start, count = parts[part]
        return out.at[pl.ds(flips(index, mask) * rows + start, count)]

    def source(mask, part):
        if mask == 0:
            start, count = parts[part]
            return x.at[pl.ds(start, count)]
        return place(mask, part)

    def slot(part, stage, mask):
        done = subsets(ORDERS[part][:stage])
        return part * 7 + 2**stage - 1 + done.index(mask)

    def forward(mask, part, stages):
        for stage in stages:
            bit = ORDERS[part][stage]
            number = slot(part, stage, mask)
            copies.append(
                send(
                    source(mask, part),
                    place(mask, part),
                    ici_send.at[number],
                    ici_recv.at[number],
                    plan.across(dp, seq, bit),
                )
            )

    def to_core(mask, part, number):
        copies.append(
            send(
                source(mask, part),
                place(mask, part),
                core_send.at[number],
                core_recv.at[number],
                plan.across(dp, seq, 1),
            )
        )

    def begin():
        pltpu.make_async_copy(x, out.at[pl.ds(index * rows, rows)], local).start()
        for stage in range(3):
            for part in range(3):
                forward(0, part, (stage,))
        for part in range(3):
            to_core(0, part, part)

    def finish():
        for stage in range(3):
            for part in range(3):
                bit = ORDERS[part][stage]
                for mask in subsets(ORDERS[part][:stage]):
                    number = slot(part, stage, mask)
                    arrived = place(mask | bit, part)
                    wait_bytes(arrived, ici_recv.at[number])
                    forward(mask | bit, part, range(stage + 1, 3))
                    to_core(mask | bit, part, 3 + number)
        for part in range(3):
            wait_bytes(place(1, part), core_recv.at[part])
            for stage in range(3):
                bit = ORDERS[part][stage]
                for mask in subsets(ORDERS[part][:stage]):
                    wait_bytes(place(1 | mask | bit, part), core_recv.at[3 + slot(part, stage, mask)])
        for copy in copies:
            copy.wait_send()
        pltpu.make_async_copy(x, out.at[pl.ds(index * rows, rows)], local).wait()

    return begin, finish


GATHER_SEMS = (DMA((21,)), DMA((21,)), DMA((24,)), DMA((24,)), DMA)


def gather_group(plan, x):
    rows, width = x.shape

    def kernel(x_ref, out_ref, *sems):
        dp, seq, index = plan.here()
        greet([plan.across(dp, seq, bit) for bit in (1, 2, 4, 8)])
        begin, finish = gather_steps(plan, x_ref, out_ref, dp, seq, index, sems)
        begin()
        finish()

    return pl.pallas_call(
        kernel,
        out_shape=jax.ShapeDtypeStruct((plan.size * rows, width), x.dtype),
        in_specs=[ANY],
        out_specs=ANY,
        scratch_shapes=list(GATHER_SEMS),
        compiler_params=pltpu.CompilerParams(collective_id=1, has_side_effects=True),
        name="gather_group",
    )(x)


def scatter_sum(plan, partial):
    rows = partial.shape[0] // plan.size
    width = partial.shape[1]
    parts = rows_of(rows)

    def kernel(p_ref, out_ref, total, got, *rest):
        stage_bufs = rest[:9]
        core_send, core_recv, ici_send, ici_recv, local = rest[9:]
        dp, seq, index = plan.here()
        greet([plan.across(dp, seq, bit) for bit in (1, 2, 4, 8)])
        copies = []
        loads = []
        order = sorted(range(8), key=lambda m: -bin(m).count("1"))
        for m in order:
            block = flips(index, 1 | (2 * m))
            copies.append(
                send(
                    p_ref.at[pl.ds(block * rows, rows)],
                    got.at[m],
                    core_send.at[m],
                    core_recv.at[m],
                    plan.across(dp, seq, 1),
                )
            )
            mine = pltpu.make_async_copy(
                p_ref.at[pl.ds(flips(index, 2 * m) * rows, rows)], total.at[m], local.at[m]
            )
            mine.start()
            loads.append((m, mine, copies[-1]))

        def add(dst, src, count):
            @pl.loop(0, count // 16)
            def _(i):
                here = pl.ds(i * 16, 16)
                dst[here, :] = (dst[here, :].astype(F32) + src[here, :].astype(F32)).astype(BF)

        for m, mine, copy in loads:
            mine.wait()
            copy.wait_recv()
            add(total.at[m], got.at[m], rows)
        for stage in (2, 1, 0):
            landed = []
            for part in range(3):
                start, count = parts[part]
                bit = ORDERS[part][stage]
                for k, mask in enumerate(subsets(ORDERS[part][:stage])):
                    number = part * 7 + 2**stage - 1 + k
                    buffer = stage_bufs[part * 3 + stage].at[k]
                    copy = send(
                        total.at[(mask | bit) // 2, pl.ds(start, count)],
                        buffer,
                        ici_send.at[number],
                        ici_recv.at[number],
                        plan.across(dp, seq, bit),
                    )
                    copies.append(copy)
                    landed.append((copy, mask, start, count, buffer))
            for copy, mask, start, count, buffer in landed:
                copy.wait_recv()
                if stage > 0:
                    add(total.at[mask // 2, pl.ds(start, count)], buffer, count)
                else:

                    @pl.loop(0, count // 16)
                    def _(i, start=start, buffer=buffer):
                        here = pl.ds(start + i * 16, 16)
                        out_ref[here, :] = total[0, here, :].astype(F32) + buffer[
                            pl.ds(i * 16, 16), :
                        ].astype(F32)

        for copy in copies:
            copy.wait_send()

    scratch = [pltpu.VMEM((8, rows, width), BF), pltpu.VMEM((8, rows, width), BF)]
    for part in range(3):
        for stage in range(3):
            scratch.append(pltpu.VMEM((2**stage, parts[part][1], width), BF))
    scratch += [DMA((8,)), DMA((8,)), DMA((21,)), DMA((21,)), DMA((8,))]
    return pl.pallas_call(
        kernel,
        out_shape=jax.ShapeDtypeStruct((rows, width), F32),
        in_specs=[ANY],
        out_specs=VM,
        scratch_shapes=scratch,
        compiler_params=pltpu.CompilerParams(
            collective_id=2, has_side_effects=True, vmem_limit_bytes=40 * 2**20
        ),
        name="scatter_sum",
    )(partial)


def start_gather(plan, x, attn_w, gains, docs):
    rows, width = x.shape
    own = attn_w.shape[0]
    per_head = HEAD // own

    def kernel(x_ref, w_ref, g_ref, d_ref, xo, wo, oo, go, do, *sems):
        gather_sems, (w_send, w_recv, o_send, o_recv, g_send, g_recv, d_send, d_recv, local) = (
            sems[:5],
            sems[5:],
        )
        dp, seq, index = plan.here()
        me = dp * plan.seq + seq
        greet_all(plan, dp, seq)
        begin, finish = gather_steps(plan, x_ref, xo, dp, seq, index, gather_sems)
        begin()
        group = dp // plan.low
        feature = me * own
        head = feature // HEAD
        o_dst = oo.at[pl.ds(pl.multiple_of(feature % HEAD, own), own)]
        o_src = w_ref.at[:, pl.ds(3 * width, width)]

        def columns(part, other):
            return pl.ds(pl.multiple_of(part * width + other * HEAD, HEAD), HEAD)

        mine = pl.ds(me * own, own)

        def w_to(away, step, carry):
            other = (index + step) % plan.size
            to_group = (group + away) % plan.groups
            device = (to_group * plan.low + other // plan.seq, other % plan.seq)
            for part in range(3):
                send(
                    w_ref.at[:, columns(part, other)],
                    wo.at[mine, pl.ds(part * HEAD, HEAD)],
                    w_send,
                    w_recv,
                    device,
                )
            return carry

        for away in range(1, plan.groups):
            lax.fori_loop(0, plan.size, functools.partial(w_to, away), 0)
        lax.fori_loop(1, plan.size, functools.partial(w_to, 0), 0)
        for part in range(3):
            pltpu.make_async_copy(
                w_ref.at[:, columns(part, index)], wo.at[mine, pl.ds(part * HEAD, HEAD)], w_recv
            ).start()

        def o_to(away, carry):
            to_group = (group + away) % plan.groups
            to_dp, to_seq = to_group * plan.low + head // plan.seq, head % plan.seq
            same = to_dp * plan.seq + to_seq == me

            @pl.when(same)
            def _():
                pltpu.make_async_copy(o_src, o_dst, o_recv).start()

            @pl.when(jnp.logical_not(same))
            def _():
                send(o_src, o_dst, o_send, o_recv, (to_dp, to_seq))

            return carry

        lax.fori_loop(0, plan.groups, o_to, 0)

        def g_to(step, carry):
            other = (me + step) % plan.devices
            send(g_ref, go.at[me], g_send, g_recv, (other // plan.seq, other % plan.seq))
            return carry

        lax.fori_loop(1, plan.devices, g_to, 0)
        pltpu.make_async_copy(g_ref, go.at[me], g_recv).start()

        def d_to(step, carry):
            send(d_ref, do.at[index], d_send, d_recv, plan.member(dp, (index + step) % plan.size))
            return carry

        lax.fori_loop(1, plan.size, d_to, 0)
        pltpu.make_async_copy(d_ref, do.at[index], d_recv).start()
        finish()
        wait_bytes(go, g_recv)
        wait_bytes(do, d_recv)
        wait_bytes(oo, o_recv)
        wait_bytes(wo, w_recv)

        def sent(step, carry):
            wait_bytes(w_ref.at[:, pl.ds(0, 3 * HEAD)], w_send)
            wait_bytes(g_ref, g_send)
            return carry

        lax.fori_loop(1, plan.devices, sent, 0)

        def sent_docs(step, carry):
            wait_bytes(d_ref, d_send)
            return carry

        lax.fori_loop(1, plan.size, sent_docs, 0)

        def sent_o(away, carry):
            to_group = (group + away) % plan.groups
            to_dp, to_seq = to_group * plan.low + head // plan.seq, head % plan.seq

            @pl.when(to_dp * plan.seq + to_seq != me)
            def _():
                wait_bytes(o_src, o_send)

            return carry

        lax.fori_loop(0, plan.groups, sent_o, 0)

    shapes = (
        ((plan.size * rows, width), BF),
        ((plan.devices * own, 3 * HEAD), BF),
        ((HEAD, width), BF),
        ((plan.devices,) + gains.shape, gains.dtype),
        ((plan.size,) + docs.shape, docs.dtype),
    )
    return pl.pallas_call(
        kernel,
        out_shape=[jax.ShapeDtypeStruct(*shape) for shape in shapes],
        in_specs=[ANY] * 4,
        out_specs=[ANY] * 5,
        scratch_shapes=list(GATHER_SEMS) + [DMA] * 9,
        compiler_params=pltpu.CompilerParams(collective_id=0, has_side_effects=True),
        name="start_gather",
    )(x, attn_w, gains, docs)


def column_blocks(plan, inner, blocks):
    wide = inner // blocks
    each = wide // plan.size
    table = []
    for half in range(2):
        for block in range(blocks):
            table.append((half * inner + block * wide, each, (half * blocks + block) * each))
    return table


def gate_up_columns(plan, weights, blocks):
    own, both = weights.shape
    table = column_blocks(plan, both // 2, blocks)
    each = table[0][1]
    mine_wide = both // plan.size

    def kernel(w_ref, out_ref, w_send, w_recv):
        dp, seq, index = plan.here()
        greet_group(plan, dp, index)
        rows = pl.ds(index * own, own)

        def to(step, carry):
            other = (index + step) % plan.size
            device = plan.member(dp, other)
            for base, each, place in table:
                send(
                    w_ref.at[:, pl.ds(pl.multiple_of(base + other * each, 128), each)],
                    out_ref.at[rows, pl.ds(place, each)],
                    w_send,
                    w_recv,
                    device,
                )
            return carry

        lax.fori_loop(1, plan.size, to, 0)
        for base, each, place in table:
            pltpu.make_async_copy(
                w_ref.at[:, pl.ds(pl.multiple_of(base + index * each, 128), each)],
                out_ref.at[rows, pl.ds(place, each)],
                w_recv,
            ).start()
        wait_bytes(out_ref, w_recv)

        def sent(step, carry):
            wait_bytes(w_ref.at[:, pl.ds(0, mine_wide)], w_send)
            return carry

        lax.fori_loop(1, plan.size, sent, 0)

    return pl.pallas_call(
        kernel,
        out_shape=jax.ShapeDtypeStruct((plan.size * own, mine_wide), BF),
        in_specs=[ANY],
        out_specs=ANY,
        scratch_shapes=[DMA, DMA],
        compiler_params=pltpu.CompilerParams(collective_id=3, has_side_effects=True),
        name="gate_up_columns",
    )(weights)


def give_back(plan, gate_up, qkv, out_rows, gains, blocks):
    own = gate_up.shape[0] // plan.size
    both = gate_up.shape[1] * plan.size
    width = out_rows.shape[1]
    table = column_blocks(plan, both // 2, blocks)

    def kernel(gu, qk, ow, ga, gu_out, qk_out, ow_out, ga_out, *sems):
        gu_s, gu_r, qk_s, qk_r, ow_s, ow_r, ga_s, ga_r = sems
        dp, seq, index = plan.here()
        me = dp * plan.seq + seq
        group = dp // plan.low
        greet_all(plan, dp, seq)

        def g_to(step, carry):
            other = (me + step) % plan.devices
            send(ga.at[other], ga_out.at[me], ga_s, ga_r, (other // plan.seq, other % plan.seq))
            return carry

        lax.fori_loop(1, plan.devices, g_to, 0)
        pltpu.make_async_copy(ga.at[me], ga_out.at[me], ga_r).start()
        pieces = HEAD // own

        def o_to(piece, carry):
            other = index * pieces + piece
            src = ow.at[pl.ds(pl.multiple_of(piece * own, own), own)]

            @pl.when(other == me)
            def _():
                pltpu.make_async_copy(src, ow_out.at[group], ow_r).start()

            @pl.when(other != me)
            def _():
                send(src, ow_out.at[group], ow_s, ow_r, (other // plan.seq, other % plan.seq))

            return carry

        lax.fori_loop(0, pieces, o_to, 0)

        def moves(other, rows):
            for base, each, place in table:
                yield (
                    gu.at[rows, pl.ds(place, each)],
                    gu_out.at[:, pl.ds(pl.multiple_of(base + index * each, 128), each)],
                    gu_s,
                    gu_r,
                )
            for part in range(3):
                yield (
                    qk.at[rows, pl.ds(part * HEAD, HEAD)],
                    qk_out.at[:, pl.ds(pl.multiple_of(part * width + index * HEAD, 128), HEAD)],
                    qk_s,
                    qk_r,
                )

        def to(step, carry):
            other = (index + step) % plan.size
            device = plan.member(dp, other)
            for src, dst, s, r in moves(other, pl.ds(pl.multiple_of(other * own, own), own)):
                send(src, dst, s, r, device)
            return carry

        lax.fori_loop(1, plan.size, to, 0)
        for src, dst, s, r in moves(index, pl.ds(pl.multiple_of(index * own, own), own)):
            pltpu.make_async_copy(src, dst, r).start()
        wait_bytes(gu_out, gu_r)
        wait_bytes(qk_out, qk_r)
        wait_bytes(ow_out, ow_r)
        wait_bytes(ga_out, ga_r)

        def sent(step, carry):
            wait_bytes(gu.at[pl.ds(0, own)], gu_s)
            wait_bytes(qk.at[pl.ds(0, own)], qk_s)
            return carry

        lax.fori_loop(1, plan.size, sent, 0)

        def sent_gains(step, carry):
            wait_bytes(ga.at[0], ga_s)
            return carry

        lax.fori_loop(1, plan.devices, sent_gains, 0)

        def sent_o(piece, carry):
            @pl.when(index * pieces + piece != me)
            def _():
                wait_bytes(ow.at[pl.ds(0, own)], ow_s)

            return carry

        lax.fori_loop(0, pieces, sent_o, 0)

    shapes = (
        ((own, both), BF),
        ((own, 3 * width), BF),
        ((plan.groups, own, width), BF),
        (gains.shape, F32),
    )
    return pl.pallas_call(
        kernel,
        out_shape=[jax.ShapeDtypeStruct(*shape) for shape in shapes],
        in_specs=[ANY] * 4,
        out_specs=[ANY] * 4,
        scratch_shapes=[DMA] * 8,
        compiler_params=pltpu.CompilerParams(collective_id=4, has_side_effects=True),
        name="give_back",
    )(gate_up, qkv, out_rows, gains)


def sum_group(plan, values):
    def kernel(v_ref, out_ref, held, s_sem, r_sem):
        dp, seq, index = plan.here()
        greet_group(plan, dp, index)

        def to(step, carry):
            send(v_ref, held.at[step - 1], s_sem, r_sem, plan.member(dp, (index + step) % plan.size))
            return carry

        lax.fori_loop(1, plan.size, to, 0)
        wait_bytes(held, r_sem)
        wait_bytes(held, s_sem)
        total = v_ref[...]
        for i in range(plan.size - 1):
            total = total + held[i]
        out_ref[...] = total

    return pl.pallas_call(
        kernel,
        out_shape=jax.ShapeDtypeStruct(values.shape, F32),
        in_specs=[VM],
        out_specs=VM,
        scratch_shapes=[pltpu.VMEM((plan.size - 1,) + values.shape, F32), DMA, DMA],
        compiler_params=pltpu.CompilerParams(collective_id=5, has_side_effects=True),
        name="sum_group",
    )(values)


def dot(left, right):
    return jnp.dot(left, right, preferred_element_type=F32)


def contract_last(left, right):
    return lax.dot_general(left, right, (((1,), (1,)), ((), ())), preferred_element_type=F32)


def contract_first(left, right):
    return lax.dot_general(left, right, (((0,), (0,)), ((), ())), preferred_element_type=F32)


Q_BLOCK = 256


def scores_of(q, k, q_docs, k_docs):
    start = pl.program_id(1) * Q_BLOCK
    scores = contract_last(q, k) * HEAD ** (-0.5)
    row = start + lax.broadcasted_iota(jnp.int32, scores.shape, 0)
    column = lax.broadcasted_iota(jnp.int32, scores.shape, 1)
    allowed = (column <= row) & (q_docs == k_docs)
    scores = jnp.where(allowed, scores, -1e30)
    top = jnp.max(scores, axis=1, keepdims=True)
    weights = jnp.exp(scores - top)
    return weights / jnp.sum(weights, axis=1, keepdims=True)


def attend(q, k, v, docs_column, docs_row, length):
    def kernel(q_ref, k_ref, v_ref, qd_ref, kd_ref, o_ref):
        probs = scores_of(q_ref[...], k_ref[...], qd_ref[...], kd_ref[0])
        o_ref[...] = dot(probs.astype(BF), v_ref[...]).astype(BF)

    total = q.shape[0]
    steps = length // Q_BLOCK
    by_query = pl.BlockSpec((Q_BLOCK, HEAD), lambda i, j: (i * steps + j, 0))
    by_key = pl.BlockSpec((length, HEAD), lambda i, j: (i, 0))
    return pl.pallas_call(
        kernel,
        grid=(total // length, steps),
        out_shape=jax.ShapeDtypeStruct((total, HEAD), BF),
        in_specs=[
            by_query,
            by_key,
            by_key,
            pl.BlockSpec((Q_BLOCK, 1), lambda i, j: (i * steps + j, 0)),
            pl.BlockSpec((1, 1, length), lambda i, j: (i, 0, 0)),
        ],
        out_specs=by_query,
        compiler_params=pltpu.CompilerParams(vmem_limit_bytes=40 * 2**20),
        name="attend",
    )(q, k, v, docs_column, docs_row)


def attend_back(q, k, v, grad, docs_column, docs_row, length):
    def kernel(q_ref, k_ref, v_ref, g_ref, qd_ref, kd_ref, dq_ref, dk_ref, dv_ref):
        @pl.when(pl.program_id(1) == 0)
        def _():
            dk_ref[...] = jnp.zeros_like(dk_ref)
            dv_ref[...] = jnp.zeros_like(dv_ref)

        probs = scores_of(q_ref[...], k_ref[...], qd_ref[...], kd_ref[0])
        grad_probs = contract_last(g_ref[...], v_ref[...])
        delta = jnp.sum(probs * grad_probs, axis=1, keepdims=True)
        grad_scores = (probs * (grad_probs - delta)).astype(BF)
        scale = HEAD ** (-0.5)
        dq_ref[...] = dot(grad_scores, k_ref[...]) * scale
        dk_ref[...] += contract_first(grad_scores, q_ref[...]) * scale
        dv_ref[...] += contract_first(probs.astype(BF), g_ref[...])

    total = q.shape[0]
    steps = length // Q_BLOCK
    by_query = pl.BlockSpec((Q_BLOCK, HEAD), lambda i, j: (i * steps + j, 0))
    by_key = pl.BlockSpec((length, HEAD), lambda i, j: (i, 0))
    return pl.pallas_call(
        kernel,
        grid=(total // length, steps),
        out_shape=[jax.ShapeDtypeStruct((total, HEAD), F32)] * 3,
        in_specs=[
            by_query,
            by_key,
            by_key,
            by_query,
            pl.BlockSpec((Q_BLOCK, 1), lambda i, j: (i * steps + j, 0)),
            pl.BlockSpec((1, 1, length), lambda i, j: (i, 0, 0)),
        ],
        out_specs=[by_query, by_key, by_key],
        compiler_params=pltpu.CompilerParams(vmem_limit_bytes=40 * 2**20),
        name="attend_back",
    )(q, k, v, grad, docs_column, docs_row)


def per_device(
    plan,
    hidden_in,
    segments,
    attn_weights,
    q_gain,
    k_gain,
    attn_gain,
    ffn_gain,
    gate_up_weights,
    down_weights,
    cotangent,
):
    x = hidden_in[0]
    rows, width = x.shape
    own = attn_weights.shape[0]
    inner = gate_up_weights.shape[1] // 2
    length = rows * plan.seq
    tokens = rows * plan.size
    groups = plan.groups
    dp, seq, index = plan.here()
    me = dp * plan.seq + seq
    group = dp // plan.low
    direct = (inner // (groups * plan.size)) % 128 == 0
    blocks = groups if direct else 1

    def from_group(value, away):
        step = away * plan.low
        return lax.ppermute(value, "dp", [(i, (i + step) % plan.dp) for i in range(plan.dp)])

    def join_groups(value):
        whole = jnp.zeros((groups,) + value.shape, value.dtype)
        whole = lax.dynamic_update_index_in_dim(whole, value, group, 0)
        for away in range(1, groups):
            other = from_group(value, away)
            whole = lax.dynamic_update_index_in_dim(whole, other, (group - away) % groups, 0)
        return whole

    def sum_groups(value):
        total = lax.dynamic_index_in_dim(value, group, 0, keepdims=False)
        for away in range(1, groups):
            theirs = lax.dynamic_index_in_dim(value, (group + away) % groups, 0, keepdims=False)
            total = total + from_group(theirs.astype(BF), away).astype(F32)
        return total

    gains_mine = jnp.stack([q_gain, k_gain, attn_gain, ffn_gain]).astype(F32)
    gains_mine = jnp.pad(gains_mine, ((0, 4), (0, 128 - own)))
    docs_mine = jnp.broadcast_to(segments, (8, rows))
    x_all, w_qkv, w_out, gains_all, docs_all = start_gather(
        plan, x, attn_weights, gains_mine, docs_mine
    )
    gains = jnp.transpose(gains_all[:, :4, :own], (1, 0, 2)).reshape(4, width)
    docs = docs_all[:, 0, :].reshape(tokens)
    docs_column = docs.reshape(tokens, 1)
    docs_row = docs.reshape(tokens // length, 1, length)
    w_gu_part = gate_up_columns(plan, gate_up_weights, blocks)
    if direct:
        w_down = join_groups(down_weights).reshape(inner // plan.size, width)
    else:
        w_all = lax.all_gather(down_weights, ("dp", "seq"), axis=0, tiled=True)
        each = inner // plan.size
        w_down = lax.dynamic_slice_in_dim(w_all, index * each, each, 0)
    w_gu = join_groups(w_gu_part).reshape(width, 2 * inner // plan.size)

    qkv = dot(x_all, w_qkv)
    q, k, v = qkv[:, :HEAD], qkv[:, HEAD : 2 * HEAD], qkv[:, 2 * HEAD :]
    my_gains = lax.dynamic_slice_in_dim(gains[:2], index * HEAD, HEAD, 1)
    q_g, k_g = my_gains[0], my_gains[1]

    def over_group(first, second):
        both = jnp.stack([first, second]).reshape(2 * tokens // 128, 128)
        both = sum_group(plan, both).reshape(2, tokens, 1)
        return both[0], both[1]

    q_sum, k_sum = over_group(jnp.sum(q * q, axis=1), jnp.sum(k * k, axis=1))
    q_r = lax.rsqrt(q_sum / width + epsilon)
    k_r = lax.rsqrt(k_sum / width + epsilon)
    positions = (jnp.arange(tokens, dtype=jnp.int32) % length).astype(F32)
    half = HEAD // 2
    frequency = rope_base ** (-2.0 * jnp.arange(half, dtype=F32) / HEAD)
    angles = positions[:, None] * frequency[None, :]
    cosine = jnp.concatenate([jnp.cos(angles)] * 2, axis=1)
    sine = jnp.concatenate([-jnp.sin(angles), jnp.sin(angles)], axis=1)

    def turn(values, sine):
        swapped = jnp.concatenate([values[:, half:], values[:, :half]], axis=1)
        return values * cosine + swapped * sine

    q_low = turn(q * q_r * q_g, sine).astype(BF)
    k_low = turn(k * k_r * k_g, sine).astype(BF)
    v_low = v.astype(BF)
    mixed = attend(q_low, k_low, v_low, docs_column, docs_row, length)
    branch = scatter_sum(plan, dot(mixed, w_out).astype(BF))

    def rms(values):
        return lax.rsqrt(jnp.mean(values * values, axis=1, keepdims=True) + epsilon)

    def rms_back(values, r, gain, grad):
        scaled = gain * grad
        inner_sum = jnp.mean(scaled * values, axis=1, keepdims=True)
        return r * scaled - values * (r * r * r * inner_sum), jnp.sum(grad * values * r, axis=0)

    branch_r = rms(branch)
    hidden = x.astype(F32) + branch * branch_r * gains[2]
    hidden_low = hidden.astype(BF)

    h_all = gather_group(plan, hidden_low)
    gate_up = dot(h_all, w_gu)
    mine = inner // plan.size
    gate, up = gate_up[:, :mine], gate_up[:, mine:]
    act = (jax.nn.silu(gate) * up).astype(BF)
    down = scatter_sum(plan, dot(act, w_down).astype(BF))
    down_r = rms(down)
    output = (hidden + down * down_r * gains[3]).astype(BF)

    grad_out = cotangent[0].astype(F32)
    grad_down_in, grad_fg = rms_back(down, down_r, gains[3], grad_out)
    d_all = gather_group(plan, grad_down_in.astype(BF))
    grad_act = contract_last(d_all, w_down)
    sigma = jax.nn.sigmoid(gate)
    grad_gate = grad_act * up * sigma * (1.0 + gate * (1.0 - sigma))
    grad_up = grad_act * (gate * sigma)
    gu_low = jnp.concatenate([grad_gate, grad_up], axis=1).astype(BF)
    g_down = contract_first(act, d_all)
    if direct:
        grad_down = sum_groups(g_down.reshape(groups, mine // groups, width))
    else:
        spread = jnp.zeros((inner, width), BF)
        spread = lax.dynamic_update_slice_in_dim(spread, g_down.astype(BF), index * mine, 0)
        grad_down = lax.psum_scatter(
            spread, ("dp", "seq"), scatter_dimension=0, tiled=True
        ).astype(F32)
    grad_hidden = grad_out + scatter_sum(plan, contract_last(gu_low, w_gu).astype(BF))
    g_gu = contract_first(h_all, gu_low)
    g_gu = sum_groups(g_gu.reshape(groups, width // groups, 2 * mine)).astype(BF)

    grad_branch, grad_ag = rms_back(branch, branch_r, gains[2], grad_hidden)
    b_all = gather_group(plan, grad_branch.astype(BF))
    grad_mixed = contract_last(b_all, w_out).astype(BF)
    g_out = contract_first(mixed, b_all).astype(BF)
    dqr, dkr, dv = attend_back(q_low, k_low, v_low, grad_mixed, docs_column, docs_row, length)
    dq_n = turn(dqr, -sine)
    dk_n = turn(dkr, -sine)
    q_dot, k_dot = over_group(
        jnp.sum(dq_n * q_g * q, axis=1), jnp.sum(dk_n * k_g * k, axis=1)
    )

    def norm_back(grad, values, r, gain, total):
        return r * (gain * grad) - values * (r * r * r * (total / width))

    dq = norm_back(dq_n, q, q_r, q_g, q_dot)
    dk = norm_back(dk_n, k, k_r, k_g, k_dot)
    grad_qg = jnp.sum(dq_n * q * q_r, axis=0)
    grad_kg = jnp.sum(dk_n * k * k_r, axis=0)
    qkv_low = jnp.concatenate([dq, dk, dv], axis=1).astype(BF)
    input_grad = grad_hidden + scatter_sum(plan, contract_last(qkv_low, w_qkv).astype(BF))
    g_qkv = contract_first(x_all, qkv_low)
    g_qkv = sum_groups(g_qkv.reshape(groups, width // groups, 3 * HEAD)).astype(BF)

    def for_head(values):
        whole = jnp.zeros((width,), F32)
        return lax.dynamic_update_slice_in_dim(whole, values, index * HEAD, 0)

    gain_parts = jnp.stack([for_head(grad_qg), for_head(grad_kg), grad_ag, grad_fg])
    gain_parts = jnp.transpose(gain_parts.reshape(4, plan.devices, own), (1, 0, 2))
    gain_parts = jnp.pad(gain_parts, ((0, 0), (0, 4), (0, 128 - own)))
    gu_rows, qkv_rows, out_rows, gain_rows = give_back(
        plan, g_gu, g_qkv, g_out, gain_parts, blocks
    )
    grad_gate_up = gu_rows.astype(F32)
    grad_attn = jnp.concatenate(
        [qkv_rows.astype(F32), jnp.sum(out_rows.astype(F32), axis=0)], axis=1
    )
    gain_grads = jnp.sum(gain_rows, axis=0)[:4, :own]
    return (
        output[None],
        input_grad[None],
        grad_attn,
        grad_gate_up,
        grad_down,
        gain_grads[0],
        gain_grads[1],
        gain_grads[2],
        gain_grads[3],
    )


def solution(mesh):
    by_token = P("dp", "seq", None)
    by_row = P(("dp", "seq"), None)
    by_gain = P(("dp", "seq"))

    def run(hidden_in, segments, attn_weights, *rest):
        plan = Plan(mesh, hidden_in.shape[2] // HEAD)
        return jax.shard_map(
            functools.partial(per_device, plan),
            mesh=mesh,
            in_specs=(by_token, P("dp", "seq"), by_row)
            + (by_gain,) * 4
            + (by_row, by_row, by_token),
            out_specs=(by_token, by_token, by_row, by_row, by_row) + (by_gain,) * 4,
            check_vma=False,
        )(hidden_in, segments, attn_weights, *rest)

    return run
```

```python
import functools

import jax
import jax.numpy as jnp
from jax import lax
from jax.experimental import pallas as pl
from jax.experimental.pallas import tpu as pltpu
from jax.sharding import PartitionSpec as P

HEAD = 128
epsilon = 1e-06
rope_base = 500000.0
MESH = pl.DeviceIdType.MESH
BF = jnp.bfloat16
F32 = jnp.float32
ANY = pl.BlockSpec(memory_space=pl.ANY)
VM = pl.BlockSpec(memory_space=pltpu.VMEM)
DMA = pltpu.SemaphoreType.DMA
LIGHT = pl.CostEstimate(flops=0, bytes_accessed=0, transcendentals=0)


class Plan:
    def __init__(self, mesh, heads):
        self.dp = mesh.shape["dp"]
        self.seq = mesh.shape["seq"]
        self.size = heads
        self.low = heads // self.seq
        self.groups = self.dp // self.low
        self.devices = self.dp * self.seq

    def here(self):
        dp = lax.axis_index("dp")
        seq = lax.axis_index("seq")
        return dp, seq, (dp % self.low) * self.seq + seq

    def member(self, dp, index):
        return (dp // self.low) * self.low + index // self.seq, index % self.seq

    def across(self, dp, seq, bit):
        if bit < self.seq:
            return dp, flip(seq, bit)
        return flip(dp, bit // self.seq), seq


def flip(value, bit):
    return value + bit * (1 - 2 * ((value // bit) % 2))


def flips(value, mask):
    bit = 1
    while bit <= mask:
        if mask & bit:
            value = flip(value, bit)
        bit *= 2
    return value


def greet(devices):
    barrier = pltpu.get_barrier_semaphore()
    for device in devices:
        pl.semaphore_signal(barrier, inc=1, device_id=device, device_id_type=MESH)
    pl.semaphore_wait(barrier, len(devices))


def greet_all(plan, dp, seq):
    barrier = pltpu.get_barrier_semaphore()
    me = dp * plan.seq + seq

    def hello(step, carry):
        other = (me + step) % plan.devices
        pl.semaphore_signal(
            barrier, inc=1, device_id=(other // plan.seq, other % plan.seq), device_id_type=MESH
        )
        return carry

    lax.fori_loop(1, plan.devices, hello, 0)
    pl.semaphore_wait(barrier, plan.devices - 1)


def greet_group(plan, dp, index):
    barrier = pltpu.get_barrier_semaphore()

    def hello(step, carry):
        other = plan.member(dp, (index + step) % plan.size)
        pl.semaphore_signal(barrier, inc=1, device_id=other, device_id_type=MESH)
        return carry

    lax.fori_loop(1, plan.size, hello, 0)
    pl.semaphore_wait(barrier, plan.size - 1)


def send(src, dst, send_sem, recv_sem, device):
    copy = pltpu.make_async_remote_copy(
        src_ref=src,
        dst_ref=dst,
        send_sem=send_sem,
        recv_sem=recv_sem,
        device_id=device,
        device_id_type=MESH,
    )
    copy.start()
    return copy


def wait_bytes(ref, sem):
    pltpu.make_async_copy(ref, ref, sem).wait()


def halves(rows):
    return ((0, rows // 2), (rows // 2, rows - rows // 2))


ORDERS = ((2, 4), (4, 2))


def gather_steps(plan, x, out, dp, seq, index, sems):
    far_send, far_recv, near_send, near_recv, core_send, core_recv, local = sems
    rows = x.shape[0]
    parts = halves(rows)
    copies = []

    def place(mask, part=None):
        start, count = (0, rows) if part is None else parts[part]
        return out.at[pl.ds(pl.multiple_of(flips(index, mask) * rows + start, 16), count)]

    def push(src, dst, send_sem, recv_sem, bit):
        copies.append(send(src, dst, send_sem, recv_sem, plan.across(dp, seq, bit)))

    def spread(src, mask):
        plane = mask // 8
        for bit in (2, 4):
            number = plane * 2 + bit // 4
            push(src, place(mask), near_send.at[number], near_recv.at[number], bit)
        push(src, place(mask), core_send.at[plane], core_recv.at[plane], 1)

    def begin():
        pltpu.make_async_copy(x, out.at[pl.ds(index * rows, rows)], local).start()
        push(x, place(0), far_send, far_recv, 8)
        spread(x, 0)

    def onward(plane):
        base = plane * 8
        for bit, other in ORDERS:
            number = plane * 2 + bit // 4
            wait_bytes(place(base | bit), near_recv.at[number])
            part = bit // 4
            push(
                place(base | bit, part),
                place(base | bit, part),
                near_send.at[4 + number],
                near_recv.at[4 + number],
                other,
            )
            push(
                place(base | bit),
                place(base | bit),
                core_send.at[2 + number],
                core_recv.at[2 + number],
                1,
            )

    def corner(plane):
        base = plane * 8
        for bit, _ in ORDERS:
            part = bit // 4
            number = plane * 2 + part
            wait_bytes(place(base | 6, part), near_recv.at[4 + number])
            push(
                place(base | 6, part),
                place(base | 6, part),
                core_send.at[6 + number],
                core_recv.at[6 + number],
                1,
            )

    def finish():
        onward(0)
        wait_bytes(place(8), far_recv)
        spread(place(8), 8)
        corner(0)
        onward(1)
        corner(1)
        for plane in range(2):
            base = plane * 8 + 1
            wait_bytes(place(base), core_recv.at[plane])
            for bit, _ in ORDERS:
                number = plane * 2 + bit // 4
                wait_bytes(place(base | bit), core_recv.at[2 + number])
                wait_bytes(place(base | 6, bit // 4), core_recv.at[6 + number])
        for copy in copies:
            copy.wait_send()
        pltpu.make_async_copy(x, out.at[pl.ds(index * rows, rows)], local).wait()

    return begin, finish


GATHER_SEMS = (DMA, DMA, DMA((8,)), DMA((8,)), DMA((10,)), DMA((10,)), DMA)


def gather_group(plan, x):
    rows, width = x.shape

    def kernel(x_ref, out_ref, *sems):
        dp, seq, index = plan.here()
        greet([plan.across(dp, seq, bit) for bit in (1, 2, 4, 8)])
        begin, finish = gather_steps(plan, x_ref, out_ref, dp, seq, index, sems)
        begin()
        finish()

    return pl.pallas_call(
        kernel,
        out_shape=jax.ShapeDtypeStruct((plan.size * rows, width), x.dtype),
        in_specs=[ANY],
        out_specs=ANY,
        scratch_shapes=list(GATHER_SEMS),
        compiler_params=pltpu.CompilerParams(collective_id=1, has_side_effects=True),
        cost_estimate=LIGHT,
        name="gather_group",
    )(x)


def scatter_steps(plan, dp, seq, index, pairs, turned, write, bufs, sems, meanwhile=None):
    theirs, mine, got_core, got_first, got_second, got_far = bufs
    core_send, core_recv, send_sems, recv_sems, far_send, far_recv = sems
    rows, width = got_far.shape
    tile = 512
    parts = halves(rows)
    copies = []

    def compute(dst, plane, core):
        starts = [flips(index, core | 2 * m | 8 * plane) * rows for m in range(4)]

        @pl.loop(0, width // tile)
        def _(j):
            columns = pl.ds(pl.multiple_of(j * tile, tile), tile)
            block = None
            for l_ref, r_ref in pairs:
                some = jnp.concatenate(
                    [l_ref[pl.ds(pl.multiple_of(start, rows), rows), :] for start in starts], axis=0
                )
                if turned:
                    part = contract_last(some, r_ref[columns, :])
                else:
                    part = dot(some, r_ref[:, columns])
                block = part if block is None else block + part
            dst[plane, :, :, columns] = block.astype(BF).reshape(4, rows, tile)

    def push(src, dst, send_sem, recv_sem, bit):
        copy = send(src, dst, send_sem, recv_sem, plan.across(dp, seq, bit))
        copies.append(copy)
        return copy

    def add(dst, src, count):
        @pl.loop(0, count // 16)
        def _(i):
            here = pl.ds(pl.multiple_of(i * 16, 16), 16)
            dst[here, :] = dst[here, :] + src[here, :]

    def to_core(plane):
        return push(
            theirs.at[plane], got_core.at[plane], core_send.at[plane], core_recv.at[plane], 1
        )

    def add_core(plane, copy):
        copy.wait_recv()
        for m in range(4):
            add(mine.at[plane, m], got_core.at[plane, m], rows)

    def first(plane):
        started = []
        for part, (bit, other) in enumerate(ORDERS):
            start, count = parts[part]
            for k, keep in enumerate((0, other)):
                number = plane * 6 + part * 2 + k
                buffer = got_first.at[plane, part * 2 + k]
                copy = push(
                    mine.at[plane, (keep | bit) // 2, pl.ds(start, count)],
                    buffer,
                    send_sems.at[number],
                    recv_sems.at[number],
                    bit,
                )
                started.append((copy, keep // 2, start, count, buffer))
        return started

    def second(plane):
        started = []
        for part, (bit, other) in enumerate(ORDERS):
            start, count = parts[part]
            number = plane * 6 + 4 + part
            buffer = got_second.at[plane, part]
            copy = push(
                mine.at[plane, other // 2, pl.ds(start, count)],
                buffer,
                send_sems.at[number],
                recv_sems.at[number],
                other,
            )
            started.append((copy, 0, start, count, buffer))
        return started

    def settle(plane, started):
        for copy, m, start, count, buffer in started:
            copy.wait_recv()
            add(mine.at[plane, m, pl.ds(start, count)], buffer, count)

    compute(theirs, 1, 1)
    core = to_core(1)
    compute(mine, 1, 0)
    add_core(1, core)
    far_first = first(1)
    compute(theirs, 0, 1)
    core = to_core(0)
    compute(mine, 0, 0)
    settle(1, far_first)
    far_second = second(1)
    add_core(0, core)
    near_first = first(0)
    if meanwhile is not None:
        meanwhile()
    settle(1, far_second)
    far = push(mine.at[1, 0], got_far, far_send, far_recv, 8)
    settle(0, near_first)
    near_second = second(0)
    settle(0, near_second)
    far.wait_recv()

    @pl.loop(0, rows // 16)
    def _(i):
        here = pl.ds(pl.multiple_of(i * 16, 16), 16)
        write(here, mine[0, 0, here, :].astype(F32) + got_far[here, :].astype(F32))

    for copy in copies:
        copy.wait_send()


def scatter_scratch(rows, width):
    block = (rows, width)
    half = (rows // 2, width)
    return [
        pltpu.VMEM((2, 4) + block, BF),
        pltpu.VMEM((2, 4) + block, BF),
        pltpu.VMEM((2, 4) + block, BF),
        pltpu.VMEM((2, 4) + half, BF),
        pltpu.VMEM((2, 2) + half, BF),
        pltpu.VMEM(block, BF),
        DMA((2,)),
        DMA((2,)),
        DMA((12,)),
        DMA((12,)),
        DMA,
        DMA,
    ]


def scatter_dot(plan, lefts, rights, turned, collective_id):
    rows = lefts[0].shape[0] // plan.size
    width = rights[0].shape[0] if turned else rights[0].shape[1]
    count = len(lefts)

    def kernel(*refs):
        pairs = list(zip(refs[:count], refs[count : 2 * count]))
        out_ref = refs[2 * count]
        rest = refs[2 * count + 1 :]
        dp, seq, index = plan.here()
        greet([plan.across(dp, seq, bit) for bit in (1, 2, 4, 8)])

        def write(here, value):
            out_ref[here, :] = value

        scatter_steps(plan, dp, seq, index, pairs, turned, write, rest[:6], rest[6:])

    return pl.pallas_call(
        kernel,
        out_shape=jax.ShapeDtypeStruct((rows, width), F32),
        in_specs=[VM] * (2 * count),
        out_specs=VM,
        scratch_shapes=scatter_scratch(rows, width),
        compiler_params=pltpu.CompilerParams(
            collective_id=collective_id, has_side_effects=True, vmem_limit_bytes=48 * 2**20
        ),
        cost_estimate=LIGHT,
        name="scatter_dot",
    )(*lefts, *rights)


def half_columns(plan, inner, blocks, half):
    wide = inner // blocks
    each = wide // plan.size
    return [(half * inner + block * wide, each, block * each) for block in range(blocks)]


def columns_out(plan, dp, index, w_ref, out_ref, table, send_sem, recv_sem):
    own = w_ref.shape[0]
    wide = out_ref.shape[1]
    rows = pl.ds(pl.multiple_of(index * own, own), own)

    def moves(other):
        for base, each, place in table:
            yield (
                w_ref.at[:, pl.ds(pl.multiple_of(base + other * each, 128), each)],
                out_ref.at[rows, pl.ds(place, each)],
            )

    def begin():
        def to(step, carry):
            other = (index + step) % plan.size
            for src, dst in moves(other):
                send(src, dst, send_sem, recv_sem, plan.member(dp, other))
            return carry

        lax.fori_loop(1, plan.size, to, 0)
        for src, dst in moves(index):
            pltpu.make_async_copy(src, dst, recv_sem).start()

    def finish():
        wait_bytes(out_ref, recv_sem)

        def sent(step, carry):
            wait_bytes(w_ref.at[:, pl.ds(0, wide)], send_sem)
            return carry

        lax.fori_loop(1, plan.size, sent, 0)

    return begin, finish


def columns_back(plan, dp, index, g_ref, out_ref, table, send_sem, recv_sem):
    own = g_ref.shape[0] // plan.size

    def moves(other):
        rows = pl.ds(pl.multiple_of(other * own, own), own)
        for base, each, place in table:
            yield (
                g_ref.at[rows, pl.ds(place, each)],
                out_ref.at[:, pl.ds(pl.multiple_of(base + index * each, 128), each)],
            )

    def begin():
        def to(step, carry):
            other = (index + step) % plan.size
            for src, dst in moves(other):
                send(src, dst, send_sem, recv_sem, plan.member(dp, other))
            return carry

        lax.fori_loop(1, plan.size, to, 0)
        for src, dst in moves(index):
            pltpu.make_async_copy(src, dst, recv_sem).start()

    def finish():
        wait_bytes(g_ref, recv_sem)

        def sent(step, carry):
            wait_bytes(g_ref.at[pl.ds(0, own)], send_sem)
            return carry

        lax.fori_loop(1, plan.size, sent, 0)

    return begin, finish


def start_gather(plan, x, attn_w, gate_up_w, gains, docs, blocks):
    rows, width = x.shape
    own, both = gate_up_w.shape
    table = half_columns(plan, both // 2, blocks, 0)

    def kernel(x_ref, w_ref, u_ref, g_ref, d_ref, xo, wo, uo, go, do, *sems):
        gather_sems = sems[:7]
        w_send, w_recv, u_send, u_recv, g_send, g_recv, d_send, d_recv = sems[7:]
        dp, seq, index = plan.here()
        me = dp * plan.seq + seq
        greet_all(plan, dp, seq)
        begin, finish = gather_steps(plan, x_ref, xo, dp, seq, index, gather_sems)
        begin()
        group = dp // plan.low
        def columns(part, other):
            return pl.ds(pl.multiple_of(part * width + other * HEAD, HEAD), HEAD)

        mine = pl.ds(me * own, own)

        def w_to(away, step, carry):
            other = (index + step) % plan.size
            to_group = (group + away) % plan.groups
            device = (to_group * plan.low + other // plan.seq, other % plan.seq)
            for part in range(3):
                send(
                    w_ref.at[:, columns(part, other)],
                    wo.at[mine, pl.ds(part * HEAD, HEAD)],
                    w_send,
                    w_recv,
                    device,
                )
            return carry

        for away in range(1, plan.groups):
            lax.fori_loop(0, plan.size, functools.partial(w_to, away), 0)
        lax.fori_loop(1, plan.size, functools.partial(w_to, 0), 0)
        for part in range(3):
            pltpu.make_async_copy(
                w_ref.at[:, columns(part, index)], wo.at[mine, pl.ds(part * HEAD, HEAD)], w_recv
            ).start()

        def g_to(step, carry):
            other = (me + step) % plan.devices
            send(g_ref, go.at[me], g_send, g_recv, (other // plan.seq, other % plan.seq))
            return carry

        lax.fori_loop(1, plan.devices, g_to, 0)
        pltpu.make_async_copy(g_ref, go.at[me], g_recv).start()

        def d_to(step, carry):
            send(d_ref, do.at[index], d_send, d_recv, plan.member(dp, (index + step) % plan.size))
            return carry

        lax.fori_loop(1, plan.size, d_to, 0)
        pltpu.make_async_copy(d_ref, do.at[index], d_recv).start()
        begin_u, finish_u = columns_out(plan, dp, index, u_ref, uo, table, u_send, u_recv)
        begin_u()
        finish()
        finish_u()
        wait_bytes(go, g_recv)
        wait_bytes(do, d_recv)
        wait_bytes(wo, w_recv)

        def sent(step, carry):
            wait_bytes(w_ref.at[:, pl.ds(0, 3 * HEAD)], w_send)
            wait_bytes(g_ref, g_send)
            return carry

        lax.fori_loop(1, plan.devices, sent, 0)

        def sent_docs(step, carry):
            wait_bytes(d_ref, d_send)
            return carry

        lax.fori_loop(1, plan.size, sent_docs, 0)

    shapes = (
        ((plan.size * rows, width), BF),
        ((plan.devices * own, 3 * HEAD), BF),
        ((plan.size * own, both // 2 // plan.size), BF),
        ((plan.devices,) + gains.shape, gains.dtype),
        ((plan.size,) + docs.shape, docs.dtype),
    )
    return pl.pallas_call(
        kernel,
        out_shape=[jax.ShapeDtypeStruct(*shape) for shape in shapes],
        in_specs=[ANY] * 5,
        out_specs=[ANY] * 5,
        scratch_shapes=list(GATHER_SEMS) + [DMA] * 8,
        compiler_params=pltpu.CompilerParams(collective_id=0, has_side_effects=True),
        cost_estimate=LIGHT,
        name="start_gather",
    )(x, attn_w, gate_up_w, gains, docs)


def dot(left, right):
    return jnp.dot(left, right, preferred_element_type=F32)


def contract_last(left, right):
    return lax.dot_general(left, right, (((1,), (1,)), ((), ())), preferred_element_type=F32)


def contract_first(left, right):
    return lax.dot_general(left, right, (((0,), (0,)), ((), ())), preferred_element_type=F32)


def row_sums(values):
    ones = jnp.ones((8, values.shape[1]), F32)
    sums = lax.dot_general(
        ones,
        values,
        (((1,), (1,)), ((), ())),
        precision=lax.Precision.HIGHEST,
        preferred_element_type=F32,
    )
    return sums[:1]


def spread_sums(rows):
    ones = jnp.ones((rows.shape[0], HEAD), F32)
    return lax.dot_general(
        rows,
        ones,
        (((0,), (0,)), ((), ())),
        precision=lax.Precision.HIGHEST,
        preferred_element_type=F32,
    )


STEP = 256


def scores_of(q, k, q_docs, k_docs, start):
    scores = contract_last(q, k) * HEAD ** (-0.5)
    row = start + lax.broadcasted_iota(jnp.int32, scores.shape, 0)
    column = lax.broadcasted_iota(jnp.int32, scores.shape, 1)
    allowed = (column <= row) & (q_docs == k_docs)
    scores = jnp.where(allowed, scores, -1e30)
    top = jnp.max(scores, axis=1, keepdims=True)
    weights = jnp.exp(scores - top)
    return weights / jnp.sum(weights, axis=1, keepdims=True)


def swap_sums(plan, dp, index, mine, held, s_sem, r_sem):
    def begin():
        def to(step, carry):
            send(mine, held.at[index], s_sem, r_sem, plan.member(dp, (index + step) % plan.size))
            return carry

        pltpu.make_async_copy(mine, held.at[index], r_sem).start()
        lax.fori_loop(1, plan.size, to, 0)

    def finish():
        wait_bytes(held, r_sem)
        wait_bytes(held.at[pl.ds(0, plan.size - 1)], s_sem)

    return begin, finish


def attend_forward(
    plan, x_all, w_qkv, attn_w, gate_up_w, gains, docs_column, docs_row, cosine, sine, blocks
):
    tokens, width = x_all.shape
    length = cosine.shape[0]
    own, both = gate_up_w.shape
    table = half_columns(plan, both // 2, blocks, 1)

    def kernel(x, wq, aw, up, gn, dc, dr, cs, sn, wo, uo, q, k, rq, rk, ql, kl, vl, mixed, *rest):
        stats, held, t_send, t_recv, o_send, o_recv, u_send, u_recv = rest
        dp, seq, index = plan.here()
        me = dp * plan.seq + seq
        group = dp // plan.low
        greet_all(plan, dp, seq)
        @pl.loop(0, tokens // STEP)
        def _(i):
            rows = pl.ds(pl.multiple_of(i * STEP, STEP), STEP)
            block = dot(x[rows, :], wq[...])
            q[rows, :] = block[:, :HEAD]
            k[rows, :] = block[:, HEAD : 2 * HEAD]
            vl[rows, :] = block[:, 2 * HEAD :].astype(BF)
            stats[0, :, rows] = row_sums(block[:, :HEAD] * block[:, :HEAD])
            stats[1, :, rows] = row_sums(block[:, HEAD : 2 * HEAD] * block[:, HEAD : 2 * HEAD])

        begin, finish = swap_sums(plan, dp, index, stats, held, t_send, t_recv)
        begin()
        feature = me * own
        head = feature // HEAD
        o_dst = wo.at[pl.ds(pl.multiple_of(feature % HEAD, own), own)]
        o_src = aw.at[:, pl.ds(3 * width, width)]

        def o_to(away, carry):
            to_group = (group + away) % plan.groups
            to_dp, to_seq = to_group * plan.low + head // plan.seq, head % plan.seq
            same = to_dp * plan.seq + to_seq == me

            @pl.when(same)
            def _():
                pltpu.make_async_copy(o_src, o_dst, o_recv).start()

            @pl.when(jnp.logical_not(same))
            def _():
                send(o_src, o_dst, o_send, o_recv, (to_dp, to_seq))

            return carry

        lax.fori_loop(0, plan.groups, o_to, 0)
        begin_u, finish_u = columns_out(plan, dp, index, up, uo, table, u_send, u_recv)
        begin_u()
        finish()

        @pl.loop(0, tokens // STEP)
        def _(i):
            rows = pl.ds(pl.multiple_of(i * STEP, STEP), STEP)
            places = pl.ds(pl.multiple_of((i % (length // STEP)) * STEP, STEP), STEP)
            for which, raw, factor, low in ((0, q, rq, ql), (1, k, rk, kl)):
                r = lax.rsqrt(spread_sums(held[:, which, 0, rows]) / width + epsilon)
                factor[rows, :] = r
                values = raw[rows, :] * r * gn[which : which + 1, :]
                turned = values * cs[places, :] + pltpu.roll(values, HEAD // 2, 1) * sn[places, :]
                low[rows, :] = turned.astype(BF)

        @pl.loop(0, tokens // length)
        def _(b):
            for j in range(length // STEP):
                start = pl.multiple_of(b * length + j * STEP, STEP)
                rows = pl.ds(start, STEP)
                keys = pl.ds(pl.multiple_of(b * length, length), (j + 1) * STEP)
                probs = scores_of(
                    ql[rows, :], kl[keys, :], dc[rows, :], dr[b, :, : (j + 1) * STEP], j * STEP
                )
                mixed[rows, :] = dot(probs.astype(BF), vl[keys, :]).astype(BF)

        wait_bytes(wo, o_recv)
        finish_u()

        def sent_o(away, carry):
            to_group = (group + away) % plan.groups
            to_dp, to_seq = to_group * plan.low + head // plan.seq, head % plan.seq

            @pl.when(to_dp * plan.seq + to_seq != me)
            def _():
                wait_bytes(o_src, o_send)

            return carry

        lax.fori_loop(0, plan.groups, sent_o, 0)

    per_head = (tokens, HEAD)
    shapes = (
        ((HEAD, width), BF),
        ((plan.size * own, both // 2 // plan.size), BF),
        (per_head, F32),
        (per_head, F32),
        (per_head, F32),
        (per_head, F32),
        (per_head, BF),
        (per_head, BF),
        (per_head, BF),
        (per_head, BF),
    )
    return pl.pallas_call(
        kernel,
        out_shape=[jax.ShapeDtypeStruct(*shape) for shape in shapes],
        in_specs=[VM, VM, ANY, ANY] + [VM] * 5,
        out_specs=[ANY, ANY] + [VM] * 8,
        scratch_shapes=[
            pltpu.VMEM((2, 1, tokens), F32),
            pltpu.VMEM((plan.size, 2, 1, tokens), F32),
        ]
        + [DMA] * 6,
        compiler_params=pltpu.CompilerParams(
            collective_id=3, has_side_effects=True, vmem_limit_bytes=56 * 2**20
        ),
        cost_estimate=LIGHT,
        name="attend_forward",
    )(x_all, w_qkv, attn_w, gate_up_w, gains, docs_column, docs_row, cosine, sine)


def attend_backward(
    plan,
    b_all,
    w_out,
    q,
    k,
    rq,
    rk,
    ql,
    kl,
    vl,
    mixed,
    gains,
    docs_column,
    docs_row,
    cosine,
    sine,
    g_gate,
    g_up,
    blocks,
):
    tokens, width = b_all.shape
    own = g_gate.shape[0] // plan.size
    inner = g_gate.shape[1] * plan.size
    length = cosine.shape[0]
    scale = HEAD ** (-0.5)

    def kernel(*refs):
        ba, wo, q, k, rq, rk, ql, kl, vl, mx, gn, dc, dr, cs, sn, gg, gu = refs[:17]
        dqkv, g_out, g_gain, gu_out = refs[17:21]
        dq, dk, dv, gm, stats, held, t_send, t_recv, gg_send, gg_recv, gu_send, gu_recv = refs[21:]
        dp, seq, index = plan.here()
        greet_group(plan, dp, index)
        begin_g, finish_g = columns_back(
            plan, dp, index, gg, gu_out, half_columns(plan, inner, blocks, 0), gg_send, gg_recv
        )
        begin_u, finish_u = columns_back(
            plan, dp, index, gu, gu_out, half_columns(plan, inner, blocks, 1), gu_send, gu_recv
        )
        begin_g()
        begin_u()
        dk[...] = jnp.zeros_like(dk)
        dv[...] = jnp.zeros_like(dv)

        @pl.loop(0, tokens // STEP)
        def _(i):
            rows = pl.ds(pl.multiple_of(i * STEP, STEP), STEP)
            gm[rows, :] = contract_last(ba[rows, :], wo[...]).astype(BF)

        @pl.loop(0, tokens // length)
        def _(b):
            for j in range(length // STEP):
                rows = pl.ds(pl.multiple_of(b * length + j * STEP, STEP), STEP)
                keys = pl.ds(pl.multiple_of(b * length, length), (j + 1) * STEP)
                probs = scores_of(
                    ql[rows, :], kl[keys, :], dc[rows, :], dr[b, :, : (j + 1) * STEP], j * STEP
                )
                grad = gm[rows, :]
                grad_probs = contract_last(grad, vl[keys, :])
                delta = jnp.sum(probs * grad_probs, axis=1, keepdims=True)
                grad_scores = (probs * (grad_probs - delta)).astype(BF)
                dq[rows, :] = dot(grad_scores, kl[keys, :]) * scale
                dk[keys, :] += contract_first(grad_scores, ql[rows, :]) * scale
                dv[keys, :] += contract_first(probs.astype(BF), grad)

        @pl.loop(0, tokens // STEP)
        def _(i):
            rows = pl.ds(pl.multiple_of(i * STEP, STEP), STEP)
            places = pl.ds(pl.multiple_of((i % (length // STEP)) * STEP, STEP), STEP)
            for which, raw, grad in ((0, q, dq), (1, k, dk)):
                values = grad[rows, :]
                turned = values * cs[places, :] - pltpu.roll(values, HEAD // 2, 1) * sn[places, :]
                grad[rows, :] = turned
                stats[which, :, rows] = row_sums(turned * gn[which : which + 1, :] * raw[rows, :])

        begin, finish = swap_sums(plan, dp, index, stats, held, t_send, t_recv)
        begin()
        turned_mixed = mx[...].T

        @pl.loop(0, width // 512)
        def _(i):
            columns = pl.ds(pl.multiple_of(i * 512, 512), 512)
            g_out[:, columns] = dot(turned_mixed, ba[:, columns]).astype(BF)

        g_gain[...] = jnp.zeros_like(g_gain)
        finish()

        @pl.loop(0, tokens // STEP)
        def _(i):
            rows = pl.ds(pl.multiple_of(i * STEP, STEP), STEP)
            for which, raw, factor, grad in ((0, q, rq, dq), (1, k, rk, dk)):
                total = spread_sums(held[:, which, 0, rows])
                r = factor[rows, :]
                u = raw[rows, :]
                e = grad[rows, :]
                back = r * (gn[which : which + 1, :] * e) - u * (r * r * r * (total / width))
                dqkv[rows, pl.ds(which * HEAD, HEAD)] = back.astype(BF)
                g_gain[which : which + 1, :] += jnp.sum(e * u * r, axis=0, keepdims=True)
            dqkv[rows, pl.ds(2 * HEAD, HEAD)] = dv[rows, :].astype(BF)

        finish_g()
        finish_u()

    per_head = (tokens, HEAD)
    shapes = (
        ((tokens, 3 * HEAD), BF),
        ((HEAD, width), BF),
        ((8, HEAD), F32),
        ((own, 2 * inner), BF),
    )
    return pl.pallas_call(
        kernel,
        out_shape=[jax.ShapeDtypeStruct(*shape) for shape in shapes],
        in_specs=[VM] * 15 + [ANY] * 2,
        out_specs=[VM] * 3 + [ANY],
        scratch_shapes=[
            pltpu.VMEM(per_head, F32),
            pltpu.VMEM(per_head, F32),
            pltpu.VMEM(per_head, F32),
            pltpu.VMEM(per_head, BF),
            pltpu.VMEM((2, 1, tokens), F32),
            pltpu.VMEM((plan.size, 2, 1, tokens), F32),
        ]
        + [DMA] * 6,
        compiler_params=pltpu.CompilerParams(
            collective_id=4, has_side_effects=True, vmem_limit_bytes=56 * 2**20
        ),
        cost_estimate=LIGHT,
        name="attend_backward",
    )(
        b_all,
        w_out,
        q,
        k,
        rq,
        rk,
        ql,
        kl,
        vl,
        mixed,
        gains,
        docs_column,
        docs_row,
        cosine,
        sine,
        g_gate,
        g_up,
    )


def finish_backward(plan, dqkv, w_qkv, x_all, g_out, gains, before):
    tokens, width = x_all.shape
    own = width // plan.devices
    rows = tokens // plan.size
    pieces = HEAD // own
    tile = 256

    def kernel(dq, wq, x, go, ga, bf, ig, w_grad, ga_out, *rest):
        bufs, sems = rest[:6], rest[6:12]
        turned, gq, got_q, got_o = rest[12:16]
        q_s, q_r, o_s, o_r, ga_s, ga_r = rest[16:]
        dp, seq, index = plan.here()
        me = dp * plan.seq + seq
        group = dp // plan.low
        greet_all(plan, dp, seq)

        def device_of(flat):
            return flat // plan.seq, flat % plan.seq

        def o_to(piece, carry):
            other = index * pieces + piece
            src = go.at[pl.ds(pl.multiple_of(piece * own, own), own)]

            @pl.when(other == me)
            def _():
                pltpu.make_async_copy(src, got_o.at[group], o_r).start()

            @pl.when(other != me)
            def _():
                send(src, got_o.at[group], o_s, o_r, device_of(other))

            return carry

        def ga_to(step, carry):
            other = (me + step) % plan.devices
            send(ga.at[other], ga_out.at[me], ga_s, ga_r, device_of(other))
            return carry

        def weights():
            turned[...] = dq[...].T

            @pl.loop(0, width // tile)
            def _(i):
                columns = pl.ds(pl.multiple_of(i * tile, tile), tile)
                block = dot(turned[...], x[:, columns])
                gq[columns, :] = block.T.astype(BF)

                def q_to(piece, carry):
                    other = i * (tile // own) + piece
                    src = gq.at[pl.ds(pl.multiple_of(other * own, own), own)]

                    @pl.when(other == me)
                    def _():
                        pltpu.make_async_copy(src, got_q.at[group, index], q_r).start()

                    @pl.when(other != me)
                    def _():
                        send(src, got_q.at[group, index], q_s, q_r, device_of(other))

                    return carry

                lax.fori_loop(0, tile // own, q_to, 0)

            lax.fori_loop(0, pieces, o_to, 0)
            lax.fori_loop(1, plan.devices, ga_to, 0)
            pltpu.make_async_copy(ga.at[me], ga_out.at[me], ga_r).start()

        def write(here, value):
            ig[here, :] = bf[here, :] + value

        scatter_steps(plan, dp, seq, index, [(dq, wq)], True, write, bufs, sems, weights)
        wait_bytes(got_o, o_r)
        wait_bytes(got_q, q_r)
        for part in range(3):
            for member in range(plan.size):
                total = got_q[0, member, :, part * HEAD : (part + 1) * HEAD].astype(F32)
                for other in range(1, plan.groups):
                    total = total + got_q[
                        other, member, :, part * HEAD : (part + 1) * HEAD
                    ].astype(F32)
                w_grad[:, pl.ds(part * width + member * HEAD, HEAD)] = total
        total = got_o[0].astype(F32)
        for other in range(1, plan.groups):
            total = total + got_o[other].astype(F32)
        w_grad[:, pl.ds(3 * width, width)] = total
        wait_bytes(ga_out, ga_r)
        wait_bytes(ga_out.at[pl.ds(0, plan.devices - 1)], ga_s)
        wait_bytes(gq.at[pl.ds(0, width - own)], q_s)

        def sent_o(piece, carry):
            @pl.when(index * pieces + piece != me)
            def _():
                wait_bytes(go.at[pl.ds(0, own)], o_s)

            return carry

        lax.fori_loop(0, pieces, sent_o, 0)

    shapes = (
        ((rows, width), F32),
        ((own, 4 * width), F32),
        (gains.shape, F32),
    )
    return pl.pallas_call(
        kernel,
        out_shape=[jax.ShapeDtypeStruct(*shape) for shape in shapes],
        in_specs=[VM] * 6,
        out_specs=[VM] * 3,
        scratch_shapes=scatter_scratch(rows, width)
        + [
            pltpu.VMEM((3 * HEAD, tokens), BF),
            pltpu.VMEM((width, 3 * HEAD), BF),
            pltpu.VMEM((plan.groups, plan.size, own, 3 * HEAD), BF),
            pltpu.VMEM((plan.groups, own, width), BF),
        ]
        + [DMA] * 6,
        compiler_params=pltpu.CompilerParams(
            collective_id=5, has_side_effects=True, vmem_limit_bytes=60 * 2**20
        ),
        cost_estimate=LIGHT,
        name="finish_backward",
    )(dqkv, w_qkv, x_all, g_out, gains, before)


def per_device(
    plan,
    hidden_in,
    segments,
    attn_weights,
    q_gain,
    k_gain,
    attn_gain,
    ffn_gain,
    gate_up_weights,
    down_weights,
    cotangent,
):
    x = hidden_in[0]
    rows, width = x.shape
    own = attn_weights.shape[0]
    inner = gate_up_weights.shape[1] // 2
    length = rows * plan.seq
    tokens = rows * plan.size
    groups = plan.groups
    dp, seq, index = plan.here()
    me = dp * plan.seq + seq
    group = dp // plan.low
    direct = (inner // (groups * plan.size)) % 128 == 0
    blocks = groups if direct else 1

    across = [[low + high * plan.low for high in range(groups)] for low in range(plan.low)]

    def join_groups(value):
        return lax.all_gather(value, "dp", axis_index_groups=across, axis=0, tiled=True)

    def sum_groups(value):
        return lax.psum_scatter(
            value.astype(BF), "dp", axis_index_groups=across, scatter_dimension=0, tiled=True
        )

    gains_mine = jnp.stack([q_gain, k_gain, attn_gain, ffn_gain]).astype(F32)
    gains_mine = jnp.pad(gains_mine, ((0, 4), (0, 128 - own)))
    docs_mine = jnp.broadcast_to(segments, (8, rows))
    x_all, w_qkv, gate_part, gains_all, docs_all = start_gather(
        plan, x, attn_weights, gate_up_weights, gains_mine, docs_mine, blocks
    )
    w_gate = join_groups(gate_part)
    gains = jnp.transpose(gains_all[:, :4, :own], (1, 0, 2)).reshape(4, width)
    docs = docs_all[:, 0, :].reshape(tokens)
    docs_column = docs.reshape(tokens, 1)
    docs_row = docs.reshape(tokens // length, 1, length)
    my_gains = lax.dynamic_slice_in_dim(gains[:2], index * HEAD, HEAD, 1)
    positions = jnp.arange(length, dtype=jnp.int32).astype(F32)
    half = HEAD // 2
    frequency = rope_base ** (-2.0 * jnp.arange(half, dtype=F32) / HEAD)
    angles = positions[:, None] * frequency[None, :]
    cosine = jnp.concatenate([jnp.cos(angles)] * 2, axis=1)
    sine = jnp.concatenate([-jnp.sin(angles), jnp.sin(angles)], axis=1)

    w_out, up_part, q, k, rq, rk, q_low, k_low, v_low, mixed = attend_forward(
        plan,
        x_all,
        w_qkv,
        attn_weights,
        gate_up_weights,
        my_gains,
        docs_column,
        docs_row,
        cosine,
        sine,
        blocks,
    )
    w_up = join_groups(up_part)
    down_weights, _ = lax.optimization_barrier((down_weights, up_part))
    if direct:
        w_down = join_groups(down_weights)
    else:
        w_all = lax.all_gather(down_weights, ("dp", "seq"), axis=0, tiled=True)
        each = inner // plan.size
        w_down = lax.dynamic_slice_in_dim(w_all, index * each, each, 0)
    branch = scatter_dot(plan, [mixed], [w_out], False, 2)

    def rms(values):
        return lax.rsqrt(jnp.mean(values * values, axis=1, keepdims=True) + epsilon)

    def rms_back(values, r, gain, grad):
        scaled = gain * grad
        inner_sum = jnp.mean(scaled * values, axis=1, keepdims=True)
        return r * scaled - values * (r * r * r * inner_sum), jnp.sum(grad * values * r, axis=0)

    branch_r = rms(branch)
    hidden = x.astype(F32) + branch * branch_r * gains[2]
    hidden_low = hidden.astype(BF)

    h_all = gather_group(plan, hidden_low)
    mine = inner // plan.size
    gate = dot(h_all, w_gate)
    up = dot(h_all, w_up)
    act = (jax.nn.silu(gate) * up).astype(BF)
    down = scatter_dot(plan, [act], [w_down], False, 6)
    down_r = rms(down)
    output = (hidden + down * down_r * gains[3]).astype(BF)

    grad_out = cotangent[0].astype(F32)
    grad_down_in, grad_fg = rms_back(down, down_r, gains[3], grad_out)
    d_all = gather_group(plan, grad_down_in.astype(BF))
    grad_act = contract_last(d_all, w_down)
    sigma = jax.nn.sigmoid(gate)
    grad_gate = (grad_act * up * sigma * (1.0 + gate * (1.0 - sigma))).astype(BF)
    grad_up = (grad_act * (gate * sigma)).astype(BF)
    g_gate = contract_first(h_all, grad_gate).astype(BF)
    g_up = contract_first(h_all, grad_up).astype(BF)
    g_down = contract_first(act, d_all).astype(BF)
    grad_gate, grad_up, g_gate, g_up, g_down = lax.optimization_barrier(
        (grad_gate, grad_up, g_gate, g_up, g_down)
    )
    g_gate = sum_groups(g_gate)
    g_up = sum_groups(g_up)
    if direct:
        grad_down = sum_groups(g_down).astype(F32)
    else:
        spread = jnp.zeros((inner, width), BF)
        spread = lax.dynamic_update_slice_in_dim(spread, g_down, index * mine, 0)
        grad_down = lax.psum_scatter(
            spread, ("dp", "seq"), scatter_dimension=0, tiled=True
        ).astype(F32)
    grad_hidden = grad_out + scatter_dot(
        plan, [grad_gate, grad_up], [w_gate, w_up], True, 7
    )

    grad_branch, grad_ag = rms_back(branch, branch_r, gains[2], grad_hidden)
    b_all = gather_group(plan, grad_branch.astype(BF))
    dqkv, g_out, g_head, gu_rows = attend_backward(
        plan,
        b_all,
        w_out,
        q,
        k,
        rq,
        rk,
        q_low,
        k_low,
        v_low,
        mixed,
        my_gains,
        docs_column,
        docs_row,
        cosine,
        sine,
        g_gate,
        g_up,
        blocks,
    )

    def for_head(values):
        whole = jnp.zeros((width,), F32)
        return lax.dynamic_update_slice_in_dim(whole, values, index * HEAD, 0)

    gain_parts = jnp.stack([for_head(g_head[0]), for_head(g_head[1]), grad_ag, grad_fg])
    gain_parts = jnp.transpose(gain_parts.reshape(4, plan.devices, own), (1, 0, 2))
    gain_parts = jnp.pad(gain_parts, ((0, 0), (0, 4), (0, 128 - own)))
    input_grad, grad_attn, gain_rows = finish_backward(
        plan, dqkv, w_qkv, x_all, g_out, gain_parts, grad_hidden
    )
    grad_gate_up = gu_rows.astype(F32)
    gain_grads = jnp.sum(gain_rows, axis=0)[:4, :own]
    return (
        output[None],
        input_grad[None],
        grad_attn,
        grad_gate_up,
        grad_down,
        gain_grads[0],
        gain_grads[1],
        gain_grads[2],
        gain_grads[3],
    )


def solution(mesh):
    by_token = P("dp", "seq", None)
    by_row = P(("dp", "seq"), None)
    by_gain = P(("dp", "seq"))

    def run(hidden_in, segments, attn_weights, *rest):
        plan = Plan(mesh, hidden_in.shape[2] // HEAD)
        return jax.shard_map(
            functools.partial(per_device, plan),
            mesh=mesh,
            in_specs=(by_token, P("dp", "seq"), by_row)
            + (by_gain,) * 4
            + (by_row, by_row, by_token),
            out_specs=(by_token, by_token, by_row, by_row, by_row) + (by_gain,) * 4,
            check_vma=False,
        )(hidden_in, segments, attn_weights, *rest)

    return run
```

```python
import functools

import jax
import jax.numpy as jnp
import numpy as np
from jax import lax
from jax.experimental import pallas as pl
from jax.experimental.pallas import tpu as pltpu
from jax.sharding import PartitionSpec as P

HEAD = 128
epsilon = 1e-06
rope_base = 500000.0
MESH = pl.DeviceIdType.MESH
BF = jnp.bfloat16
F32 = jnp.float32
ANY = pl.BlockSpec(memory_space=pl.ANY)
VM = pl.BlockSpec(memory_space=pltpu.VMEM)
DMA = pltpu.SemaphoreType.DMA
LIGHT = pl.CostEstimate(flops=0, bytes_accessed=0, transcendentals=0)


class Plan:
    def __init__(self, mesh, heads):
        self.dp = mesh.shape["dp"]
        self.seq = mesh.shape["seq"]
        self.size = heads
        self.low = heads // self.seq
        self.groups = self.dp // self.low
        self.devices = self.dp * self.seq
        self.pieces = self.devices // heads

    def here(self):
        dp = lax.axis_index("dp")
        seq = lax.axis_index("seq")
        return dp, seq, (dp % self.low) * self.seq + seq

    def head(self, index):
        return index // 2 + (self.size // 2) * (index % 2)

    def of_head(self, head):
        return (head % (self.size // 2)) * 2 + head // (self.size // 2)

    def member(self, dp, index):
        return (dp // self.low) * self.low + index // self.seq, index % self.seq

    def across(self, dp, seq, bit):
        if bit < self.seq:
            return dp, flip(seq, bit)
        return flip(dp, bit // self.seq), seq


def flip(value, bit):
    return value + bit * (1 - 2 * ((value // bit) % 2))


def flips(value, mask):
    bit = 1
    while bit <= mask:
        if mask & bit:
            value = flip(value, bit)
        bit *= 2
    return value


def greet(devices):
    barrier = pltpu.get_barrier_semaphore()
    for device in devices:
        pl.semaphore_signal(barrier, inc=1, device_id=device, device_id_type=MESH)
    pl.semaphore_wait(barrier, len(devices))


def greet_all(plan, dp, seq):
    barrier = pltpu.get_barrier_semaphore()
    me = dp * plan.seq + seq

    def hello(step, carry):
        other = (me + step) % plan.devices
        pl.semaphore_signal(
            barrier, inc=1, device_id=(other // plan.seq, other % plan.seq), device_id_type=MESH
        )
        return carry

    lax.fori_loop(1, plan.devices, hello, 0)
    pl.semaphore_wait(barrier, plan.devices - 1)


def greet_group(plan, dp, index):
    barrier = pltpu.get_barrier_semaphore()

    def hello(step, carry):
        other = plan.member(dp, (index + step) % plan.size)
        pl.semaphore_signal(barrier, inc=1, device_id=other, device_id_type=MESH)
        return carry

    lax.fori_loop(1, plan.size, hello, 0)
    pl.semaphore_wait(barrier, plan.size - 1)


def send(src, dst, send_sem, recv_sem, device):
    copy = pltpu.make_async_remote_copy(
        src_ref=src,
        dst_ref=dst,
        send_sem=send_sem,
        recv_sem=recv_sem,
        device_id=device,
        device_id_type=MESH,
    )
    copy.start()
    return copy


def wait_bytes(ref, sem):
    pltpu.make_async_copy(ref, ref, sem).wait()


def halves(rows):
    return ((0, rows // 2), (rows // 2, rows - rows // 2))


ORDERS = ((2, 4), (4, 2))


def gather_steps(plan, x, out, dp, seq, index, sems):
    far_send, far_recv, near_send, near_recv, core_send, core_recv, local = sems
    rows = x.shape[0]
    parts = halves(rows)
    copies = []

    def place(mask, part=None):
        start, count = (0, rows) if part is None else parts[part]
        return out.at[pl.ds(pl.multiple_of(flips(index, mask) * rows + start, 16), count)]

    def push(src, dst, send_sem, recv_sem, bit):
        copies.append(send(src, dst, send_sem, recv_sem, plan.across(dp, seq, bit)))

    def near(mask, part, number, bit):
        push(place(mask, part), place(mask, part), near_send.at[number], near_recv.at[number], bit)

    def to_core(mask, part, number):
        push(place(mask, part), place(mask, part), core_send.at[number], core_recv.at[number], 1)

    def begin():
        pltpu.make_async_copy(x, out.at[pl.ds(index * rows, rows)], local).start()
        for part in range(2):
            start, count = parts[part]
            push(
                x.at[pl.ds(start, count)], place(0, part), far_send.at[part], far_recv.at[part], 8
            )
        for bit in (2, 4):
            push(x, place(0), near_send.at[bit // 4], near_recv.at[bit // 4], bit)
        push(x, place(0), core_send.at[0], core_recv.at[0], 1)

    def own_plane():
        for bit, other in ORDERS:
            part = bit // 4
            wait_bytes(place(bit), near_recv.at[part])
            near(bit, part, 2 + part, other)
            to_core(bit, None, 1 + part)
        for part in range(2):
            wait_bytes(place(8, part), far_recv.at[part])
            for bit in (2, 4):
                near(8, part, 4 + 2 * part + bit // 4, bit)
            to_core(8, part, 5 + part)
        for part in range(2):
            wait_bytes(place(6, part), near_recv.at[2 + part])
            to_core(6, part, 3 + part)
        wait_bytes(place(1), core_recv.at[0])
        for part in range(2):
            wait_bytes(place(1 | (2 + 2 * part)), core_recv.at[1 + part])
            wait_bytes(place(7, part), core_recv.at[3 + part])
        pltpu.make_async_copy(x, out.at[pl.ds(index * rows, rows)], local).wait()

    def other_plane():
        for part in range(2):
            for bit, other in ORDERS:
                wait_bytes(place(8 | bit, part), near_recv.at[4 + 2 * part + bit // 4])
                if part == bit // 4:
                    near(8 | bit, part, 8 + part, other)
                to_core(8 | bit, part, 7 + 2 * part + bit // 4)
        for part in range(2):
            wait_bytes(place(14, part), near_recv.at[8 + part])
            to_core(14, part, 11 + part)
        for part in range(2):
            wait_bytes(place(9, part), core_recv.at[5 + part])
            for bit in (2, 4):
                wait_bytes(place(9 | bit, part), core_recv.at[7 + 2 * part + bit // 4])
            wait_bytes(place(15, part), core_recv.at[11 + part])

    def finish(use=None):
        own_plane()
        if use is not None:
            use(0)
        other_plane()
        if use is not None:
            use(1)
        for copy in copies:
            copy.wait_send()

    return begin, finish


GATHER_SEMS = (DMA((2,)), DMA((2,)), DMA((10,)), DMA((10,)), DMA((13,)), DMA((13,)), DMA)


def scatter_steps(plan, dp, seq, index, pairs, turned, write, bufs, sems, meanwhile=None):
    theirs, mine, got_core, got_first, got_second, got_far = bufs
    core_send, core_recv, send_sems, recv_sems, far_send, far_recv = sems
    rows, width = got_far.shape
    tile = 512
    piece = rows // 4
    copies = []

    def compute(dst, plane, core, blocks):
        starts = [flips(index, core | 2 * m | 8 * plane) * rows for m in blocks]

        @pl.loop(0, width // tile)
        def _(j):
            columns = pl.ds(pl.multiple_of(j * tile, tile), tile)
            block = None
            for l_ref, offset, r_ref in pairs:
                depth = r_ref.shape[1] if turned else r_ref.shape[0]
                some = jnp.concatenate(
                    [
                        l_ref[pl.ds(pl.multiple_of(start, rows), rows), pl.ds(offset, depth)]
                        for start in starts
                    ],
                    axis=0,
                )
                if turned:
                    part = contract_last(some, r_ref[columns, :])
                else:
                    part = dot(some, r_ref[:, columns])
                block = part if block is None else block + part
            block = block.astype(BF)
            for i, m in enumerate(blocks):
                dst[plane, m, :, columns] = block[i * rows : (i + 1) * rows]

    def push(src, dst, send_sem, recv_sem, bit):
        copy = send(src, dst, send_sem, recv_sem, plan.across(dp, seq, bit))
        copies.append(copy)
        return copy

    def add(dst, src, count):
        @pl.loop(0, count // 16)
        def _(i):
            here = pl.ds(pl.multiple_of(i * 16, 16), 16)
            dst[here, :] = dst[here, :] + src[here, :]

    def to_core(plane, blocks):
        started = []
        for m in blocks:
            number = plane * 4 + m
            started.append(
                (
                    push(
                        theirs.at[plane, m],
                        got_core.at[plane, m],
                        core_send.at[number],
                        core_recv.at[number],
                        1,
                    ),
                    m,
                )
            )
        return started

    def add_core(plane, started):
        for copy, m in started:
            copy.wait_recv()
            add(mine.at[plane, m], got_core.at[plane, m], rows)

    def start_of(chunk, part):
        return (chunk * 2 + part) * piece

    def first(plane, chunk):
        started = []
        for part, (bit, other) in enumerate(ORDERS):
            here = pl.ds(start_of(chunk, part), piece)
            for k, keep in enumerate((other, 0)):
                number = (plane * 2 + chunk) * 6 + part * 2 + k
                buffer = got_first.at[plane, chunk, part * 2 + k]
                copy = push(
                    mine.at[plane, (keep | bit) // 2, here],
                    buffer,
                    send_sems.at[number],
                    recv_sems.at[number],
                    bit,
                )
                started.append((copy, keep // 2, here, buffer))
        return started

    def second(plane, chunk):
        started = []
        for part, (bit, other) in enumerate(ORDERS):
            here = pl.ds(start_of(chunk, part), piece)
            number = (plane * 2 + chunk) * 6 + 4 + part
            buffer = got_second.at[plane, chunk, part]
            copy = push(
                mine.at[plane, other // 2, here],
                buffer,
                send_sems.at[number],
                recv_sems.at[number],
                other,
            )
            started.append((copy, 0, here, buffer))
        return started

    def far(chunk):
        here = pl.ds(chunk * 2 * piece, 2 * piece)
        return push(
            mine.at[1, 0, here], got_far.at[here], far_send.at[chunk], far_recv.at[chunk], 8
        )

    def settle(plane, started):
        for copy, m, here, buffer in started:
            copy.wait_recv()
            add(mine.at[plane, m, here], buffer, piece)

    def hook(i):
        if meanwhile is not None:
            meanwhile(i)

    compute(theirs, 1, 1, (3, 1))
    core_a = to_core(1, (3, 1))
    compute(theirs, 1, 1, (2, 0))
    core_b = to_core(1, (2, 0))
    compute(mine, 1, 0, (3, 1, 2, 0))
    hook(0)
    add_core(1, core_a)
    add_core(1, core_b)
    one = [first(1, chunk) for chunk in range(2)]
    compute(theirs, 0, 1, (3, 1, 2, 0))
    core = to_core(0, (3, 1, 2, 0))
    compute(mine, 0, 0, (3, 1, 2, 0))
    hook(1)
    for chunk in range(2):
        settle(1, one[chunk])
        one[chunk] = second(1, chunk)
    add_core(0, core)
    zero = [first(0, chunk) for chunk in range(2)]
    hook(2)
    fars = []
    for chunk in range(2):
        settle(1, one[chunk])
        fars.append(far(chunk))
    hook(3)
    for chunk in range(2):
        settle(0, zero[chunk])
        zero[chunk] = second(0, chunk)
    for chunk in range(2):
        settle(0, zero[chunk])
        fars[chunk].wait_recv()

        @pl.loop(0, 2 * piece // 16)
        def _(i):
            here = pl.ds(pl.multiple_of(chunk * 2 * piece + i * 16, 16), 16)
            write(here, mine[0, 0, here, :].astype(F32) + got_far[here, :].astype(F32))

    for copy in copies:
        copy.wait_send()


def scatter_scratch(rows, width):
    block = (rows, width)
    piece = (rows // 4, width)
    return [
        pltpu.VMEM((2, 4) + block, BF),
        pltpu.VMEM((2, 4) + block, BF),
        pltpu.VMEM((2, 4) + block, BF),
        pltpu.VMEM((2, 2, 4) + piece, BF),
        pltpu.VMEM((2, 2, 2) + piece, BF),
        pltpu.VMEM(block, BF),
        DMA((8,)),
        DMA((8,)),
        DMA((24,)),
        DMA((24,)),
        DMA((2,)),
        DMA((2,)),
    ]


def scatter_dot(plan, left, rights, turned, collective_id):
    rows = left.shape[0] // plan.size
    width = rights[0].shape[0] if turned else rights[0].shape[1]
    count = len(rights)
    depth = left.shape[1] // count

    def kernel(*refs):
        pairs = [(refs[0], i * depth, refs[1 + i]) for i in range(count)]
        out_ref = refs[1 + count]
        rest = refs[2 + count :]
        dp, seq, index = plan.here()
        greet([plan.across(dp, seq, bit) for bit in (1, 2, 4, 8)])

        def write(here, value):
            out_ref[here, :] = value

        scatter_steps(plan, dp, seq, index, pairs, turned, write, rest[:6], rest[6:])

    return pl.pallas_call(
        kernel,
        out_shape=jax.ShapeDtypeStruct((rows, width), F32),
        in_specs=[VM] * (1 + count),
        out_specs=VM,
        scratch_shapes=scatter_scratch(rows, width),
        compiler_params=pltpu.CompilerParams(
            collective_id=collective_id, has_side_effects=True, vmem_limit_bytes=48 * 2**20
        ),
        cost_estimate=LIGHT,
        name="scatter_dot",
    )(left, *rights)


def half_columns(plan, inner, blocks, half):
    wide = inner // blocks
    each = wide // plan.size
    return [(half * inner + block * wide, each, block * each) for block in range(blocks)]


def columns_out(plan, dp, index, w_ref, out_ref, table, send_sem, recv_sem):
    own = w_ref.shape[0]
    wide = out_ref.shape[1]
    rows = pl.ds(pl.multiple_of(index * own, own), own)

    def moves(other):
        for base, each, place in table:
            yield (
                w_ref.at[:, pl.ds(pl.multiple_of(base + other * each, 128), each)],
                out_ref.at[rows, pl.ds(place, each)],
            )

    def begin():
        def to(step, carry):
            other = (index + step) % plan.size
            for src, dst in moves(other):
                send(src, dst, send_sem, recv_sem, plan.member(dp, other))
            return carry

        lax.fori_loop(1, plan.size, to, 0)
        for src, dst in moves(index):
            pltpu.make_async_copy(src, dst, recv_sem).start()

    def finish():
        wait_bytes(out_ref, recv_sem)

        def sent(step, carry):
            wait_bytes(w_ref.at[:, pl.ds(0, wide)], send_sem)
            return carry

        lax.fori_loop(1, plan.size, sent, 0)

    return begin, finish


def columns_back(plan, dp, index, g_ref, out_ref, table, send_sem, recv_sem):
    own = g_ref.shape[0] // plan.size

    def moves(other):
        rows = pl.ds(pl.multiple_of(other * own, own), own)
        for base, each, place in table:
            yield (
                g_ref.at[rows, pl.ds(place, each)],
                out_ref.at[:, pl.ds(pl.multiple_of(base + index * each, 128), each)],
            )

    def begin(plane):
        first = flips(index, 8 * plane) // 8 * 8

        def to(step, carry):
            other = first + (index + step) % 8
            for src, dst in moves(other):
                send(src, dst, send_sem, recv_sem, plan.member(dp, other))
            return carry

        lax.fori_loop(1 - plane, 8, to, 0)
        if plane == 0:
            for src, dst in moves(index):
                pltpu.make_async_copy(src, dst, recv_sem).start()

    def finish():
        wait_bytes(g_ref, recv_sem)

        def sent(step, carry):
            wait_bytes(g_ref.at[pl.ds(0, own)], send_sem)
            return carry

        lax.fori_loop(1, plan.size, sent, 0)

    return begin, finish


def hidden_backward(plan, g_low, rights, grad_out, branch, gain):
    rows, width = branch.shape
    count = len(rights)
    depth = g_low.shape[1] // count

    def kernel(*refs):
        pairs = [(refs[0], i * depth, refs[1 + i]) for i in range(count)]
        dy, u, g, grad, g_gain, low = refs[1 + count : 7 + count]
        rest = refs[7 + count :]
        dp, seq, index = plan.here()
        greet([plan.across(dp, seq, bit) for bit in (1, 2, 4, 8)])
        g_gain[...] = jnp.zeros_like(g_gain)

        def write(here, value):
            e = dy[here, :].astype(F32) + value
            grad[here, :] = e
            values = u[here, :]
            r = lax.rsqrt(jnp.mean(values * values, axis=1, keepdims=True) + epsilon)
            scaled = e * g[...]
            inner = jnp.mean(scaled * values, axis=1, keepdims=True)
            low[here, :] = (r * scaled - values * (r * r * r * inner)).astype(BF)
            g_gain[...] += jnp.sum(e * values * r, axis=0, keepdims=True)

        scatter_steps(plan, dp, seq, index, pairs, True, write, rest[:6], rest[6:])

    return pl.pallas_call(
        kernel,
        out_shape=[
            jax.ShapeDtypeStruct((rows, width), F32),
            jax.ShapeDtypeStruct((1, width), F32),
            jax.ShapeDtypeStruct((rows, width), BF),
        ],
        in_specs=[VM] * (4 + count),
        out_specs=[VM] * 3,
        scratch_shapes=scatter_scratch(rows, width),
        compiler_params=pltpu.CompilerParams(
            collective_id=7, has_side_effects=True, vmem_limit_bytes=48 * 2**20
        ),
        cost_estimate=LIGHT,
        name="hidden_backward",
    )(g_low, *rights, grad_out, branch, gain)


def start_gather(plan, x, attn_w, gate_up_w, gains, segments, blocks):
    rows, width = x.shape
    own, both = gate_up_w.shape
    table = half_columns(plan, both // 2, blocks, 0)

    count = len(gains)

    def kernel(x_ref, w_ref, u_ref, s_ref, *refs):
        gain_refs, (xo, wo, uo, oo, go, do) = refs[:count], refs[count : count + 6]
        g_ref, d_ref = refs[count + 6 : count + 8]
        sems = refs[count + 8 :]
        gather_sems = sems[:7]
        w_send, w_recv, u_send, u_recv, o_send, o_recv, g_send, g_recv, d_send, d_recv = sems[7:]
        g_ref[...] = jnp.zeros_like(g_ref)
        for i, gain in enumerate(gain_refs):
            g_ref[i : i + 1, :own] = gain[...].astype(F32)
        d_ref[...] = jnp.broadcast_to(s_ref[...], d_ref.shape)
        dp, seq, index = plan.here()
        me = dp * plan.seq + seq
        greet_all(plan, dp, seq)
        begin, finish = gather_steps(plan, x_ref, xo, dp, seq, index, gather_sems)
        begin()
        group = dp // plan.low
        def columns(part, other):
            return pl.ds(pl.multiple_of(part * width + plan.head(other) * HEAD, HEAD), HEAD)

        mine = pl.ds(pl.multiple_of(me * own, own), own)

        def w_to(away, step, carry):
            other = (index + step) % plan.size
            to_group = (group + away) % plan.groups
            device = (to_group * plan.low + other // plan.seq, other % plan.seq)
            for part in range(3):
                send(
                    w_ref.at[:, columns(part, other)],
                    wo.at[mine, pl.ds(part * HEAD, HEAD)],
                    w_send,
                    w_recv,
                    device,
                )
            return carry

        for away in range(1, plan.groups):
            lax.fori_loop(0, plan.size, functools.partial(w_to, away), 0)
        lax.fori_loop(1, plan.size, functools.partial(w_to, 0), 0)
        for part in range(3):
            pltpu.make_async_copy(
                w_ref.at[:, columns(part, index)], wo.at[mine, pl.ds(part * HEAD, HEAD)], w_recv
            ).start()

        feature = me * own
        keeper = plan.of_head(feature // HEAD)
        o_dst = oo.at[pl.ds(pl.multiple_of(feature % HEAD, own), own)]
        o_src = w_ref.at[:, pl.ds(3 * width, width)]

        def o_to(away, carry):
            to_group = (group + away) % plan.groups
            to_dp, to_seq = to_group * plan.low + keeper // plan.seq, keeper % plan.seq
            same = to_dp * plan.seq + to_seq == me

            @pl.when(same)
            def _():
                pltpu.make_async_copy(o_src, o_dst, o_recv).start()

            @pl.when(jnp.logical_not(same))
            def _():
                send(o_src, o_dst, o_send, o_recv, (to_dp, to_seq))

            return carry

        lax.fori_loop(0, plan.groups, o_to, 0)

        def g_to(step, carry):
            other = (me + step) % plan.devices
            send(g_ref, go.at[me], g_send, g_recv, (other // plan.seq, other % plan.seq))
            return carry

        lax.fori_loop(1, plan.devices, g_to, 0)
        pltpu.make_async_copy(g_ref, go.at[me], g_recv).start()

        def d_to(step, carry):
            send(d_ref, do.at[index], d_send, d_recv, plan.member(dp, (index + step) % plan.size))
            return carry

        lax.fori_loop(1, plan.size, d_to, 0)
        pltpu.make_async_copy(d_ref, do.at[index], d_recv).start()
        begin_u, finish_u = columns_out(plan, dp, index, u_ref, uo, table, u_send, u_recv)
        begin_u()
        finish()
        finish_u()
        wait_bytes(go, g_recv)
        wait_bytes(do, d_recv)
        wait_bytes(wo, w_recv)

        def sent(step, carry):
            wait_bytes(w_ref.at[:, pl.ds(0, 3 * HEAD)], w_send)
            wait_bytes(g_ref, g_send)
            return carry

        lax.fori_loop(1, plan.devices, sent, 0)

        def sent_docs(step, carry):
            wait_bytes(d_ref, d_send)
            return carry

        lax.fori_loop(1, plan.size, sent_docs, 0)
        wait_bytes(oo, o_recv)

        def sent_o(away, carry):
            to_group = (group + away) % plan.groups
            to_dp, to_seq = to_group * plan.low + keeper // plan.seq, keeper % plan.seq

            @pl.when(to_dp * plan.seq + to_seq != me)
            def _():
                wait_bytes(o_src, o_send)

            return carry

        lax.fori_loop(0, plan.groups, sent_o, 0)


    shapes = (
        ((plan.size * rows, width), BF),
        ((plan.devices * own, 3 * HEAD), BF),
        ((plan.size * own, both // 2 // plan.size), BF),
        ((HEAD, width), BF),
        ((plan.devices, 8, 128), F32),
        ((plan.size, 8, rows), jnp.int32),
    )
    return pl.pallas_call(
        kernel,
        out_shape=[jax.ShapeDtypeStruct(*shape) for shape in shapes],
        in_specs=[ANY] * 3 + [VM] * (1 + count),
        out_specs=[ANY] * 6,
        scratch_shapes=[pltpu.VMEM((8, 128), F32), pltpu.VMEM((8, rows), jnp.int32)]
        + list(GATHER_SEMS)
        + [DMA] * 10,
        compiler_params=pltpu.CompilerParams(collective_id=0, has_side_effects=True),
        cost_estimate=LIGHT,
        name="start_gather",
    )(x, attn_w, gate_up_w, segments, *[gain.reshape(1, own) for gain in gains])


def dot(left, right):
    return jnp.dot(left, right, preferred_element_type=F32)


def contract_last(left, right):
    return lax.dot_general(left, right, (((1,), (1,)), ((), ())), preferred_element_type=F32)


def contract_first(left, right):
    return lax.dot_general(left, right, (((0,), (0,)), ((), ())), preferred_element_type=F32)


def plane_rows(index, plane, rows):
    return pl.multiple_of(flips(index, 8 * plane) // 8 * (8 * rows), 8 * rows)


def ffn_forward(plan, h, w_gate, w_up):
    rows, width = h.shape
    tokens = rows * plan.size
    units = w_gate.shape[1]

    def kernel(h_ref, wg_ref, wu_ref, h_out, gate, up, act, h_all, wg, wu, *sems):
        wg_sem, wu_sem, out_sem = sems[7:]
        dp, seq, index = plan.here()
        loads = [
            pltpu.make_async_copy(wg_ref, wg, wg_sem),
            pltpu.make_async_copy(wu_ref, wu, wu_sem),
        ]
        for load in loads:
            load.start()
        greet([plan.across(dp, seq, bit) for bit in (1, 2, 4, 8)])
        begin, finish = gather_steps(plan, h_ref, h_all, dp, seq, index, sems[:7])
        begin()
        stores = []

        def use(plane):
            if plane == 0:
                for load in loads:
                    load.wait()
            first = plane_rows(index, plane, rows)
            here = pl.ds(first, 8 * rows)
            stores.append(pltpu.make_async_copy(h_all.at[here], h_out.at[here], out_sem.at[plane]))
            stores[-1].start()

            @pl.loop(0, 8 * rows // STEP)
            def _(i):
                some = pl.ds(pl.multiple_of(first + i * STEP, STEP), STEP)
                values = h_all[some, :]
                g = dot(values, wg[...])
                u = dot(values, wu[...])
                gate[some, :] = g.astype(BF)
                up[some, :] = u.astype(BF)
                act[some, :] = (g * jax.nn.sigmoid(g) * u).astype(BF)

        finish(use)
        for store in stores:
            store.wait()

    part = jax.ShapeDtypeStruct((tokens, units), BF)
    return pl.pallas_call(
        kernel,
        out_shape=[jax.ShapeDtypeStruct((tokens, width), BF), part, part, part],
        in_specs=[VM, ANY, ANY],
        out_specs=[ANY, VM, VM, VM],
        scratch_shapes=[
            pltpu.VMEM((tokens, width), BF),
            pltpu.VMEM(w_gate.shape, BF),
            pltpu.VMEM(w_up.shape, BF),
        ]
        + list(GATHER_SEMS)
        + [DMA, DMA, DMA((2,))],
        compiler_params=pltpu.CompilerParams(
            collective_id=9, has_side_effects=True, vmem_limit_bytes=48 * 2**20
        ),
        cost_estimate=LIGHT,
        name="ffn_forward",
    )(h, w_gate, w_up)


def ffn_backward(plan, d, h_all, w_down, gate, up, act):
    rows, width = d.shape
    tokens = rows * plan.size
    half = tokens // 2
    units = w_down.shape[0]
    tile = 256

    def kernel(d_ref, *refs):
        ins, (out, g_gate, g_up, g_down), held = refs[:5], refs[5:9], refs[9:14]
        d_all, gu_turned, act_turned, gu_sum, down_sum = refs[14:19]
        sems, load_sems = refs[19:26], refs[26]
        h_all, wd, gate, up, act = held
        dp, seq, index = plan.here()
        loads = [
            pltpu.make_async_copy(src, dst, load_sems.at[i])
            for i, (src, dst) in enumerate(zip(ins, held))
        ]
        for load in loads[1:] + loads[:1]:
            load.start()
        greet([plan.across(dp, seq, bit) for bit in (1, 2, 4, 8)])
        begin, finish = gather_steps(plan, d_ref, d_all, dp, seq, index, sems)
        begin()

        def use(plane):
            if plane == 0:
                for load in loads:
                    load.wait()
            first = plane_rows(index, plane, rows)
            here = pl.ds(first, half)

            @pl.loop(0, half // STEP)
            def _(i):
                some = pl.ds(pl.multiple_of(first + i * STEP, STEP), STEP)
                columns = pl.ds(pl.multiple_of(i * STEP, STEP), STEP)
                grad = contract_last(d_all[some, :], wd[...])
                g = gate[some, :].astype(F32)
                u = up[some, :].astype(F32)
                sigma = jax.nn.sigmoid(g)
                grad_gate = (grad * u * sigma * (1.0 + g * (1.0 - sigma))).astype(BF)
                grad_up = (grad * (g * sigma)).astype(BF)
                out[some, pl.ds(0, units)] = grad_gate
                out[some, pl.ds(units, units)] = grad_up
                gu_turned[pl.ds(0, units), columns] = grad_gate.T
                gu_turned[pl.ds(units, units), columns] = grad_up.T
                act_turned[:, columns] = act[some, :].T

            @pl.loop(0, width // tile)
            def _(i):
                columns = pl.ds(pl.multiple_of(i * tile, tile), tile)
                block = dot(gu_turned[...], h_all[here, columns])
                if plane == 0:
                    gu_sum[:, columns] = block
                else:
                    block = (gu_sum[:, columns] + block).T.astype(BF)
                    g_gate[columns, :] = block[:, :units]
                    g_up[columns, :] = block[:, units:]

            @pl.loop(0, width // tile)
            def _(i):
                columns = pl.ds(pl.multiple_of(i * tile, tile), tile)
                block = dot(act_turned[...], d_all[here, columns])
                if plane == 0:
                    down_sum[:, columns] = block
                else:
                    g_down[:, columns] = (down_sum[:, columns] + block).astype(BF)

        finish(use)

    return pl.pallas_call(
        kernel,
        out_shape=[
            jax.ShapeDtypeStruct((tokens, 2 * units), BF),
            jax.ShapeDtypeStruct((width, units), BF),
            jax.ShapeDtypeStruct((width, units), BF),
            jax.ShapeDtypeStruct((units, width), BF),
        ],
        in_specs=[VM] + [ANY] * 5,
        out_specs=[VM] * 4,
        scratch_shapes=[
            pltpu.VMEM(value.shape, BF) for value in (h_all, w_down, gate, up, act, h_all)
        ]
        + [
            pltpu.VMEM((2 * units, half), BF),
            pltpu.VMEM((units, half), BF),
            pltpu.VMEM((2 * units, width), F32),
            pltpu.VMEM((units, width), F32),
        ]
        + list(GATHER_SEMS)
        + [DMA((5,))],
        compiler_params=pltpu.CompilerParams(
            collective_id=10, has_side_effects=True, vmem_limit_bytes=62 * 2**20
        ),
        cost_estimate=LIGHT,
        name="ffn_backward",
    )(d, h_all, w_down, gate, up, act)


def row_sums(values):
    ones = jnp.ones((8, values.shape[1]), F32)
    sums = lax.dot_general(
        ones,
        values,
        (((1,), (1,)), ((), ())),
        precision=lax.Precision.HIGHEST,
        preferred_element_type=F32,
    )
    return sums[:1]


def spread_sums(rows):
    ones = jnp.ones((rows.shape[0], HEAD), F32)
    return lax.dot_general(
        rows,
        ones,
        (((0,), (0,)), ((), ())),
        precision=lax.Precision.HIGHEST,
        preferred_element_type=F32,
    )


STEP = 256


def lay_out(docs_ref, row_ref):
    for i in range(docs_ref.shape[0]):
        rows = docs_ref.shape[2]
        row_ref[:, i * rows : (i + 1) * rows] = docs_ref[i, :1, :].astype(F32)


def my_gain(plan, gains_ref, which, head):
    own = HEAD // plan.pieces
    parts = [gains_ref[head * plan.pieces + i, which : which + 1, :own] for i in range(plan.pieces)]
    return jnp.concatenate(parts, axis=1)


def scores_of(q, k, q_docs, k_docs, start):
    scores = contract_last(q, k) * HEAD ** (-0.5)
    row = start + lax.broadcasted_iota(jnp.int32, scores.shape, 0)
    column = lax.broadcasted_iota(jnp.int32, scores.shape, 1)
    allowed = (column <= row) & (spread_sums(q_docs)[:, :1] == k_docs)
    scores = jnp.where(allowed, scores, -1e30)
    top = jnp.max(scores, axis=1, keepdims=True)
    weights = jnp.exp(scores - top)
    return weights / jnp.sum(weights, axis=1, keepdims=True)


def swap_sums(plan, dp, index, mine, held, s_sem, r_sem):
    def begin():
        def to(step, carry):
            send(mine, held.at[index], s_sem, r_sem, plan.member(dp, (index + step) % plan.size))
            return carry

        pltpu.make_async_copy(mine, held.at[index], r_sem).start()
        lax.fori_loop(1, plan.size, to, 0)

    def finish():
        wait_bytes(held, r_sem)
        wait_bytes(held.at[pl.ds(0, plan.size - 1)], s_sem)

    return begin, finish


def attend_forward(
    plan, x_all, w_qkv, gate_up_w, gains, docs, cosine, sine, blocks
):
    tokens, width = x_all.shape
    length = cosine.shape[0]
    own, both = gate_up_w.shape
    table = half_columns(plan, both // 2, blocks, 1)

    def kernel(x, wq, up, ga, do, cs, sn, uo, q, k, sums, ql, kl, vl, mixed, *rest):
        gn, dr, stats, held, t_send, t_recv, u_send, u_recv = rest
        dp, seq, index = plan.here()
        greet_group(plan, dp, index)
        lay_out(do, dr)
        for which in range(2):
            gn[which : which + 1, :] = my_gain(plan, ga, which, plan.head(index))
        @pl.loop(0, tokens // STEP)
        def _(i):
            rows = pl.ds(pl.multiple_of(i * STEP, STEP), STEP)
            block = dot(x[rows, :], wq[...])
            q[rows, :] = block[:, :HEAD]
            k[rows, :] = block[:, HEAD : 2 * HEAD]
            vl[rows, :] = block[:, 2 * HEAD :].astype(BF)
            stats[0, :, rows] = row_sums(block[:, :HEAD] * block[:, :HEAD])
            stats[1, :, rows] = row_sums(block[:, HEAD : 2 * HEAD] * block[:, HEAD : 2 * HEAD])

        begin, finish = swap_sums(plan, dp, index, stats, held, t_send, t_recv)
        begin()
        begin_u, finish_u = columns_out(plan, dp, index, up, uo, table, u_send, u_recv)
        begin_u()
        finish()
        for which in range(2):
            sums[which] = jnp.sum(held[:, which, 0, :], axis=0, keepdims=True)

        @pl.loop(0, tokens // STEP)
        def _(i):
            rows = pl.ds(pl.multiple_of(i * STEP, STEP), STEP)
            places = pl.ds(pl.multiple_of((i % (length // STEP)) * STEP, STEP), STEP)
            for which, raw, low in ((0, q, ql), (1, k, kl)):
                r = lax.rsqrt(spread_sums(sums[which, :, rows]) / width + epsilon)
                values = raw[rows, :] * r * gn[which : which + 1, :]
                turned = values * cs[places, :] + pltpu.roll(values, HEAD // 2, 1) * sn[places, :]
                low[rows, :] = turned.astype(BF)

        @pl.loop(0, tokens // length)
        def _(b):
            for j in range(length // STEP):
                start = pl.multiple_of(b * length + j * STEP, STEP)
                rows = pl.ds(start, STEP)
                keys = pl.ds(pl.multiple_of(b * length, length), (j + 1) * STEP)
                probs = scores_of(
                    ql[rows, :], kl[keys, :], dr[:, rows], dr[:, keys], j * STEP
                )
                mixed[rows, :] = dot(probs.astype(BF), vl[keys, :]).astype(BF)

        finish_u()

    per_head = (tokens, HEAD)
    shapes = (
        ((plan.size * own, both // 2 // plan.size), BF),
        (per_head, F32),
        (per_head, F32),
        ((2, 1, tokens), F32),
        (per_head, BF),
        (per_head, BF),
        (per_head, BF),
        (per_head, BF),
    )
    return pl.pallas_call(
        kernel,
        out_shape=[jax.ShapeDtypeStruct(*shape) for shape in shapes],
        in_specs=[VM, VM, ANY] + [VM] * 4,
        out_specs=[ANY] + [VM] * 7,
        scratch_shapes=[
            pltpu.VMEM((8, HEAD), F32),
            pltpu.VMEM((1, tokens), F32),
            pltpu.VMEM((2, 1, tokens), F32),
            pltpu.VMEM((plan.size, 2, 1, tokens), F32),
        ]
        + [DMA] * 4,
        compiler_params=pltpu.CompilerParams(
            collective_id=3, has_side_effects=True, vmem_limit_bytes=56 * 2**20
        ),
        cost_estimate=LIGHT,
        name="attend_forward",
    )(x_all, w_qkv, gate_up_w, gains, docs, cosine, sine)


def attend_backward(
    plan,
    b,
    w_out,
    q,
    k,
    sums,
    ql,
    kl,
    vl,
    mixed,
    gains,
    docs,
    cosine,
    sine,
    g_gate,
    blocks,
):
    rows_here, width = b.shape
    tokens = rows_here * plan.size
    in_plane = 8 * rows_here
    own = g_gate.shape[0] // plan.size
    inner = g_gate.shape[1] * plan.size
    length = cosine.shape[0]
    scale = HEAD ** (-0.5)

    def kernel(*refs):
        b_ref, wo, q, k, sums, ql, kl, vl, mx, ga, do, cs, sn, gg = refs[:14]
        dqkv, g_out, g_gain, gate_out = refs[14:18]
        ba, dq, dk, dv, gn, dr, stats, held, t_send, t_recv, gg_send, gg_recv = refs[18:30]
        dp, seq, index = plan.here()
        greet_group(plan, dp, index)
        begin_b, finish_b = gather_steps(plan, b_ref, ba, dp, seq, index, refs[30:])
        begin_b()
        lay_out(do, dr)
        for which in range(2):
            gn[which : which + 1, :] = my_gain(plan, ga, which, plan.head(index))
        begin_g, finish_g = columns_back(
            plan, dp, index, gg, gate_out, half_columns(plan, inner, blocks, 0), gg_send, gg_recv
        )
        dk[...] = jnp.zeros_like(dk)
        dv[...] = jnp.zeros_like(dv)

        def use(plane):
            if plane == 1:
                begin_g(0)
            plane_first = plane_rows(index, plane, rows_here)
            for j in range(in_plane // STEP):
                first = pl.multiple_of(plane_first + j * STEP, STEP)
                rows = pl.ds(first, STEP)
                start = first % length
                count = (j + 1) * STEP if length == in_plane else length
                base = pl.multiple_of(first - start, STEP)
                keys = pl.ds(base, count)
                grad = contract_last(ba[rows, :], wo[...]).astype(BF)
                probs = scores_of(
                    ql[rows, :], kl[keys, :], dr[:, rows], dr[:, keys], start
                )
                grad_probs = contract_last(grad, vl[keys, :])
                delta = jnp.sum(probs * grad_probs, axis=1, keepdims=True)
                grad_scores = (probs * (grad_probs - delta)).astype(BF)
                dq[rows, :] = dot(grad_scores, kl[keys, :]) * scale
                dk[keys, :] += contract_first(grad_scores, ql[rows, :]) * scale
                dv[keys, :] += contract_first(probs.astype(BF), grad)

        finish_b(use)

        @pl.loop(0, tokens // STEP)
        def _(i):
            rows = pl.ds(pl.multiple_of(i * STEP, STEP), STEP)
            places = pl.ds(pl.multiple_of((i % (length // STEP)) * STEP, STEP), STEP)
            for which, raw, grad in ((0, q, dq), (1, k, dk)):
                values = grad[rows, :]
                turned = values * cs[places, :] - pltpu.roll(values, HEAD // 2, 1) * sn[places, :]
                grad[rows, :] = turned
                stats[which, :, rows] = row_sums(turned * gn[which : which + 1, :] * raw[rows, :])

        begin, finish = swap_sums(plan, dp, index, stats, held, t_send, t_recv)
        begin()
        begin_g(1)
        turned_mixed = mx[...].T

        @pl.loop(0, width // 512)
        def _(i):
            columns = pl.ds(pl.multiple_of(i * 512, 512), 512)
            g_out[:, columns] = dot(turned_mixed, ba[:, columns]).astype(BF)

        g_gain[...] = jnp.zeros_like(g_gain)
        finish()

        @pl.loop(0, tokens // STEP)
        def _(i):
            rows = pl.ds(pl.multiple_of(i * STEP, STEP), STEP)
            for which, raw, grad in ((0, q, dq), (1, k, dk)):
                total = spread_sums(held[:, which, 0, rows])
                r = lax.rsqrt(spread_sums(sums[which, :, rows]) / width + epsilon)
                u = raw[rows, :]
                e = grad[rows, :]
                back = r * (gn[which : which + 1, :] * e) - u * (r * r * r * (total / width))
                dqkv[rows, pl.ds(which * HEAD, HEAD)] = back.astype(BF)
                g_gain[which : which + 1, :] += jnp.sum(e * u * r, axis=0, keepdims=True)
            dqkv[rows, pl.ds(2 * HEAD, HEAD)] = dv[rows, :].astype(BF)

        finish_g()

    per_head = (tokens, HEAD)
    shapes = (
        ((tokens, 3 * HEAD), BF),
        ((HEAD, width), BF),
        ((8, HEAD), F32),
        ((own, inner), BF),
    )
    return pl.pallas_call(
        kernel,
        out_shape=[jax.ShapeDtypeStruct(*shape) for shape in shapes],
        in_specs=[VM] * 13 + [ANY],
        out_specs=[VM] * 3 + [ANY],
        scratch_shapes=[
            pltpu.VMEM((tokens, width), BF),
            pltpu.VMEM(per_head, F32),
            pltpu.VMEM(per_head, F32),
            pltpu.VMEM(per_head, F32),
            pltpu.VMEM((8, HEAD), F32),
            pltpu.VMEM((1, tokens), F32),
            pltpu.VMEM((2, 1, tokens), F32),
            pltpu.VMEM((plan.size, 2, 1, tokens), F32),
        ]
        + [DMA] * 4
        + list(GATHER_SEMS),
        compiler_params=pltpu.CompilerParams(
            collective_id=4, has_side_effects=True, vmem_limit_bytes=56 * 2**20
        ),
        cost_estimate=LIGHT,
        name="attend_backward",
    )(
        b,
        w_out,
        q,
        k,
        sums,
        ql,
        kl,
        vl,
        mixed,
        gains,
        docs,
        cosine,
        sine,
        g_gate,
    )


def finish_backward(
    plan, dqkv, w_qkv, x_all, g_up, g_out, g_head, g_attn, g_ffn, before, blocks
):
    tokens, width = x_all.shape
    own = width // plan.devices
    rows = tokens // plan.size
    inner = g_up.shape[1] * plan.size
    pieces = HEAD // own
    tile = 256

    def kernel(dq, wq, x, gu, go, gh, gat, gff, bf, ig, w_grad, up_out, ga_out, *rest):
        bufs, sems = rest[:6], rest[6:12]
        turned, gq, got_q, got_o, ga = rest[12:17]
        q_s, q_r, o_s, o_r, ga_s, ga_r, gu_s, gu_r = rest[17:]
        dp, seq, index = plan.here()
        me = dp * plan.seq + seq
        group = dp // plan.low
        greet_all(plan, dp, seq)

        def device_of(flat):
            return flat // plan.seq, flat % plan.seq

        def o_to(piece, carry):
            other = plan.head(index) * pieces + piece
            src = go.at[pl.ds(pl.multiple_of(piece * own, own), own)]

            @pl.when(other == me)
            def _():
                pltpu.make_async_copy(src, got_o.at[group], o_r).start()

            @pl.when(other != me)
            def _():
                send(src, got_o.at[group], o_s, o_r, device_of(other))

            return carry

        def ga_to(step, carry):
            other = (me + step) % plan.devices
            send(ga.at[other], ga_out.at[me], ga_s, ga_r, device_of(other))
            return carry

        tiles = width // tile
        table = half_columns(plan, inner, blocks, 0)
        begin_u, finish_u = columns_back(plan, dp, index, gu, up_out, table, gu_s, gu_r)

        def weights(first, last):
            @pl.loop(first, last)
            def _(i):
                at = (i + (me * own) // tile) % tiles
                columns = pl.ds(pl.multiple_of(at * tile, tile), tile)
                block = dot(turned[...], x[:, columns])
                gq[columns, :] = block.T.astype(BF)

                def q_to(piece, carry):
                    other = at * (tile // own) + piece
                    src = gq.at[pl.ds(pl.multiple_of(other * own, own), own)]

                    @pl.when(other == me)
                    def _():
                        pltpu.make_async_copy(src, got_q.at[group, index], q_r).start()

                    @pl.when(other != me)
                    def _():
                        send(src, got_q.at[group, index], q_s, q_r, device_of(other))

                    return carry

                lax.fori_loop(0, tile // own, q_to, 0)

        def meanwhile(i):
            if i == 0:
                turned[...] = dq[...].T
                weights(0, tiles // 4)
            elif i == 1:
                weights(tiles // 4, 5 * tiles // 8)
            elif i == 2:
                lax.fori_loop(0, pieces, o_to, 0)
                begin_u(1)
            else:
                begin_u(0)
                weights(5 * tiles // 8, tiles)
                ga[...] = jnp.zeros_like(ga)
                for other in range(plan.devices):
                    part = slice(other * own, (other + 1) * own)
                    ga[other, 2:3, :own] = gat[:, part]
                    ga[other, 3:4, :own] = gff[:, part]
                for piece in range(pieces):
                    part = slice(piece * own, (piece + 1) * own)
                    ga[plan.head(index) * pieces + piece, 0:2, :own] = gh[0:2, part]
                lax.fori_loop(1, plan.devices, ga_to, 0)
                pltpu.make_async_copy(ga.at[me], ga_out.at[me], ga_r).start()

        def write(here, value):
            ig[here, :] = bf[here, :] + value

        scatter_steps(plan, dp, seq, index, [(dq, 0, wq)], True, write, bufs, sems, meanwhile)
        wait_bytes(got_o, o_r)
        wait_bytes(got_q, q_r)
        for part in range(3):
            for member in range(plan.size):
                total = got_q[0, member, :, part * HEAD : (part + 1) * HEAD].astype(F32)
                for other in range(1, plan.groups):
                    total = total + got_q[
                        other, member, :, part * HEAD : (part + 1) * HEAD
                    ].astype(F32)
                w_grad[:, pl.ds(part * width + plan.head(member) * HEAD, HEAD)] = total
        total = got_o[0].astype(F32)
        for other in range(1, plan.groups):
            total = total + got_o[other].astype(F32)
        w_grad[:, pl.ds(3 * width, width)] = total
        finish_u()
        wait_bytes(ga_out, ga_r)
        wait_bytes(ga_out.at[pl.ds(0, plan.devices - 1)], ga_s)
        wait_bytes(gq.at[pl.ds(0, width - own)], q_s)

        def sent_o(piece, carry):
            @pl.when(plan.head(index) * pieces + piece != me)
            def _():
                wait_bytes(go.at[pl.ds(0, own)], o_s)

            return carry

        lax.fori_loop(0, pieces, sent_o, 0)

    shapes = (
        ((rows, width), F32),
        ((own, 4 * width), F32),
        ((own, inner), BF),
        ((plan.devices, 8, 128), F32),
    )
    return pl.pallas_call(
        kernel,
        out_shape=[jax.ShapeDtypeStruct(*shape) for shape in shapes],
        in_specs=[VM, VM, VM, ANY] + [VM] * 5,
        out_specs=[VM, VM, ANY, VM],
        scratch_shapes=scatter_scratch(rows, width)
        + [
            pltpu.VMEM((3 * HEAD, tokens), BF),
            pltpu.VMEM((width, 3 * HEAD), BF),
            pltpu.VMEM((plan.groups, plan.size, own, 3 * HEAD), BF),
            pltpu.VMEM((plan.groups, own, width), BF),
            pltpu.VMEM((plan.devices, 8, 128), F32),
        ]
        + [DMA] * 8,
        compiler_params=pltpu.CompilerParams(
            collective_id=5, has_side_effects=True, vmem_limit_bytes=60 * 2**20
        ),
        cost_estimate=LIGHT,
        name="finish_backward",
    )(dqkv, w_qkv, x_all, g_up, g_out, g_head, g_attn, g_ffn, before)


def per_device(
    plan,
    hidden_in,
    segments,
    attn_weights,
    q_gain,
    k_gain,
    attn_gain,
    ffn_gain,
    gate_up_weights,
    down_weights,
    cotangent,
):
    x = hidden_in[0]
    rows, width = x.shape
    own = attn_weights.shape[0]
    inner = gate_up_weights.shape[1] // 2
    length = rows * plan.seq
    tokens = rows * plan.size
    groups = plan.groups
    dp, seq, index = plan.here()
    me = dp * plan.seq + seq
    group = dp // plan.low
    direct = (inner // (groups * plan.size)) % 128 == 0
    blocks = groups if direct else 1

    across = [[low + high * plan.low for high in range(groups)] for low in range(plan.low)]

    def join_groups(value):
        return lax.all_gather(value, "dp", axis_index_groups=across, axis=0, tiled=True)

    def sum_groups(value):
        return lax.psum_scatter(
            value.astype(BF), "dp", axis_index_groups=across, scatter_dimension=0, tiled=True
        )

    x_all, w_qkv, gate_part, w_out, gains_all, docs = start_gather(
        plan,
        x,
        attn_weights,
        gate_up_weights,
        [q_gain, k_gain, attn_gain, ffn_gain],
        segments,
        blocks,
    )
    w_gate = join_groups(gate_part)
    gains = jnp.transpose(gains_all[:, 2:4, :own], (1, 0, 2)).reshape(2, width)
    positions = np.arange(length, dtype=np.float32)
    frequency = rope_base ** (-2.0 * np.arange(HEAD // 2, dtype=np.float32) / HEAD)
    angles = positions[:, None] * frequency.astype(np.float32)[None, :]
    cosine = jnp.asarray(np.concatenate([np.cos(angles)] * 2, axis=1), F32)
    sine = jnp.asarray(np.concatenate([-np.sin(angles), np.sin(angles)], axis=1), F32)

    up_part, q, k, row_sums_qk, q_low, k_low, v_low, mixed = attend_forward(
        plan,
        x_all,
        w_qkv,
        gate_up_weights,
        gains_all,
        docs,
        cosine,
        sine,
        blocks,
    )
    w_up = join_groups(up_part)
    down_weights, _ = lax.optimization_barrier((down_weights, up_part))
    if direct:
        w_down = join_groups(down_weights)
    else:
        w_all = lax.all_gather(down_weights, ("dp", "seq"), axis=0, tiled=True)
        each = inner // plan.size
        w_down = lax.dynamic_slice_in_dim(w_all, index * each, each, 0)
    branch = scatter_dot(plan, mixed, [w_out], False, 2)
    branch, w_gate = lax.optimization_barrier((branch, w_gate))

    def rms(values):
        return lax.rsqrt(jnp.mean(values * values, axis=1, keepdims=True) + epsilon)

    def rms_back(values, r, gain, grad):
        scaled = gain * grad
        inner_sum = jnp.mean(scaled * values, axis=1, keepdims=True)
        return r * scaled - values * (r * r * r * inner_sum), jnp.sum(grad * values * r, axis=0)

    branch_r = rms(branch)
    hidden = x.astype(F32) + branch * branch_r * gains[0]
    hidden_low = hidden.astype(BF)

    h_all, gate, up, act = ffn_forward(plan, hidden_low, w_gate, w_up)
    down = scatter_dot(plan, act, [w_down], False, 6)
    down_r = rms(down)
    output = (hidden + down * down_r * gains[1]).astype(BF)

    grad_out = cotangent[0].astype(F32)
    grad_down_in, grad_fg = rms_back(down, down_r, gains[1], grad_out)
    gu_low, g_gate, g_up, g_down = ffn_backward(
        plan, grad_down_in.astype(BF), h_all, w_down, gate, up, act
    )
    g_gate = sum_groups(g_gate)
    g_up = sum_groups(g_up)
    if direct:
        grad_down = sum_groups(g_down).astype(F32)
    else:
        spread = jnp.zeros((inner, width), BF)
        spread = lax.dynamic_update_slice_in_dim(spread, g_down, index * g_down.shape[0], 0)
        grad_down = lax.psum_scatter(
            spread, ("dp", "seq"), scatter_dimension=0, tiled=True
        ).astype(F32)

    grad_hidden, grad_ag, grad_branch = hidden_backward(
        plan, gu_low, [w_gate, w_up], cotangent[0], branch, gains[:1]
    )
    dqkv, g_out, g_head, gate_rows = attend_backward(
        plan,
        grad_branch,
        w_out,
        q,
        k,
        row_sums_qk,
        q_low,
        k_low,
        v_low,
        mixed,
        gains_all,
        docs,
        cosine,
        sine,
        g_gate,
        blocks,
    )

    input_grad, grad_attn, up_rows, gain_rows = finish_backward(
        plan,
        dqkv,
        w_qkv,
        x_all,
        g_up,
        g_out,
        g_head,
        grad_ag,
        grad_fg.reshape(1, width),
        grad_hidden,
        blocks,
    )
    grad_gate_up = jnp.concatenate([gate_rows, up_rows], axis=1).astype(F32)
    gain_grads = jnp.sum(gain_rows, axis=0)[:4, :own]
    return (
        output[None],
        input_grad[None],
        grad_attn,
        grad_gate_up,
        grad_down,
        gain_grads[0],
        gain_grads[1],
        gain_grads[2],
        gain_grads[3],
    )


def solution(mesh):
    by_token = P("dp", "seq", None)
    by_row = P(("dp", "seq"), None)
    by_gain = P(("dp", "seq"))

    def run(hidden_in, segments, attn_weights, *rest):
        plan = Plan(mesh, hidden_in.shape[2] // HEAD)
        return jax.shard_map(
            functools.partial(per_device, plan),
            mesh=mesh,
            in_specs=(by_token, P("dp", "seq"), by_row)
            + (by_gain,) * 4
            + (by_row, by_row, by_token),
            out_specs=(by_token, by_token, by_row, by_row, by_row) + (by_gain,) * 4,
            check_vma=False,
        )(hidden_in, segments, attn_weights, *rest)

    return run
```

```python
import functools

import jax
import jax.numpy as jnp
import numpy as np
from jax import lax
from jax.experimental import pallas as pl
from jax.experimental.pallas import tpu as pltpu
from jax.sharding import PartitionSpec as P

HEAD = 128
epsilon = 1e-06
rope_base = 500000.0
MESH = pl.DeviceIdType.MESH
BF = jnp.bfloat16
F32 = jnp.float32
ANY = pl.BlockSpec(memory_space=pl.ANY)
VM = pl.BlockSpec(memory_space=pltpu.VMEM)
DMA = pltpu.SemaphoreType.DMA
LIGHT = pl.CostEstimate(flops=0, bytes_accessed=0, transcendentals=0)


class Plan:
    def __init__(self, mesh, heads):
        self.dp = mesh.shape["dp"]
        self.seq = mesh.shape["seq"]
        self.size = heads
        self.low = heads // self.seq
        self.groups = self.dp // self.low
        self.devices = self.dp * self.seq
        self.pieces = self.devices // heads
        self.chips = self.seq // 2
        self.by_chip = self.groups == 2 and self.size == self.dp * self.chips

    def group_of(self, dp):
        return dp % self.groups + (dp // self.groups) * (self.groups - 1 - 2 * (dp % self.groups))

    def dp_of(self, group, low):
        return low * self.groups + group + low * (self.groups - 1 - 2 * group)

    def flat(self, group, index):
        return self.dp_of(group, index // self.seq) * self.seq + index % self.seq

    def place(self, dp):
        return self.group_of(dp) * self.low + dp // self.groups

    def natural(self, rows):
        if self.low == 1:
            return [(0, 0, rows)]
        count = rows // self.dp
        return [(self.place(i) * count, i * count, count) for i in range(self.dp)]

    def here(self):
        dp = lax.axis_index("dp")
        seq = lax.axis_index("seq")
        return dp, seq, (dp // self.groups) * self.seq + seq

    def head(self, index):
        if self.by_chip:
            return self.dp_of(index % 2, index // self.seq) * self.chips + (index % self.seq) // 2
        return index

    def of_head(self, head):
        if self.by_chip:
            dp = head // self.chips
            low = dp // self.groups
            return low * self.seq + (head % self.chips) * 2 + self.group_of(dp)
        return head

    def in_group(self, group, index):
        return self.dp_of(group, index // self.seq), index % self.seq

    def member(self, dp, index):
        return self.in_group(self.group_of(dp), index)

    def across(self, dp, seq, bit):
        if bit < self.seq:
            return dp, flip(seq, bit)
        return 2 * self.groups - 1 - dp, seq


def flip(value, bit):
    return value + bit * (1 - 2 * ((value // bit) % 2))


def flips(value, mask):
    bit = 1
    while bit <= mask:
        if mask & bit:
            value = flip(value, bit)
        bit *= 2
    return value


def greet(devices):
    barrier = pltpu.get_barrier_semaphore()
    for device in devices:
        pl.semaphore_signal(barrier, inc=1, device_id=device, device_id_type=MESH)
    pl.semaphore_wait(barrier, len(devices))


def greet_all(plan, dp, seq):
    barrier = pltpu.get_barrier_semaphore()
    me = dp * plan.seq + seq

    def hello(step, carry):
        other = (me + step) % plan.devices
        pl.semaphore_signal(
            barrier, inc=1, device_id=(other // plan.seq, other % plan.seq), device_id_type=MESH
        )
        return carry

    lax.fori_loop(1, plan.devices, hello, 0)
    pl.semaphore_wait(barrier, plan.devices - 1)


def greet_group(plan, dp, index):
    barrier = pltpu.get_barrier_semaphore()

    def hello(step, carry):
        other = plan.member(dp, (index + step) % plan.size)
        pl.semaphore_signal(barrier, inc=1, device_id=other, device_id_type=MESH)
        return carry

    lax.fori_loop(1, plan.size, hello, 0)
    pl.semaphore_wait(barrier, plan.size - 1)


def send(src, dst, send_sem, recv_sem, device):
    copy = pltpu.make_async_remote_copy(
        src_ref=src,
        dst_ref=dst,
        send_sem=send_sem,
        recv_sem=recv_sem,
        device_id=device,
        device_id_type=MESH,
    )
    copy.start()
    return copy


def wait_bytes(ref, sem):
    pltpu.make_async_copy(ref, ref, sem).wait()


class Loads:
    def __init__(self, sources, buffers, sems):
        self.copies = [
            pltpu.make_async_copy(src, dst, sems.at[i])
            for i, (src, dst) in enumerate(zip(sources, buffers))
        ]
        for copy in self.copies:
            copy.start()

    def wait(self, *which):
        for i in which or range(len(self.copies)):
            self.copies[i].wait()


def like(value):
    return pltpu.VMEM(value.shape, value.dtype)


def halves(rows):
    return ((0, rows // 2), (rows // 2, rows - rows // 2))


ORDERS = ((2, 4), (4, 2))


def gather_steps(plan, x, out, dp, seq, index, sems):
    far_send, far_recv, near_send, near_recv, core_send, core_recv, local = sems
    rows = x.shape[0]
    parts = halves(rows)
    copies = []

    def place(mask, part=None):
        start, count = (0, rows) if part is None else parts[part]
        return out.at[pl.ds(pl.multiple_of(flips(index, mask) * rows + start, 16), count)]

    def push(src, dst, send_sem, recv_sem, bit):
        copies.append(send(src, dst, send_sem, recv_sem, plan.across(dp, seq, bit)))

    def near(mask, part, number, bit):
        push(place(mask, part), place(mask, part), near_send.at[number], near_recv.at[number], bit)

    def to_core(mask, part, number):
        push(place(mask, part), place(mask, part), core_send.at[number], core_recv.at[number], 1)

    def begin():
        pltpu.make_async_copy(x, out.at[pl.ds(index * rows, rows)], local).start()
        for part in range(2):
            start, count = parts[part]
            push(
                x.at[pl.ds(start, count)], place(0, part), far_send.at[part], far_recv.at[part], 8
            )
        for bit in (2, 4):
            push(x, place(0), near_send.at[bit // 4], near_recv.at[bit // 4], bit)
        push(x, place(0), core_send.at[0], core_recv.at[0], 1)

    def finish(use=None):
        def here(chip):
            if use is not None:
                use(chip)

        pltpu.make_async_copy(x, out.at[pl.ds(index * rows, rows)], local).wait()
        wait_bytes(place(1), core_recv.at[0])
        here(0)
        for bit, other in ORDERS:
            part = bit // 4
            wait_bytes(place(bit), near_recv.at[part])
            near(bit, part, 2 + part, other)
            to_core(bit, None, 1 + part)
        for part in range(2):
            wait_bytes(place(8, part), far_recv.at[part])
            for bit in (2, 4):
                near(8, part, 4 + 2 * part + bit // 4, bit)
            to_core(8, part, 5 + part)
        for bit in (2, 4):
            wait_bytes(place(1 | bit), core_recv.at[1 + bit // 4])
            here(bit)
        for part in range(2):
            wait_bytes(place(6, part), near_recv.at[2 + part])
            to_core(6, part, 3 + part)
        for part in range(2):
            wait_bytes(place(9, part), core_recv.at[5 + part])
        here(8)
        for part in range(2):
            wait_bytes(place(7, part), core_recv.at[3 + part])
        here(6)
        for part in range(2):
            for bit, other in ORDERS:
                wait_bytes(place(8 | bit, part), near_recv.at[4 + 2 * part + bit // 4])
                if part == bit // 4:
                    near(8 | bit, part, 8 + part, other)
                to_core(8 | bit, part, 7 + 2 * part + bit // 4)
        for bit in (2, 4):
            for part in range(2):
                wait_bytes(place(9 | bit, part), core_recv.at[7 + 2 * part + bit // 4])
            if bit == 2:
                here(10)
        for part in range(2):
            wait_bytes(place(14, part), near_recv.at[8 + part])
            to_core(14, part, 11 + part)
        here(12)
        for part in range(2):
            wait_bytes(place(15, part), core_recv.at[11 + part])
        here(14)
        for copy in copies:
            copy.wait_send()

    return begin, finish


GATHER_SEMS = (DMA((2,)), DMA((2,)), DMA((10,)), DMA((10,)), DMA((13,)), DMA((13,)), DMA)


def scatter_steps(plan, dp, seq, index, pairs, turned, write, bufs, sems, meanwhile=None):
    theirs, mine, got_core, got_first, got_second, got_far = bufs
    core_send, core_recv, send_sems, recv_sems, far_send, far_recv = sems
    rows, width = got_far.shape
    tile = 512
    piece = rows // 4
    copies = []

    def compute(dst, plane, core, blocks):
        starts = [flips(index, core | 2 * m | 8 * plane) * rows for m in blocks]

        @pl.loop(0, width // tile)
        def _(j):
            columns = pl.ds(pl.multiple_of(j * tile, tile), tile)
            block = None
            for l_ref, offset, r_ref in pairs:
                depth = r_ref.shape[1] if turned else r_ref.shape[0]
                some = jnp.concatenate(
                    [
                        l_ref[pl.ds(pl.multiple_of(start, rows), rows), pl.ds(offset, depth)]
                        for start in starts
                    ],
                    axis=0,
                )
                if turned:
                    part = contract_last(some, r_ref[columns, :])
                else:
                    part = dot(some, r_ref[:, columns])
                block = part if block is None else block + part
            block = block.astype(BF)
            for i, m in enumerate(blocks):
                dst[plane, m, :, columns] = block[i * rows : (i + 1) * rows]

    def push(src, dst, send_sem, recv_sem, bit):
        copy = send(src, dst, send_sem, recv_sem, plan.across(dp, seq, bit))
        copies.append(copy)
        return copy

    def add(dst, src, count):
        @pl.loop(0, count // 16)
        def _(i):
            here = pl.ds(pl.multiple_of(i * 16, 16), 16)
            dst[here, :] = dst[here, :] + src[here, :]

    def to_core(plane, blocks):
        started = []
        for m in blocks:
            number = plane * 4 + m
            started.append(
                (
                    push(
                        theirs.at[plane, m],
                        got_core.at[plane, m],
                        core_send.at[number],
                        core_recv.at[number],
                        1,
                    ),
                    m,
                )
            )
        return started

    def add_core(plane, started):
        for copy, m in started:
            copy.wait_recv()
            add(mine.at[plane, m], got_core.at[plane, m], rows)

    def start_of(chunk, part):
        return (chunk * 2 + part) * piece

    def first(plane, chunk):
        started = []
        for part, (bit, other) in enumerate(ORDERS):
            here = pl.ds(start_of(chunk, part), piece)
            for k, keep in enumerate((other, 0)):
                number = (plane * 2 + chunk) * 6 + part * 2 + k
                buffer = got_first.at[plane, chunk, part * 2 + k]
                copy = push(
                    mine.at[plane, (keep | bit) // 2, here],
                    buffer,
                    send_sems.at[number],
                    recv_sems.at[number],
                    bit,
                )
                started.append((copy, keep // 2, here, buffer))
        return started

    def second(plane, chunk):
        started = []
        for part, (bit, other) in enumerate(ORDERS):
            here = pl.ds(start_of(chunk, part), piece)
            number = (plane * 2 + chunk) * 6 + 4 + part
            buffer = got_second.at[plane, chunk, part]
            copy = push(
                mine.at[plane, other // 2, here],
                buffer,
                send_sems.at[number],
                recv_sems.at[number],
                other,
            )
            started.append((copy, 0, here, buffer))
        return started

    def far(chunk):
        here = pl.ds(chunk * 2 * piece, 2 * piece)
        return push(
            mine.at[1, 0, here], got_far.at[here], far_send.at[chunk], far_recv.at[chunk], 8
        )

    def settle(plane, started):
        for copy, m, here, buffer in started:
            copy.wait_recv()
            add(mine.at[plane, m, here], buffer, piece)

    def hook(i):
        if meanwhile is not None:
            meanwhile(i)

    compute(theirs, 1, 1, (3, 1))
    core_a = to_core(1, (3, 1))
    compute(theirs, 1, 1, (2, 0))
    core_b = to_core(1, (2, 0))
    compute(mine, 1, 0, (3, 1, 2, 0))
    hook(0)
    add_core(1, core_a)
    add_core(1, core_b)
    one = [first(1, chunk) for chunk in range(2)]
    compute(theirs, 0, 1, (3, 1, 2, 0))
    core = to_core(0, (3, 1, 2, 0))
    compute(mine, 0, 0, (3, 1, 2, 0))
    hook(1)
    for chunk in range(2):
        settle(1, one[chunk])
        one[chunk] = second(1, chunk)
    add_core(0, core)
    zero = [first(0, chunk) for chunk in range(2)]
    hook(2)
    fars = []
    for chunk in range(2):
        settle(1, one[chunk])
        fars.append(far(chunk))
    hook(3)
    for chunk in range(2):
        settle(0, zero[chunk])
        zero[chunk] = second(0, chunk)
    for chunk in range(2):
        settle(0, zero[chunk])
        fars[chunk].wait_recv()

        @pl.loop(0, 2 * piece // 16)
        def _(i):
            here = pl.ds(pl.multiple_of(chunk * 2 * piece + i * 16, 16), 16)
            write(here, mine[0, 0, here, :].astype(F32) + got_far[here, :].astype(F32))

    for copy in copies:
        copy.wait_send()


def scatter_scratch(rows, width):
    block = (rows, width)
    piece = (rows // 4, width)
    return [
        pltpu.VMEM((2, 4) + block, BF),
        pltpu.VMEM((2, 4) + block, BF),
        pltpu.VMEM((2, 4) + block, BF),
        pltpu.VMEM((2, 2, 4) + piece, BF),
        pltpu.VMEM((2, 2, 2) + piece, BF),
        pltpu.VMEM(block, BF),
        DMA((8,)),
        DMA((8,)),
        DMA((24,)),
        DMA((24,)),
        DMA((2,)),
        DMA((2,)),
    ]


def scatter_call(
    plan, left, rights, turned, collective_id, name, extras, outs, begin, write, gather=False, moves=None
):
    rows = left.shape[0] // plan.size
    width = rights[0].shape[0] if turned else rights[0].shape[1]
    count = len(rights)
    depth = left.shape[1] // count
    moves = moves or [(0, 0, rights[0].shape[0])]

    def kernel(*refs):
        refs = list(refs)

        def take(number):
            taken = refs[:number]
            del refs[:number]
            return taken

        sources, more, results = take(1 + count), take(len(extras)), take(len(outs))
        everyone = take(1) if gather else None
        held, (sem,) = take(1 + count), take(1)
        pieces = [(sources[0], held[0])] + [
            (src.at[pl.ds(first, rows)], dst.at[pl.ds(to, rows)])
            for src, dst in zip(sources[1:], held[1:])
            for first, to, rows in moves
        ]
        loads = Loads(*zip(*pieces), sem)
        pairs = [(held[0], i * depth, held[1 + i]) for i in range(count)]
        dp, seq, index = plan.here()
        greet([plan.across(dp, seq, bit) for bit in (1, 2, 4, 8)])
        begin(results)
        loads.wait()

        def put(here, value):
            write(here, value, more, results)

        scatter_steps(plan, dp, seq, index, pairs, turned, put, refs[:6], refs[6:12])
        if gather:
            start, finish = gather_steps(
                plan, results[-1], everyone[0], dp, seq, index, refs[12:]
            )
            start()
            finish()

    shapes = [jax.ShapeDtypeStruct(*out) for out in outs]
    if gather:
        shapes.append(jax.ShapeDtypeStruct((plan.size * rows, width), outs[-1][1]))
    return pl.pallas_call(
        kernel,
        out_shape=shapes,
        in_specs=[ANY] * (1 + count) + [VM] * len(extras),
        out_specs=[VM] * len(outs) + [ANY] * gather,
        scratch_shapes=[like(value) for value in (left, *rights)]
        + [DMA((1 + count * len(moves),))]
        + scatter_scratch(rows, width)
        + list(GATHER_SEMS) * gather,
        compiler_params=pltpu.CompilerParams(
            collective_id=collective_id, has_side_effects=True, vmem_limit_bytes=60 * 2**20
        ),
        cost_estimate=LIGHT,
        name=name,
    )(left, *rights, *extras)


def rms(values):
    return lax.rsqrt(jnp.mean(values * values, axis=1, keepdims=True) + epsilon)


def rms_back(values, gain, grad):
    r = rms(values)
    scaled = grad * gain
    inner = jnp.mean(scaled * values, axis=1, keepdims=True)
    back = r * scaled - values * (r * r * r * inner)
    return back, jnp.sum(grad * values * r, axis=0, keepdims=True)


def hidden_forward(plan, mixed, w_out, x, gain):
    def write(here, value, extras, outs):
        x_ref, g = extras
        branch, hidden, low = outs
        branch[here, :] = value
        h = x_ref[here, :].astype(F32) + value * rms(value) * g[...]
        hidden[here, :] = h
        low[here, :] = h.astype(BF)

    outs = ((x.shape, F32), (x.shape, F32), (x.shape, BF))
    return scatter_call(
        plan,
        mixed,
        [w_out],
        False,
        2,
        "hidden_forward",
        (x, gain),
        outs,
        lambda outs: None,
        write,
        gather=True,
    )


def output_norm(plan, act, w_down, hidden, grad_out, gain):
    def begin(outs):
        outs[2][...] = jnp.zeros_like(outs[2])

    def write(here, value, extras, outs):
        hidden_ref, dy, g = extras
        output, back, g_gain = outs
        output[here, :] = (hidden_ref[here, :] + value * rms(value) * g[...]).astype(BF)
        grad, part = rms_back(value, g[...], dy[here, :].astype(F32))
        back[here, :] = grad.astype(BF)
        g_gain[...] += part

    outs = ((hidden.shape, BF), (hidden.shape, BF), (gain.shape, F32))
    return scatter_call(
        plan, act, [w_down], False, 6, "output_norm", (hidden, grad_out, gain), outs, begin, write
    )


def hidden_backward(plan, g_low, rights, grad_out, branch, gain):
    def begin(outs):
        outs[1][...] = jnp.zeros_like(outs[1])

    def write(here, value, extras, outs):
        dy, u, g = extras
        grad, g_gain, low = outs
        e = dy[here, :].astype(F32) + value
        grad[here, :] = e
        back, part = rms_back(u[here, :], g[...], e)
        low[here, :] = back.astype(BF)
        g_gain[...] += part

    outs = ((branch.shape, F32), (gain.shape, F32), (branch.shape, BF))
    return scatter_call(
        plan,
        g_low,
        rights,
        True,
        7,
        "hidden_backward",
        (grad_out, branch, gain),
        outs,
        begin,
        write,
        moves=plan.natural(rights[0].shape[0]),
    )


def half_columns(plan, inner, blocks, half):
    each = inner // blocks // plan.size

    def offset(block):
        if blocks > 1:
            return lambda member: half * inner + plan.flat(block, member) * each
        return lambda member: half * inner + member * each

    return [(offset(block), each, block * each) for block in range(blocks)]


def columns_out(plan, dp, index, w_ref, out_ref, table, send_sem, recv_sem):
    own = w_ref.shape[0]
    wide = out_ref.shape[1]
    rows = pl.ds(pl.multiple_of(index * own, own), own)

    def moves(other):
        for offset, each, place in table:
            yield (
                w_ref.at[:, pl.ds(pl.multiple_of(offset(other), 128), each)],
                out_ref.at[rows, pl.ds(place, each)],
            )

    def begin():
        def to(step, carry):
            other = (index + step) % plan.size
            for src, dst in moves(other):
                send(src, dst, send_sem, recv_sem, plan.member(dp, other))
            return carry

        lax.fori_loop(1, plan.size, to, 0)
        for src, dst in moves(index):
            pltpu.make_async_copy(src, dst, recv_sem).start()

    def finish():
        wait_bytes(out_ref, recv_sem)

        def sent(step, carry):
            wait_bytes(w_ref.at[:, pl.ds(0, wide)], send_sem)
            return carry

        lax.fori_loop(1, plan.size, sent, 0)

    return begin, finish


def columns_back(plan, dp, index, g_ref, out_ref, table, send_sem, recv_sem):
    own = g_ref.shape[0] // plan.size

    def moves(other):
        rows = pl.ds(pl.multiple_of(other * own, own), own)
        for offset, each, place in table:
            yield (
                g_ref.at[rows, pl.ds(place, each)],
                out_ref.at[:, pl.ds(pl.multiple_of(offset(index), 128), each)],
            )

    def begin(plane):
        first = flips(index, 8 * plane) // 8 * 8

        def to(step, carry):
            other = first + (index + step) % 8
            for src, dst in moves(other):
                send(src, dst, send_sem, recv_sem, plan.member(dp, other))
            return carry

        lax.fori_loop(1 - plane, 8, to, 0)
        if plane == 0:
            for src, dst in moves(index):
                pltpu.make_async_copy(src, dst, recv_sem).start()

    def finish():
        wait_bytes(g_ref, recv_sem)

        def sent(step, carry):
            wait_bytes(g_ref.at[pl.ds(0, own)], send_sem)
            return carry

        lax.fori_loop(1, plan.size, sent, 0)

    return begin, finish


def start_gather(plan, x, attn_w, gate_up_w, gains, segments, blocks):
    rows, width = x.shape
    own, both = gate_up_w.shape
    table = half_columns(plan, both // 2, blocks, 0)

    count = len(gains)

    def kernel(x_ref, w_ref, u_ref, s_ref, *refs):
        gain_refs, (xo, wo, uo, oo, go, do) = refs[:count], refs[count : count + 6]
        g_ref, d_ref = refs[count + 6 : count + 8]
        sems = refs[count + 8 :]
        gather_sems = sems[:7]
        w_send, w_recv, u_send, u_recv, o_send, o_recv, g_send, g_recv, d_send, d_recv = sems[7:17]
        far_send, far_recv = sems[17:]
        g_ref[...] = jnp.zeros_like(g_ref)
        for i, gain in enumerate(gain_refs):
            g_ref[i : i + 1, :own] = gain[...].astype(F32)
        d_ref[...] = jnp.broadcast_to(s_ref[...], d_ref.shape)
        dp, seq, index = plan.here()
        me = dp * plan.seq + seq
        greet_all(plan, dp, seq)
        begin, finish = gather_steps(plan, x_ref, xo, dp, seq, index, gather_sems)
        group = plan.group_of(dp)

        def columns(part, other):
            return pl.ds(pl.multiple_of(part * width + plan.head(other) * HEAD, HEAD), HEAD)

        def rows_of(member):
            return pl.ds(pl.multiple_of(plan.flat(group, member) * own, own), own)

        def w_to(step, carry):
            other = (index + step) % plan.size
            for part in range(3):
                send(
                    w_ref.at[:, columns(part, other)],
                    wo.at[rows_of(index), pl.ds(part * HEAD, HEAD)],
                    w_send,
                    w_recv.at[index],
                    plan.member(dp, other),
                )
            return carry

        lax.fori_loop(1, plan.size, w_to, 0)
        begin()
        for part in range(3):
            pltpu.make_async_copy(
                w_ref.at[:, columns(part, index)],
                wo.at[rows_of(index), pl.ds(part * HEAD, HEAD)],
                w_recv.at[index],
            ).start()

        def onward(step, carry):
            rows = wo.at[rows_of((index + plan.size - step) % plan.size)]
            wait_bytes(rows, w_recv.at[(index + plan.size - step) % plan.size])
            for away in range(1, plan.groups):
                to_group = (group + away) % plan.groups
                send(rows, rows, far_send, far_recv, plan.in_group(to_group, index))
            return carry

        lax.fori_loop(0, plan.size, onward, 0)
        feature = me * own
        keeper = plan.of_head(feature // HEAD)
        o_dst = oo.at[pl.ds(pl.multiple_of(feature % HEAD, own), own)]
        o_src = w_ref.at[:, pl.ds(3 * width, width)]

        def o_to(away, carry):
            to_group = (group + away) % plan.groups
            to_dp, to_seq = plan.in_group(to_group, keeper)
            same = to_dp * plan.seq + to_seq == me

            @pl.when(same)
            def _():
                pltpu.make_async_copy(o_src, o_dst, o_recv).start()

            @pl.when(jnp.logical_not(same))
            def _():
                send(o_src, o_dst, o_send, o_recv, (to_dp, to_seq))

            return carry

        lax.fori_loop(0, plan.groups, o_to, 0)
        begin_u, finish_u = columns_out(plan, dp, index, u_ref, uo, table, u_send, u_recv)
        begin_u()

        def g_to(step, carry):
            other = (me + step) % plan.devices
            send(g_ref, go.at[me], g_send, g_recv, (other // plan.seq, other % plan.seq))
            return carry

        lax.fori_loop(1, plan.devices, g_to, 0)
        pltpu.make_async_copy(g_ref, go.at[me], g_recv).start()

        def d_to(step, carry):
            send(d_ref, do.at[index], d_send, d_recv, plan.member(dp, (index + step) % plan.size))
            return carry

        lax.fori_loop(1, plan.size, d_to, 0)
        pltpu.make_async_copy(d_ref, do.at[index], d_recv).start()
        finish()
        finish_u()
        wait_bytes(go, g_recv)
        wait_bytes(do, d_recv)
        far = wo.at[pl.ds(0, (plan.groups - 1) * plan.size * own)]
        wait_bytes(far, far_recv)
        wait_bytes(far, far_send)

        def sent(step, carry):
            wait_bytes(g_ref, g_send)
            return carry

        lax.fori_loop(1, plan.devices, sent, 0)

        def sent_w(step, carry):
            wait_bytes(w_ref.at[:, pl.ds(0, 3 * HEAD)], w_send)
            return carry

        lax.fori_loop(1, plan.size, sent_w, 0)

        def sent_docs(step, carry):
            wait_bytes(d_ref, d_send)
            return carry

        lax.fori_loop(1, plan.size, sent_docs, 0)
        wait_bytes(oo, o_recv)

        def sent_o(away, carry):
            to_group = (group + away) % plan.groups
            to_dp, to_seq = plan.in_group(to_group, keeper)

            @pl.when(to_dp * plan.seq + to_seq != me)
            def _():
                wait_bytes(o_src, o_send)

            return carry

        lax.fori_loop(0, plan.groups, sent_o, 0)

    shapes = (
        ((plan.size * rows, width), BF),
        ((plan.devices * own, 3 * HEAD), BF),
        ((plan.size * own, both // 2 // plan.size), BF),
        ((HEAD, width), BF),
        ((plan.devices, 8, 128), F32),
        ((plan.size, 8, rows), jnp.int32),
    )
    return pl.pallas_call(
        kernel,
        out_shape=[jax.ShapeDtypeStruct(*shape) for shape in shapes],
        in_specs=[ANY] * 3 + [VM] * (1 + count),
        out_specs=[ANY] * 6,
        scratch_shapes=[pltpu.VMEM((8, 128), F32), pltpu.VMEM((8, rows), jnp.int32)]
        + list(GATHER_SEMS)
        + [DMA, DMA((plan.size,))]
        + [DMA] * 10,
        compiler_params=pltpu.CompilerParams(collective_id=0, has_side_effects=True),
        cost_estimate=LIGHT,
        name="start_gather",
    )(x, attn_w, gate_up_w, segments, *[gain.reshape(1, own) for gain in gains])


def dot(left, right):
    return jnp.dot(left, right, preferred_element_type=F32)


def contract_last(left, right):
    return lax.dot_general(left, right, (((1,), (1,)), ((), ())), preferred_element_type=F32)


def contract_first(left, right):
    return lax.dot_general(left, right, (((0,), (0,)), ((), ())), preferred_element_type=F32)


def chip_rows(index, chip, rows):
    return pl.multiple_of(flips(index, chip) // 2 * (2 * rows), 2 * rows)


def ffn_forward(plan, h_all, w_gate, w_up):
    tokens, width = h_all.shape
    units = w_gate.shape[1]
    moves = plan.natural(width)

    def kernel(h, wg_ref, wu_ref, gate, up, act, wg, wu, sem):
        @pl.when(pl.program_id(0) == 0)
        def _():
            pieces = [
                (src.at[pl.ds(first, rows)], dst.at[pl.ds(to, rows)])
                for src, dst in ((wg_ref, wg), (wu_ref, wu))
                for first, to, rows in moves
            ]
            Loads(*zip(*pieces), sem).wait()

        values = h[...]
        g = dot(values, wg[...])
        u = dot(values, wu[...])
        gate[...] = g.astype(BF)
        up[...] = u.astype(BF)
        act[...] = (g * jax.nn.sigmoid(g) * u).astype(BF)

    rows = 2 * STEP
    part = pl.BlockSpec((rows, units), lambda i: (i, 0))
    return pl.pallas_call(
        kernel,
        grid=(tokens // rows,),
        out_shape=[jax.ShapeDtypeStruct((tokens, units), BF)] * 3,
        in_specs=[pl.BlockSpec((rows, width), lambda i: (i, 0)), ANY, ANY],
        out_specs=[part] * 3,
        scratch_shapes=[like(w_gate), like(w_up), DMA((2 * len(moves),))],
        compiler_params=pltpu.CompilerParams(vmem_limit_bytes=60 * 2**20),
        cost_estimate=LIGHT,
        name="ffn_forward",
    )(h_all, w_gate, w_up)


def ffn_backward(plan, d, h_all, w_down, gate, up, act):
    rows, width = d.shape
    tokens = rows * plan.size
    units = gate.shape[1]
    at_dp = width // plan.dp
    tile = 256
    two = 2 * rows

    def kernel(d_ref, *refs):
        ins, refs = refs[:5], refs[5:]
        outs, (h_all, wd, gate, up, act) = refs[:4], refs[4:9]
        d_all, gu_turned, act_turned, gu_sum, down_sum, out, g_gate, g_up, g_down = refs[9:18]
        sems, load_sems, store_sems, out_sems = refs[18:25], refs[25], refs[26], refs[27]
        dp, seq, index = plan.here()
        loads = Loads(ins, (wd, gate, up, act, h_all), load_sems)
        greet([plan.across(dp, seq, bit) for bit in (1, 2, 4, 8)])
        begin, finish = gather_steps(plan, d_ref, d_all, dp, seq, index, sems)
        begin()
        stores = []
        pair = []

        def products(first, last):
            chips = [pl.ds(chip_rows(index, chip, rows), two) for chip in pair]

            @pl.loop(0, width // tile)
            def _(i):
                columns = pl.ds(pl.multiple_of(i * tile, tile), tile)
                block = dot(
                    gu_turned[...],
                    jnp.concatenate([h_all[chip, columns] for chip in chips], axis=0),
                )
                if not first:
                    block = gu_sum[:, columns] + block
                if last:
                    block = block.T.astype(BF)
                    row = i * tile
                    row = plan.place(row // at_dp) * at_dp + row % at_dp
                    to = pl.ds(pl.multiple_of(row, tile), tile)
                    g_gate[to, :] = block[:, :units]
                    g_up[to, :] = block[:, units:]
                else:
                    gu_sum[:, columns] = block

            @pl.loop(0, width // tile)
            def _(i):
                columns = pl.ds(pl.multiple_of(i * tile, tile), tile)
                block = dot(
                    act_turned[...],
                    jnp.concatenate([d_all[chip, columns] for chip in chips], axis=0),
                )
                if not first:
                    block = down_sum[:, columns] + block
                if last:
                    g_down[:, columns] = block.astype(BF)
                else:
                    down_sum[:, columns] = block

        def use(chip):
            if chip == 0:
                loads.wait()
            some = pl.ds(chip_rows(index, chip, rows), two)
            columns = pl.ds(len(pair) * two, two)
            grad = contract_last(d_all[some, :], wd[...])
            g = gate[some, :].astype(F32)
            u = up[some, :].astype(F32)
            sigma = jax.nn.sigmoid(g)
            grad_gate = (grad * u * sigma * (1.0 + g * (1.0 - sigma))).astype(BF)
            grad_up = (grad * (g * sigma)).astype(BF)
            out[some, pl.ds(0, units)] = grad_gate
            out[some, pl.ds(units, units)] = grad_up
            store = pltpu.make_async_copy(out.at[some], outs[0].at[some], store_sems.at[chip // 2])
            store.start()
            stores.append(store)
            gu_turned[pl.ds(0, units), columns] = grad_gate.T
            gu_turned[pl.ds(units, units), columns] = grad_up.T
            act_turned[:, columns] = act[some, :].T
            pair.append(chip)
            if len(pair) == 2:
                products(len(stores) == 2, len(stores) == 8)
                pair.clear()

        finish(use)
        for i, src in enumerate((g_gate, g_up, g_down)):
            store = pltpu.make_async_copy(src, outs[1 + i], out_sems.at[i])
            store.start()
            stores.append(store)
        for store in stores:
            store.wait()

    return pl.pallas_call(
        kernel,
        out_shape=[
            jax.ShapeDtypeStruct((tokens, 2 * units), BF),
            jax.ShapeDtypeStruct((width, units), BF),
            jax.ShapeDtypeStruct((width, units), BF),
            jax.ShapeDtypeStruct((units, width), BF),
        ],
        in_specs=[VM] + [ANY] * 5,
        out_specs=[ANY] * 4,
        scratch_shapes=[
            pltpu.VMEM(shape, BF)
            for shape in (h_all.shape, (units, width), gate.shape, up.shape, act.shape, h_all.shape)
        ]
        + [
            pltpu.VMEM((2 * units, 2 * two), BF),
            pltpu.VMEM((units, 2 * two), BF),
            pltpu.VMEM((2 * units, width), F32),
            pltpu.VMEM((units, width), F32),
            pltpu.VMEM((tokens, 2 * units), BF),
            pltpu.VMEM((width, units), BF),
            pltpu.VMEM((width, units), BF),
            pltpu.VMEM((units, width), BF),
        ]
        + list(GATHER_SEMS)
        + [DMA((5,)), DMA((8,)), DMA((3,))],
        compiler_params=pltpu.CompilerParams(
            collective_id=10, has_side_effects=True, vmem_limit_bytes=62 * 2**20
        ),
        cost_estimate=LIGHT,
        name="ffn_backward",
    )(d, w_down, gate, up, act, h_all)


def row_sums(values):
    ones = jnp.ones((8, values.shape[1]), F32)
    sums = lax.dot_general(
        ones,
        values,
        (((1,), (1,)), ((), ())),
        precision=lax.Precision.HIGHEST,
        preferred_element_type=F32,
    )
    return sums[:1]


def spread_sums(rows):
    ones = jnp.ones((rows.shape[0], HEAD), F32)
    return lax.dot_general(
        rows,
        ones,
        (((0,), (0,)), ((), ())),
        precision=lax.Precision.HIGHEST,
        preferred_element_type=F32,
    )


STEP = 256


def lay_out(docs_ref, row_ref):
    for i in range(docs_ref.shape[0]):
        rows = docs_ref.shape[2]
        row_ref[:, i * rows : (i + 1) * rows] = docs_ref[i, :1, :].astype(F32)


def my_gain(plan, gains_ref, which, head):
    own = HEAD // plan.pieces
    parts = [gains_ref[head * plan.pieces + i, which : which + 1, :own] for i in range(plan.pieces)]
    return jnp.concatenate(parts, axis=1)


def scores_of(q, k, q_docs, k_docs, start):
    scores = contract_last(q, k) * HEAD ** (-0.5)
    row = start + lax.broadcasted_iota(jnp.int32, scores.shape, 0)
    column = lax.broadcasted_iota(jnp.int32, scores.shape, 1)
    allowed = (column <= row) & (spread_sums(q_docs)[:, :1] == k_docs)
    scores = jnp.where(allowed, scores, -1e30)
    top = jnp.max(scores, axis=1, keepdims=True)
    weights = jnp.exp(scores - top)
    return weights / jnp.sum(weights, axis=1, keepdims=True)


def swap_sums(plan, dp, index, mine, held, s_sem, r_sem):
    def begin():
        def to(step, carry):
            send(mine, held.at[index], s_sem, r_sem, plan.member(dp, (index + step) % plan.size))
            return carry

        pltpu.make_async_copy(mine, held.at[index], r_sem).start()
        lax.fori_loop(1, plan.size, to, 0)

    def finish():
        wait_bytes(held, r_sem)
        wait_bytes(held.at[pl.ds(0, plan.size - 1)], s_sem)

    return begin, finish


def attend_forward(
    plan, x_all, w_qkv, gate_up_w, gains, docs, cosine, sine, blocks
):
    tokens, width = x_all.shape
    length = cosine.shape[0]
    own, both = gate_up_w.shape
    table = half_columns(plan, both // 2, blocks, 1)

    def kernel(x_ref, wq_ref, up, ga, do, cs_ref, sn_ref, uo, q, k, sums, ql, kl, vl, mixed, *rest):
        x, wq, cs, sn, sem = rest[:5]
        loads = Loads((wq_ref, cs_ref, sn_ref), (wq, cs, sn), sem)
        step_rows = [pl.ds(i * STEP, STEP) for i in range(tokens // STEP)]
        Loads(
            [x_ref.at[rows] for rows in step_rows], [x.at[rows] for rows in step_rows], rest[5]
        )
        tile_sem, rest = rest[5], rest[6:]
        gn, dr, stats, held, t_send, t_recv, u_send, u_recv = rest
        dp, seq, index = plan.here()
        greet_group(plan, dp, index)
        lay_out(do, dr)
        for which in range(2):
            gn[which : which + 1, :] = my_gain(plan, ga, which, plan.head(index))
        loads.wait()

        @pl.loop(0, tokens // STEP)
        def _(i):
            rows = pl.ds(pl.multiple_of(i * STEP, STEP), STEP)
            pltpu.make_async_copy(x_ref.at[rows], x.at[rows], tile_sem.at[i]).wait()
            block = dot(x[rows, :], wq[...])
            q[rows, :] = block[:, :HEAD]
            k[rows, :] = block[:, HEAD : 2 * HEAD]
            vl[rows, :] = block[:, 2 * HEAD :].astype(BF)
            stats[0, :, rows] = row_sums(block[:, :HEAD] * block[:, :HEAD])
            stats[1, :, rows] = row_sums(block[:, HEAD : 2 * HEAD] * block[:, HEAD : 2 * HEAD])

        begin, finish = swap_sums(plan, dp, index, stats, held, t_send, t_recv)
        begin()
        begin_u, finish_u = columns_out(plan, dp, index, up, uo, table, u_send, u_recv)
        begin_u()
        finish()
        for which in range(2):
            sums[which] = jnp.sum(held[:, which, 0, :], axis=0, keepdims=True)

        @pl.loop(0, tokens // STEP)
        def _(i):
            rows = pl.ds(pl.multiple_of(i * STEP, STEP), STEP)
            places = pl.ds(pl.multiple_of((i % (length // STEP)) * STEP, STEP), STEP)
            for which, raw, low in ((0, q, ql), (1, k, kl)):
                r = lax.rsqrt(spread_sums(sums[which, :, rows]) / width + epsilon)
                values = raw[rows, :] * r * gn[which : which + 1, :]
                turned = values * cs[places, :] + pltpu.roll(values, HEAD // 2, 1) * sn[places, :]
                low[rows, :] = turned.astype(BF)

        @pl.loop(0, tokens // length)
        def _(b):
            for j in range(length // STEP):
                start = pl.multiple_of(b * length + j * STEP, STEP)
                rows = pl.ds(start, STEP)
                keys = pl.ds(pl.multiple_of(b * length, length), (j + 1) * STEP)
                probs = scores_of(
                    ql[rows, :], kl[keys, :], dr[:, rows], dr[:, keys], j * STEP
                )
                mixed[rows, :] = dot(probs.astype(BF), vl[keys, :]).astype(BF)

        finish_u()

    per_head = (tokens, HEAD)
    shapes = (
        ((plan.size * own, both // 2 // plan.size), BF),
        (per_head, F32),
        (per_head, F32),
        ((2, 1, tokens), F32),
        (per_head, BF),
        (per_head, BF),
        (per_head, BF),
        (per_head, BF),
    )
    return pl.pallas_call(
        kernel,
        out_shape=[jax.ShapeDtypeStruct(*shape) for shape in shapes],
        in_specs=[ANY] * 3 + [VM] * 2 + [ANY] * 2,
        out_specs=[ANY] + [VM] * 7,
        scratch_shapes=[like(value) for value in (x_all, w_qkv, cosine, sine)]
        + [DMA((3,)), DMA((tokens // STEP,))]
        + [
            pltpu.VMEM((8, HEAD), F32),
            pltpu.VMEM((1, tokens), F32),
            pltpu.VMEM((2, 1, tokens), F32),
            pltpu.VMEM((plan.size, 2, 1, tokens), F32),
        ]
        + [DMA] * 4,
        compiler_params=pltpu.CompilerParams(
            collective_id=3, has_side_effects=True, vmem_limit_bytes=56 * 2**20
        ),
        cost_estimate=LIGHT,
        name="attend_forward",
    )(x_all, w_qkv, gate_up_w, gains, docs, cosine, sine)


def attend_backward(
    plan,
    b,
    w_out,
    q,
    k,
    sums,
    ql,
    kl,
    vl,
    mixed,
    gains,
    docs,
    cosine,
    sine,
    g_gate,
    blocks,
):
    rows_here, width = b.shape
    tokens = rows_here * plan.size
    own = g_gate.shape[0] // plan.size
    inner = g_gate.shape[1] * plan.size
    length = cosine.shape[0]
    scale = HEAD ** (-0.5)

    def kernel(*refs):
        b_ref, sums, ga, do, gg = refs[:5]
        wo, q, k, ql, kl, vl, mx, cs, sn = refs[30:39]
        loads = Loads(refs[5:14], refs[30:39], refs[39])
        dqkv, g_out, g_gain, gate_out = refs[14:18]
        ba, dq, dk, dv, gn, dr, stats, held, t_send, t_recv, gg_send, gg_recv = refs[18:30]
        dp, seq, index = plan.here()
        greet_group(plan, dp, index)
        begin_b, finish_b = gather_steps(plan, b_ref, ba, dp, seq, index, refs[40:])
        begin_b()
        lay_out(do, dr)
        for which in range(2):
            gn[which : which + 1, :] = my_gain(plan, ga, which, plan.head(index))
        begin_g, finish_g = columns_back(
            plan, dp, index, gg, gate_out, half_columns(plan, inner, blocks, 0), gg_send, gg_recv
        )
        dk[...] = jnp.zeros_like(dk)
        dv[...] = jnp.zeros_like(dv)

        def use(chip):
            if chip == 0:
                loads.wait()
            if chip == 8:
                begin_g(1)
            if chip == 10:
                begin_g(0)
            first = chip_rows(index, chip, rows_here)
            rows = pl.ds(first, STEP)
            start = first % length

            def block(count):
                keys = pl.ds(pl.multiple_of(first - start, STEP), count)
                grad = contract_last(ba[rows, :], wo[...]).astype(BF)
                probs = scores_of(ql[rows, :], kl[keys, :], dr[:, rows], dr[:, keys], start)
                grad_probs = contract_last(grad, vl[keys, :])
                delta = jnp.sum(probs * grad_probs, axis=1, keepdims=True)
                grad_scores = (probs * (grad_probs - delta)).astype(BF)
                dq[rows, :] = dot(grad_scores, kl[keys, :]) * scale
                dk[keys, :] += contract_first(grad_scores, ql[rows, :]) * scale
                dv[keys, :] += contract_first(probs.astype(BF), grad)

            @pl.when(start < length // 2)
            def _():
                block(length // 2)

            @pl.when(start >= length // 2)
            def _():
                block(length)

        finish_b(use)

        @pl.loop(0, tokens // STEP)
        def _(i):
            rows = pl.ds(pl.multiple_of(i * STEP, STEP), STEP)
            places = pl.ds(pl.multiple_of((i % (length // STEP)) * STEP, STEP), STEP)
            for which, raw, grad in ((0, q, dq), (1, k, dk)):
                values = grad[rows, :]
                turned = values * cs[places, :] - pltpu.roll(values, HEAD // 2, 1) * sn[places, :]
                grad[rows, :] = turned
                stats[which, :, rows] = row_sums(turned * gn[which : which + 1, :] * raw[rows, :])

        begin, finish = swap_sums(plan, dp, index, stats, held, t_send, t_recv)
        begin()
        turned_mixed = mx[...].T

        @pl.loop(0, width // 512)
        def _(i):
            columns = pl.ds(pl.multiple_of(i * 512, 512), 512)
            g_out[:, columns] = dot(turned_mixed, ba[:, columns]).astype(BF)

        g_gain[...] = jnp.zeros_like(g_gain)
        finish()

        @pl.loop(0, tokens // STEP)
        def _(i):
            rows = pl.ds(pl.multiple_of(i * STEP, STEP), STEP)
            for which, raw, grad in ((0, q, dq), (1, k, dk)):
                total = spread_sums(held[:, which, 0, rows])
                r = lax.rsqrt(spread_sums(sums[which, :, rows]) / width + epsilon)
                u = raw[rows, :]
                e = grad[rows, :]
                back = r * (gn[which : which + 1, :] * e) - u * (r * r * r * (total / width))
                dqkv[rows, pl.ds(which * HEAD, HEAD)] = back.astype(BF)
                g_gain[which : which + 1, :] += jnp.sum(e * u * r, axis=0, keepdims=True)
            dqkv[rows, pl.ds(2 * HEAD, HEAD)] = dv[rows, :].astype(BF)

        finish_g()

    per_head = (tokens, HEAD)
    shapes = (
        ((tokens, 3 * HEAD), BF),
        ((HEAD, width), BF),
        ((8, HEAD), F32),
        ((own, inner), BF),
    )
    return pl.pallas_call(
        kernel,
        out_shape=[jax.ShapeDtypeStruct(*shape) for shape in shapes],
        in_specs=[VM] * 4 + [ANY] * 10,
        out_specs=[VM] * 3 + [ANY],
        scratch_shapes=[
            pltpu.VMEM((tokens, width), BF),
            pltpu.VMEM(per_head, F32),
            pltpu.VMEM(per_head, F32),
            pltpu.VMEM(per_head, F32),
            pltpu.VMEM((8, HEAD), F32),
            pltpu.VMEM((1, tokens), F32),
            pltpu.VMEM((2, 1, tokens), F32),
            pltpu.VMEM((plan.size, 2, 1, tokens), F32),
        ]
        + [DMA] * 4
        + [like(value) for value in (w_out, q, k, ql, kl, vl, mixed, cosine, sine)]
        + [DMA((9,))]
        + list(GATHER_SEMS),
        compiler_params=pltpu.CompilerParams(
            collective_id=4, has_side_effects=True, vmem_limit_bytes=56 * 2**20
        ),
        cost_estimate=LIGHT,
        name="attend_backward",
    )(b, sums, gains, docs, g_gate, w_out, q, k, ql, kl, vl, mixed, cosine, sine)


def finish_backward(
    plan, dqkv, w_qkv, x_all, g_up, g_out, g_head, g_attn, g_ffn, before, blocks
):
    tokens, width = x_all.shape
    own = width // plan.devices
    rows = tokens // plan.size
    inner = g_up.shape[1] * plan.size
    pieces = HEAD // own
    tile = 256
    at_dp = width // plan.dp
    per_dp = at_dp // tile
    tiles = width // plan.groups // tile

    def kernel(dq_ref, wq_ref, x_ref, gu, go, gh, gat, gff, bf, ig, w_grad, up_out, ga_out, *rest):
        (dq, wq, x), load_sem = rest[:3], rest[3]
        loads = Loads((dq_ref, wq_ref, x_ref), (dq, wq, x), load_sem)
        rest = rest[4:]
        bufs, sems = rest[:6], rest[6:12]
        turned, gq, gq_far, got_x, got_q, got_o, ga = rest[12:19]
        q_s, q_r, o_s, o_r, ga_s, ga_r, gu_s, gu_r, x_s, x_r = rest[19:]
        dp, seq, index = plan.here()
        me = dp * plan.seq + seq
        group = plan.group_of(dp)
        greet_all(plan, dp, seq)

        def device_of(flat):
            return flat // plan.seq, flat % plan.seq

        def o_to(piece, carry):
            other = plan.head(index) * pieces + piece
            src = go.at[pl.ds(pl.multiple_of(piece * own, own), own)]

            @pl.when(other == me)
            def _():
                pltpu.make_async_copy(src, got_o.at[group], o_r).start()

            @pl.when(other != me)
            def _():
                send(src, got_o.at[group], o_s, o_r, device_of(other))

            return carry

        def ga_to(step, carry):
            other = (me + step) % plan.devices
            send(ga.at[other], ga_out.at[me], ga_s, ga_r, device_of(other))
            return carry

        table = half_columns(plan, inner, blocks, 0)
        begin_u, finish_u = columns_back(plan, dp, index, gu, up_out, table, gu_s, gu_r)

        def product(of_group, u):
            row = plan.dp_of(of_group, u // per_dp) * at_dp + (u % per_dp) * tile
            block = dot(turned[...], x[:, pl.ds(pl.multiple_of(row, tile), tile)])
            return block.T.astype(BF)

        def others():
            for away in range(1, plan.groups):
                to_group = (group + away) % plan.groups

                @pl.loop(0, tiles)
                def _(u, away=away, to_group=to_group):
                    gq_far[away - 1, u] = product(to_group, u)
                    send(
                        gq_far.at[away - 1, u],
                        got_x.at[away - 1, u],
                        x_s,
                        x_r.at[away - 1, u],
                        plan.in_group(to_group, index),
                    )

        def ours():
            @pl.loop(0, tiles)
            def _(u):
                gq[u] = product(group, u)

        def collect():
            @pl.loop(0, tiles)
            def _(u):
                total = gq[u].astype(F32)
                for away in range(1, plan.groups):
                    wait_bytes(got_x.at[away - 1, u], x_r.at[away - 1, u])
                    total = total + got_x[away - 1, u].astype(F32)
                gq[u] = total.astype(BF)
                owner_dp = plan.dp_of(group, u // per_dp)
                for piece in range(tile // own):
                    owner_seq = (u % per_dp) * (tile // own) + piece
                    src = gq.at[u, pl.ds(piece * own, own)]
                    mine = owner_dp * plan.seq + owner_seq == me

                    @pl.when(mine)
                    def _(src=src):
                        pltpu.make_async_copy(src, got_q.at[index], q_r).start()

                    @pl.when(jnp.logical_not(mine))
                    def _(src=src, owner_seq=owner_seq):
                        send(src, got_q.at[index], q_s, q_r, (owner_dp, owner_seq))

        def meanwhile(i):
            if i == 0:
                loads.wait(2)
                turned[...] = dq[...].T
                others()
            elif i == 1:
                ours()
            elif i == 2:
                lax.fori_loop(0, pieces, o_to, 0)
            else:
                collect()
                ga[...] = jnp.zeros_like(ga)
                for other in range(plan.devices):
                    part = slice(other * own, (other + 1) * own)
                    ga[other, 2:3, :own] = gat[:, part]
                    ga[other, 3:4, :own] = gff[:, part]
                for piece in range(pieces):
                    part = slice(piece * own, (piece + 1) * own)
                    ga[plan.head(index) * pieces + piece, 0:2, :own] = gh[0:2, part]
                lax.fori_loop(1, plan.devices, ga_to, 0)
                pltpu.make_async_copy(ga.at[me], ga_out.at[me], ga_r).start()

        def write(here, value):
            ig[here, :] = bf[here, :] + value

        begin_u(1)
        begin_u(0)
        loads.wait(0, 1)
        scatter_steps(plan, dp, seq, index, [(dq, 0, wq)], True, write, bufs, sems, meanwhile)
        wait_bytes(got_o, o_r)
        wait_bytes(got_q, q_r)
        for part in range(3):
            for member in range(plan.size):
                total = got_q[member, :, part * HEAD : (part + 1) * HEAD].astype(F32)
                w_grad[:, pl.ds(part * width + plan.head(member) * HEAD, HEAD)] = total
        total = got_o[0].astype(F32)
        for other in range(1, plan.groups):
            total = total + got_o[other].astype(F32)
        w_grad[:, pl.ds(3 * width, width)] = total
        finish_u()
        wait_bytes(ga_out, ga_r)
        wait_bytes(ga_out.at[pl.ds(0, plan.devices - 1)], ga_s)
        wait_bytes(got_q.at[pl.ds(0, plan.size - 1)], q_s)
        wait_bytes(gq_far, x_s)

        def sent_o(piece, carry):
            @pl.when(plan.head(index) * pieces + piece != me)
            def _():
                wait_bytes(go.at[pl.ds(0, own)], o_s)

            return carry

        lax.fori_loop(0, pieces, sent_o, 0)

    shapes = (
        ((rows, width), F32),
        ((own, 4 * width), F32),
        ((own, inner), BF),
        ((plan.devices, 8, 128), F32),
    )
    return pl.pallas_call(
        kernel,
        out_shape=[jax.ShapeDtypeStruct(*shape) for shape in shapes],
        in_specs=[ANY] * 5 + [VM] * 4,
        out_specs=[VM, VM, ANY, VM],
        scratch_shapes=[like(value) for value in (dqkv, w_qkv, x_all)]
        + [DMA((3,))]
        + scatter_scratch(rows, width)
        + [
            pltpu.VMEM((3 * HEAD, tokens), BF),
            pltpu.VMEM((tiles, tile, 3 * HEAD), BF),
            pltpu.VMEM((plan.groups - 1, tiles, tile, 3 * HEAD), BF),
            pltpu.VMEM((plan.groups - 1, tiles, tile, 3 * HEAD), BF),
            pltpu.VMEM((plan.size, own, 3 * HEAD), BF),
            pltpu.VMEM((plan.groups, own, width), BF),
            pltpu.VMEM((plan.devices, 8, 128), F32),
        ]
        + [DMA] * 9
        + [DMA((plan.groups - 1, tiles))],
        compiler_params=pltpu.CompilerParams(
            collective_id=5, has_side_effects=True, vmem_limit_bytes=60 * 2**20
        ),
        cost_estimate=LIGHT,
        name="finish_backward",
    )(dqkv, w_qkv, x_all, g_up, g_out, g_head, g_attn, g_ffn, before)


def per_device(
    plan,
    hidden_in,
    segments,
    attn_weights,
    q_gain,
    k_gain,
    attn_gain,
    ffn_gain,
    gate_up_weights,
    down_weights,
    cotangent,
):
    x = hidden_in[0]
    rows, width = x.shape
    own = attn_weights.shape[0]
    inner = gate_up_weights.shape[1] // 2
    length = rows * plan.seq
    tokens = rows * plan.size
    groups = plan.groups
    dp, seq, index = plan.here()
    me = dp * plan.seq + seq
    direct = (inner // (groups * plan.size)) % 128 == 0
    blocks = groups if direct else 1

    across = [[plan.dp_of(high, low) for high in range(groups)] for low in range(plan.low)]

    def join_groups(value):
        return lax.all_gather(value, "dp", axis_index_groups=across, axis=0, tiled=True)

    def sum_groups(value):
        return lax.psum_scatter(
            value.astype(BF), "dp", axis_index_groups=across, scatter_dimension=0, tiled=True
        )

    x_all, w_qkv, gate_part, w_out, gains_all, docs = start_gather(
        plan,
        x,
        attn_weights,
        gate_up_weights,
        [q_gain, k_gain, attn_gain, ffn_gain],
        segments,
        blocks,
    )
    w_gate = join_groups(gate_part)
    gains = jnp.transpose(gains_all[:, 2:4, :own], (1, 0, 2)).reshape(2, width)
    positions = np.arange(length, dtype=np.float32)
    frequency = rope_base ** (-2.0 * np.arange(HEAD // 2, dtype=np.float32) / HEAD)
    angles = positions[:, None] * frequency.astype(np.float32)[None, :]
    cosine = jnp.asarray(np.concatenate([np.cos(angles)] * 2, axis=1), F32)
    sine = jnp.asarray(np.concatenate([-np.sin(angles), np.sin(angles)], axis=1), F32)

    up_part, q, k, row_sums_qk, q_low, k_low, v_low, mixed = attend_forward(
        plan,
        x_all,
        w_qkv,
        gate_up_weights,
        gains_all,
        docs,
        cosine,
        sine,
        blocks,
    )
    w_up = join_groups(up_part)
    down_weights, _ = lax.optimization_barrier((down_weights, up_part))
    if direct:
        w_down = join_groups(down_weights)
    else:
        w_all = lax.all_gather(down_weights, ("dp", "seq"), axis=0, tiled=True)
        each = inner // plan.size
        w_down = lax.dynamic_slice_in_dim(w_all, index * each, each, 0)
    branch, hidden, _, h_all = hidden_forward(plan, mixed, w_out, x, gains[:1])
    branch, w_gate = lax.optimization_barrier((branch, w_gate))

    gate, up, act = ffn_forward(plan, h_all, w_gate, w_up)
    output, grad_down_in, grad_fg = output_norm(
        plan, act, w_down, hidden, cotangent[0], gains[1:]
    )

    gu_low, g_gate, g_up, g_down = ffn_backward(
        plan, grad_down_in, h_all, w_down, gate, up, act
    )
    g_gate = sum_groups(g_gate)
    g_up = sum_groups(g_up)
    if direct:
        grad_down = sum_groups(g_down).astype(F32)
    else:
        spread = jnp.zeros((inner, width), BF)
        spread = lax.dynamic_update_slice_in_dim(spread, g_down, index * g_down.shape[0], 0)
        grad_down = lax.psum_scatter(
            spread, ("dp", "seq"), scatter_dimension=0, tiled=True
        ).astype(F32)

    grad_hidden, grad_ag, grad_branch = hidden_backward(
        plan, gu_low, [w_gate, w_up], cotangent[0], branch, gains[:1]
    )
    dqkv, g_out, g_head, gate_rows = attend_backward(
        plan,
        grad_branch,
        w_out,
        q,
        k,
        row_sums_qk,
        q_low,
        k_low,
        v_low,
        mixed,
        gains_all,
        docs,
        cosine,
        sine,
        g_gate,
        blocks,
    )

    input_grad, grad_attn, up_rows, gain_rows = finish_backward(
        plan,
        dqkv,
        w_qkv,
        x_all,
        g_up,
        g_out,
        g_head,
        grad_ag,
        grad_fg,
        grad_hidden,
        blocks,
    )
    grad_gate_up = jnp.concatenate([gate_rows, up_rows], axis=1).astype(F32)
    gain_grads = jnp.sum(gain_rows, axis=0)[:4, :own]
    return (
        output[None],
        input_grad[None],
        grad_attn,
        grad_gate_up,
        grad_down,
        gain_grads[0],
        gain_grads[1],
        gain_grads[2],
        gain_grads[3],
    )


def solution(mesh):
    by_token = P("dp", "seq", None)
    by_row = P(("dp", "seq"), None)
    by_gain = P(("dp", "seq"))

    def run(hidden_in, segments, attn_weights, *rest):
        plan = Plan(mesh, hidden_in.shape[2] // HEAD)
        return jax.shard_map(
            functools.partial(per_device, plan),
            mesh=mesh,
            in_specs=(by_token, P("dp", "seq"), by_row)
            + (by_gain,) * 4
            + (by_row, by_row, by_token),
            out_specs=(by_token, by_token, by_row, by_row, by_row) + (by_gain,) * 4,
            check_vma=False,
        )(hidden_in, segments, attn_weights, *rest)

    return run
```

```python
import functools

import jax
import jax.numpy as jnp
import numpy as np
from jax import lax
from jax.experimental import pallas as pl
from jax.experimental.pallas import tpu as pltpu
from jax.sharding import PartitionSpec as P

HEAD = 128
epsilon = 1e-06
rope_base = 500000.0
MESH = pl.DeviceIdType.MESH
BF = jnp.bfloat16
F32 = jnp.float32
ANY = pl.BlockSpec(memory_space=pl.ANY)
VM = pl.BlockSpec(memory_space=pltpu.VMEM)
DMA = pltpu.SemaphoreType.DMA
LIGHT = pl.CostEstimate(flops=0, bytes_accessed=0, transcendentals=0)


class Plan:
    def __init__(self, mesh, heads):
        self.dp = mesh.shape["dp"]
        self.seq = mesh.shape["seq"]
        self.size = heads
        self.low = heads // self.seq
        self.groups = self.dp // self.low
        self.devices = self.dp * self.seq
        self.pieces = self.devices // heads
        self.chips = self.seq // 2
        self.by_chip = self.groups == 2 and self.size == self.dp * self.chips

    def group_of(self, dp):
        return dp % self.groups + (dp // self.groups) * (self.groups - 1 - 2 * (dp % self.groups))

    def dp_of(self, group, low):
        return low * self.groups + group + low * (self.groups - 1 - 2 * group)

    def flat(self, group, index):
        return self.dp_of(group, index // self.seq) * self.seq + index % self.seq

    def place(self, dp):
        return self.group_of(dp) * self.low + dp // self.groups

    def natural(self, rows):
        if self.low == 1:
            return [(0, 0, rows)]
        count = rows // self.dp
        return [(self.place(i) * count, i * count, count) for i in range(self.dp)]

    def here(self):
        dp = lax.axis_index("dp")
        seq = lax.axis_index("seq")
        return dp, seq, (dp // self.groups) * self.seq + seq

    def head(self, index):
        if self.by_chip:
            return self.dp_of(index % 2, index // self.seq) * self.chips + (index % self.seq) // 2
        return index

    def of_head(self, head):
        if self.by_chip:
            dp = head // self.chips
            low = dp // self.groups
            return low * self.seq + (head % self.chips) * 2 + self.group_of(dp)
        return head

    def in_group(self, group, index):
        return self.dp_of(group, index // self.seq), index % self.seq

    def member(self, dp, index):
        return self.in_group(self.group_of(dp), index)

    def across(self, dp, seq, bit):
        if bit < self.seq:
            return dp, flip(seq, bit)
        return 2 * self.groups - 1 - dp, seq


def flip(value, bit):
    return value + bit * (1 - 2 * ((value // bit) % 2))


def flips(value, mask):
    bit = 1
    while bit <= mask:
        if mask & bit:
            value = flip(value, bit)
        bit *= 2
    return value


def greet(devices):
    barrier = pltpu.get_barrier_semaphore()
    for device in devices:
        pl.semaphore_signal(barrier, inc=1, device_id=device, device_id_type=MESH)
    pl.semaphore_wait(barrier, len(devices))


def greet_all(plan, dp, seq):
    barrier = pltpu.get_barrier_semaphore()
    me = dp * plan.seq + seq

    def hello(step, carry):
        other = (me + step) % plan.devices
        pl.semaphore_signal(
            barrier, inc=1, device_id=(other // plan.seq, other % plan.seq), device_id_type=MESH
        )
        return carry

    lax.fori_loop(1, plan.devices, hello, 0)
    pl.semaphore_wait(barrier, plan.devices - 1)


def greet_group(plan, dp, index):
    barrier = pltpu.get_barrier_semaphore()

    def hello(step, carry):
        other = plan.member(dp, (index + step) % plan.size)
        pl.semaphore_signal(barrier, inc=1, device_id=other, device_id_type=MESH)
        return carry

    lax.fori_loop(1, plan.size, hello, 0)
    pl.semaphore_wait(barrier, plan.size - 1)


def send(src, dst, send_sem, recv_sem, device):
    copy = pltpu.make_async_remote_copy(
        src_ref=src,
        dst_ref=dst,
        send_sem=send_sem,
        recv_sem=recv_sem,
        device_id=device,
        device_id_type=MESH,
    )
    copy.start()
    return copy


def wait_bytes(ref, sem):
    pltpu.make_async_copy(ref, ref, sem).wait()


class Loads:
    def __init__(self, sources, buffers, sems):
        self.copies = [
            pltpu.make_async_copy(src, dst, sems.at[i])
            for i, (src, dst) in enumerate(zip(sources, buffers))
        ]
        for copy in self.copies:
            copy.start()

    def wait(self, *which):
        for i in which or range(len(self.copies)):
            self.copies[i].wait()


def like(value):
    return pltpu.VMEM(value.shape, value.dtype)


def halves(rows):
    return ((0, rows // 2), (rows // 2, rows - rows // 2))


ORDERS = ((2, 4), (4, 2))


def gather_steps(plan, x, out, dp, seq, index, sems):
    far_send, far_recv, near_send, near_recv, core_send, core_recv, local = sems
    rows = x.shape[0]
    parts = halves(rows)
    copies = []

    def place(mask, part=None):
        start, count = (0, rows) if part is None else parts[part]
        return out.at[pl.ds(pl.multiple_of(flips(index, mask) * rows + start, 16), count)]

    def push(src, dst, send_sem, recv_sem, bit):
        copies.append(send(src, dst, send_sem, recv_sem, plan.across(dp, seq, bit)))

    def near(mask, part, number, bit):
        push(place(mask, part), place(mask, part), near_send.at[number], near_recv.at[number], bit)

    def to_core(mask, part, number):
        push(place(mask, part), place(mask, part), core_send.at[number], core_recv.at[number], 1)

    def begin():
        pltpu.make_async_copy(x, out.at[pl.ds(index * rows, rows)], local).start()
        for part in range(2):
            start, count = parts[part]
            push(
                x.at[pl.ds(start, count)], place(0, part), far_send.at[part], far_recv.at[part], 8
            )
        for bit in (2, 4):
            push(x, place(0), near_send.at[bit // 4], near_recv.at[bit // 4], bit)
        push(x, place(0), core_send.at[0], core_recv.at[0], 1)

    def finish(use=None):
        def here(chip):
            if use is not None:
                use(chip)

        pltpu.make_async_copy(x, out.at[pl.ds(index * rows, rows)], local).wait()
        wait_bytes(place(1), core_recv.at[0])
        here(0)
        for bit, other in ORDERS:
            part = bit // 4
            wait_bytes(place(bit), near_recv.at[part])
            near(bit, part, 2 + part, other)
            to_core(bit, None, 1 + part)
        def from_far(part):
            wait_bytes(place(8, part), far_recv.at[part])
            for bit in (2, 4):
                near(8, part, 4 + 2 * part + bit // 4, bit)
            to_core(8, part, 5 + part)

        wait_bytes(place(3), core_recv.at[1])
        here(2)
        from_far(0)
        wait_bytes(place(5), core_recv.at[2])
        here(4)
        for part in range(2):
            wait_bytes(place(6, part), near_recv.at[2 + part])
            to_core(6, part, 3 + part)
        from_far(1)
        for part in range(2):
            wait_bytes(place(7, part), core_recv.at[3 + part])
        here(6)
        for part in range(2):
            wait_bytes(place(9, part), core_recv.at[5 + part])
        here(8)
        for part in range(2):
            for bit, other in ORDERS:
                wait_bytes(place(8 | bit, part), near_recv.at[4 + 2 * part + bit // 4])
                if part == bit // 4:
                    near(8 | bit, part, 8 + part, other)
                to_core(8 | bit, part, 7 + 2 * part + bit // 4)
        for bit in (2, 4):
            for part in range(2):
                wait_bytes(place(9 | bit, part), core_recv.at[7 + 2 * part + bit // 4])
            if bit == 2:
                here(10)
        for part in range(2):
            wait_bytes(place(14, part), near_recv.at[8 + part])
            to_core(14, part, 11 + part)
        here(12)
        for part in range(2):
            wait_bytes(place(15, part), core_recv.at[11 + part])
        here(14)
        for copy in copies:
            copy.wait_send()

    return begin, finish


GATHER_SEMS = (DMA((2,)), DMA((2,)), DMA((10,)), DMA((10,)), DMA((13,)), DMA((13,)), DMA)


def scatter_steps(plan, dp, seq, index, pairs, turned, write, bufs, sems, meanwhile=None):
    theirs, mine, got_core, got_first, got_second, got_far = bufs
    core_send, core_recv, send_sems, recv_sems, far_send, far_recv = sems
    rows, width = got_far.shape
    tile = 512
    piece = rows // (2 * CHUNKS)
    copies = []

    def compute(dst, plane, core, blocks):
        starts = [flips(index, core | 2 * m | 8 * plane) * rows for m in blocks]

        @pl.loop(0, width // tile)
        def _(j):
            columns = pl.ds(pl.multiple_of(j * tile, tile), tile)
            block = None
            for l_ref, offset, r_ref in pairs:
                depth = r_ref.shape[1] if turned else r_ref.shape[0]
                some = jnp.concatenate(
                    [
                        l_ref[pl.ds(pl.multiple_of(start, rows), rows), pl.ds(offset, depth)]
                        for start in starts
                    ],
                    axis=0,
                )
                if turned:
                    part = contract_last(some, r_ref[columns, :])
                else:
                    part = dot(some, r_ref[:, columns])
                block = part if block is None else block + part
            block = block.astype(BF)
            for i, m in enumerate(blocks):
                dst[plane, m, :, columns] = block[i * rows : (i + 1) * rows]

    def push(src, dst, send_sem, recv_sem, bit):
        copy = send(src, dst, send_sem, recv_sem, plan.across(dp, seq, bit))
        copies.append(copy)
        return copy

    def add(dst, src, count):
        @pl.loop(0, count // 16)
        def _(i):
            here = pl.ds(pl.multiple_of(i * 16, 16), 16)
            dst[here, :] = dst[here, :] + src[here, :]

    def to_core(plane, blocks):
        started = []
        for m in blocks:
            number = plane * 4 + m
            started.append(
                (
                    push(
                        theirs.at[plane, m],
                        got_core.at[plane, m],
                        core_send.at[number],
                        core_recv.at[number],
                        1,
                    ),
                    m,
                )
            )
        return started

    def add_core(plane, started):
        for copy, m in started:
            copy.wait_recv()
            add(mine.at[plane, m], got_core.at[plane, m], rows)

    def start_of(chunk, part):
        return (chunk * 2 + part) * piece

    def first(plane, chunk):
        started = []
        for part, (bit, other) in enumerate(ORDERS):
            here = pl.ds(start_of(chunk, part), piece)
            for k, keep in enumerate((other, 0)):
                number = (plane * CHUNKS + chunk) * 6 + part * 2 + k
                buffer = got_first.at[plane, chunk, part * 2 + k]
                copy = push(
                    mine.at[plane, (keep | bit) // 2, here],
                    buffer,
                    send_sems.at[number],
                    recv_sems.at[number],
                    bit,
                )
                started.append((copy, keep // 2, here, buffer))
        return started

    def second(plane, chunk):
        started = []
        for part, (bit, other) in enumerate(ORDERS):
            here = pl.ds(start_of(chunk, part), piece)
            number = (plane * CHUNKS + chunk) * 6 + 4 + part
            buffer = got_second.at[plane, chunk, part]
            copy = push(
                mine.at[plane, other // 2, here],
                buffer,
                send_sems.at[number],
                recv_sems.at[number],
                other,
            )
            started.append((copy, 0, here, buffer))
        return started

    def far(chunk):
        here = pl.ds(chunk * 2 * piece, 2 * piece)
        return push(
            mine.at[1, 0, here], got_far.at[here], far_send.at[chunk], far_recv.at[chunk], 8
        )

    def settle(plane, started):
        for copy, m, here, buffer in started:
            copy.wait_recv()
            add(mine.at[plane, m, here], buffer, piece)

    def hook(i):
        if meanwhile is not None:
            meanwhile(i)

    compute(theirs, 1, 1, (3, 1))
    core_a = to_core(1, (3, 1))
    compute(theirs, 1, 1, (2, 0))
    core_b = to_core(1, (2, 0))
    compute(mine, 1, 0, (3, 1, 2, 0))
    hook(0)
    add_core(1, core_a)
    add_core(1, core_b)
    one = [first(1, chunk) if chunk < 2 else None for chunk in range(CHUNKS)]
    compute(theirs, 0, 1, (3, 1, 2, 0))
    core = to_core(0, (3, 1, 2, 0))
    fars = []

    def advance(chunk):
        settle(1, one[chunk])
        one[chunk] = second(1, chunk)
        if chunk + 2 < CHUNKS:
            one[chunk + 2] = first(1, chunk + 2)

    def cross(chunk):
        settle(1, one[chunk])
        fars.append(far(chunk))

    advance(0)
    compute(mine, 0, 0, (3, 1, 2, 0))
    hook(1)
    advance(1)
    add_core(0, core)
    for chunk in range(2, CHUNKS):
        cross(chunk - 2)
        advance(chunk)
    zero = [first(0, chunk) for chunk in range(CHUNKS)]
    hook(2)
    for chunk in range(CHUNKS - 2, CHUNKS):
        cross(chunk)
    hook(3)
    for chunk in range(CHUNKS):
        settle(0, zero[chunk])
        zero[chunk] = second(0, chunk)
    hook(4)
    for chunk in range(CHUNKS):
        settle(0, zero[chunk])
        fars[chunk].wait_recv()

        @pl.loop(0, 2 * piece // 16)
        def _(i):
            here = pl.ds(pl.multiple_of(chunk * 2 * piece + i * 16, 16), 16)
            write(here, mine[0, 0, here, :].astype(F32) + got_far[here, :].astype(F32))

    for copy in copies:
        copy.wait_send()


CHUNKS = 4


def scatter_scratch(rows, width):
    block = (rows, width)
    piece = (rows // (2 * CHUNKS), width)
    return [
        pltpu.VMEM((2, 4) + block, BF),
        pltpu.VMEM((2, 4) + block, BF),
        pltpu.VMEM((2, 4) + block, BF),
        pltpu.VMEM((2, CHUNKS, 4) + piece, BF),
        pltpu.VMEM((2, CHUNKS, 2) + piece, BF),
        pltpu.VMEM(block, BF),
        DMA((8,)),
        DMA((8,)),
        DMA((12 * CHUNKS,)),
        DMA((12 * CHUNKS,)),
        DMA((CHUNKS,)),
        DMA((CHUNKS,)),
    ]


def scatter_call(
    plan,
    left,
    rights,
    turned,
    collective_id,
    name,
    gains,
    which,
    extras,
    outs,
    begin,
    write,
    gather=False,
    moves=None,
):
    rows = left.shape[0] // plan.size
    width = rights[0].shape[0] if turned else rights[0].shape[1]
    count = len(rights)
    depth = left.shape[1] // count
    moves = moves or [(0, 0, rights[0].shape[0])]

    def kernel(*refs):
        refs = list(refs)

        def take(number):
            taken = refs[:number]
            del refs[:number]
            return taken

        sources, (gains_ref,), more = take(1 + count), take(1), take(len(extras))
        results = take(len(outs))
        everyone = take(1) if gather else None
        held, (sem, gain_row) = take(1 + count), take(2)
        pieces = [(sources[0], held[0])] + [
            (src.at[pl.ds(first, rows)], dst.at[pl.ds(to, rows)])
            for src, dst in zip(sources[1:], held[1:])
            for first, to, rows in moves
        ]
        loads = Loads(*zip(*pieces), sem)
        own = width // plan.devices
        for device in range(plan.devices):
            gain_row[:, device * own : (device + 1) * own] = gains_ref[
                device, which : which + 1, :own
            ]
        more = [*more, gain_row]
        pairs = [(held[0], i * depth, held[1 + i]) for i in range(count)]
        dp, seq, index = plan.here()
        greet([plan.across(dp, seq, bit) for bit in (1, 2, 4, 8)])
        begin(results)
        loads.wait()

        def put(here, value):
            write(here, value, more, results)

        scatter_steps(plan, dp, seq, index, pairs, turned, put, refs[:6], refs[6:12])
        if gather:
            start, finish = gather_steps(
                plan, results[-1], everyone[0], dp, seq, index, refs[12:]
            )
            start()
            finish()

    shapes = [jax.ShapeDtypeStruct(*out) for out in outs]
    if gather:
        shapes.append(jax.ShapeDtypeStruct((plan.size * rows, width), outs[-1][1]))
    return pl.pallas_call(
        kernel,
        out_shape=shapes,
        in_specs=[ANY] * (1 + count) + [VM] * (1 + len(extras)),
        out_specs=[VM] * len(outs) + [ANY] * gather,
        scratch_shapes=[like(value) for value in (left, *rights)]
        + [DMA((1 + count * len(moves),)), pltpu.VMEM((1, width), F32)]
        + scatter_scratch(rows, width)
        + list(GATHER_SEMS) * gather,
        compiler_params=pltpu.CompilerParams(
            collective_id=collective_id, has_side_effects=True, vmem_limit_bytes=60 * 2**20
        ),
        cost_estimate=LIGHT,
        name=name,
    )(left, *rights, gains, *extras)


def rms(values):
    return lax.rsqrt(jnp.mean(values * values, axis=1, keepdims=True) + epsilon)


def rms_back(values, gain, grad):
    r = rms(values)
    scaled = grad * gain
    inner = jnp.mean(scaled * values, axis=1, keepdims=True)
    back = r * scaled - values * (r * r * r * inner)
    return back, jnp.sum(grad * values * r, axis=0, keepdims=True)


def hidden_forward(plan, mixed, w_out, x, gains):
    def write(here, value, extras, outs):
        x_ref, g = extras
        branch, hidden, low = outs
        branch[here, :] = value
        h = x_ref[here, :].astype(F32) + value * rms(value) * g[...]
        hidden[here, :] = h
        low[here, :] = h.astype(BF)

    outs = ((x.shape, F32), (x.shape, F32), (x.shape, BF))
    return scatter_call(
        plan,
        mixed,
        [w_out],
        False,
        2,
        "hidden_forward",
        gains,
        2,
        (x,),
        outs,
        lambda outs: None,
        write,
        gather=True,
    )


def output_norm(plan, act, w_down, hidden, grad_out, gains):
    def begin(outs):
        outs[2][...] = jnp.zeros_like(outs[2])

    def write(here, value, extras, outs):
        hidden_ref, dy, g = extras
        output, back, g_gain = outs
        output[here, :] = (hidden_ref[here, :] + value * rms(value) * g[...]).astype(BF)
        grad, part = rms_back(value, g[...], dy[here, :].astype(F32))
        back[here, :] = grad.astype(BF)
        g_gain[...] += part

    outs = ((hidden.shape, BF), (hidden.shape, BF), ((1, hidden.shape[1]), F32))
    return scatter_call(
        plan,
        act,
        [w_down],
        False,
        6,
        "output_norm",
        gains,
        3,
        (hidden, grad_out),
        outs,
        begin,
        write,
    )


def hidden_backward(plan, g_low, rights, grad_out, branch, gains):
    def begin(outs):
        outs[1][...] = jnp.zeros_like(outs[1])

    def write(here, value, extras, outs):
        dy, u, g = extras
        grad, g_gain, low = outs
        e = dy[here, :].astype(F32) + value
        grad[here, :] = e
        back, part = rms_back(u[here, :], g[...], e)
        low[here, :] = back.astype(BF)
        g_gain[...] += part

    outs = ((branch.shape, F32), ((1, branch.shape[1]), F32), (branch.shape, BF))
    return scatter_call(
        plan,
        g_low,
        rights,
        True,
        7,
        "hidden_backward",
        gains,
        2,
        (grad_out, branch),
        outs,
        begin,
        write,
        moves=plan.natural(rights[0].shape[0]),
    )


def half_columns(plan, inner, blocks, half):
    each = inner // blocks // plan.size

    def offset(block):
        if blocks > 1:
            return lambda member: half * inner + plan.flat(block, member) * each
        return lambda member: half * inner + member * each

    return [(offset(block), each, block * each) for block in range(blocks)]


def columns_out(plan, dp, index, w_ref, out_ref, table, send_sem, recv_sem):
    own = w_ref.shape[0]
    wide = out_ref.shape[1]
    rows = pl.ds(pl.multiple_of(index * own, own), own)

    def moves(other):
        for offset, each, place in table:
            yield (
                w_ref.at[:, pl.ds(pl.multiple_of(offset(other), 128), each)],
                out_ref.at[rows, pl.ds(place, each)],
            )

    def begin():
        def to(step, carry):
            other = (index + step) % plan.size
            for src, dst in moves(other):
                send(src, dst, send_sem, recv_sem, plan.member(dp, other))
            return carry

        lax.fori_loop(1, plan.size, to, 0)
        for src, dst in moves(index):
            pltpu.make_async_copy(src, dst, recv_sem).start()

    def finish():
        wait_bytes(out_ref, recv_sem)

        def sent(step, carry):
            wait_bytes(w_ref.at[:, pl.ds(0, wide)], send_sem)
            return carry

        lax.fori_loop(1, plan.size, sent, 0)

    return begin, finish


def columns_back(plan, dp, index, g_ref, out_ref, table, send_sem, recv_sem):
    own = g_ref.shape[0] // plan.size

    def moves(other):
        rows = pl.ds(pl.multiple_of(other * own, own), own)
        for offset, each, place in table:
            yield (
                g_ref.at[rows, pl.ds(place, each)],
                out_ref.at[:, pl.ds(pl.multiple_of(offset(index), 128), each)],
            )

    def begin(plane):
        first = flips(index, 8 * plane) // 8 * 8

        def to(step, carry):
            other = first + (index + step) % 8
            for src, dst in moves(other):
                send(src, dst, send_sem, recv_sem, plan.member(dp, other))
            return carry

        lax.fori_loop(1 - plane, 8, to, 0)
        if plane == 0:
            for src, dst in moves(index):
                pltpu.make_async_copy(src, dst, recv_sem).start()

    def finish():
        wait_bytes(g_ref, recv_sem)

        def sent(step, carry):
            wait_bytes(g_ref.at[pl.ds(0, own)], send_sem)
            return carry

        lax.fori_loop(1, plan.size, sent, 0)

    return begin, finish


def start_gather(plan, x, attn_w, gate_up_w, gains, segments, blocks):
    rows, width = x.shape
    own, both = gate_up_w.shape
    table = half_columns(plan, both // 2, blocks, 0)

    count = len(gains)

    def kernel(x_ref, w_ref, u_ref, s_ref, *refs):
        gain_refs, (xo, wo, uo, oo, go, do) = refs[:count], refs[count : count + 6]
        g_ref, d_ref = refs[count + 6 : count + 8]
        sems = refs[count + 8 :]
        gather_sems = sems[:7]
        w_send, w_recv, u_send, u_recv, o_send, o_recv, g_send, g_recv, d_send, d_recv = sems[7:17]
        far_send, far_recv = sems[17:]
        g_ref[...] = jnp.zeros_like(g_ref)
        for i, gain in enumerate(gain_refs):
            g_ref[i : i + 1, :own] = gain[...].astype(F32)
        d_ref[...] = jnp.broadcast_to(s_ref[...], d_ref.shape)
        dp, seq, index = plan.here()
        me = dp * plan.seq + seq
        greet_all(plan, dp, seq)
        begin, finish = gather_steps(plan, x_ref, xo, dp, seq, index, gather_sems)
        group = plan.group_of(dp)

        def columns(part, other):
            return pl.ds(pl.multiple_of(part * width + plan.head(other) * HEAD, HEAD), HEAD)

        def rows_of(member):
            return pl.ds(pl.multiple_of(plan.flat(group, member) * own, own), own)

        def w_to(step, carry):
            other = (index + step) % plan.size
            for part in range(3):
                send(
                    w_ref.at[:, columns(part, other)],
                    wo.at[rows_of(index), pl.ds(part * HEAD, HEAD)],
                    w_send,
                    w_recv.at[index],
                    plan.member(dp, other),
                )
            return carry

        lax.fori_loop(1, plan.size, w_to, 0)
        begin()
        for part in range(3):
            pltpu.make_async_copy(
                w_ref.at[:, columns(part, index)],
                wo.at[rows_of(index), pl.ds(part * HEAD, HEAD)],
                w_recv.at[index],
            ).start()

        def onward(step, carry):
            rows = wo.at[rows_of((index + plan.size - step) % plan.size)]
            wait_bytes(rows, w_recv.at[(index + plan.size - step) % plan.size])
            for away in range(1, plan.groups):
                to_group = (group + away) % plan.groups
                send(rows, rows, far_send, far_recv, plan.in_group(to_group, index))
            return carry

        lax.fori_loop(0, plan.size, onward, 0)
        feature = me * own
        keeper = plan.of_head(feature // HEAD)
        o_dst = oo.at[pl.ds(pl.multiple_of(feature % HEAD, own), own)]
        o_src = w_ref.at[:, pl.ds(3 * width, width)]

        def o_to(away, carry):
            to_group = (group + away) % plan.groups
            to_dp, to_seq = plan.in_group(to_group, keeper)
            same = to_dp * plan.seq + to_seq == me

            @pl.when(same)
            def _():
                pltpu.make_async_copy(o_src, o_dst, o_recv).start()

            @pl.when(jnp.logical_not(same))
            def _():
                send(o_src, o_dst, o_send, o_recv, (to_dp, to_seq))

            return carry

        lax.fori_loop(0, plan.groups, o_to, 0)
        begin_u, finish_u = columns_out(plan, dp, index, u_ref, uo, table, u_send, u_recv)
        begin_u()

        def g_to(step, carry):
            other = (me + step) % plan.devices
            send(g_ref, go.at[me], g_send, g_recv, (other // plan.seq, other % plan.seq))
            return carry

        lax.fori_loop(1, plan.devices, g_to, 0)
        pltpu.make_async_copy(g_ref, go.at[me], g_recv).start()

        def d_to(step, carry):
            send(d_ref, do.at[index], d_send, d_recv, plan.member(dp, (index + step) % plan.size))
            return carry

        lax.fori_loop(1, plan.size, d_to, 0)
        pltpu.make_async_copy(d_ref, do.at[index], d_recv).start()
        finish()
        finish_u()
        wait_bytes(go, g_recv)
        wait_bytes(do, d_recv)
        far = wo.at[pl.ds(0, (plan.groups - 1) * plan.size * own)]
        wait_bytes(far, far_recv)
        wait_bytes(far, far_send)

        def sent(step, carry):
            wait_bytes(g_ref, g_send)
            return carry

        lax.fori_loop(1, plan.devices, sent, 0)

        def sent_w(step, carry):
            wait_bytes(w_ref.at[:, pl.ds(0, 3 * HEAD)], w_send)
            return carry

        lax.fori_loop(1, plan.size, sent_w, 0)

        def sent_docs(step, carry):
            wait_bytes(d_ref, d_send)
            return carry

        lax.fori_loop(1, plan.size, sent_docs, 0)
        wait_bytes(oo, o_recv)

        def sent_o(away, carry):
            to_group = (group + away) % plan.groups
            to_dp, to_seq = plan.in_group(to_group, keeper)

            @pl.when(to_dp * plan.seq + to_seq != me)
            def _():
                wait_bytes(o_src, o_send)

            return carry

        lax.fori_loop(0, plan.groups, sent_o, 0)

    shapes = (
        ((plan.size * rows, width), BF),
        ((plan.devices * own, 3 * HEAD), BF),
        ((plan.size * own, both // 2 // plan.size), BF),
        ((HEAD, width), BF),
        ((plan.devices, 8, 128), F32),
        ((plan.size, 8, rows), jnp.int32),
    )
    return pl.pallas_call(
        kernel,
        out_shape=[jax.ShapeDtypeStruct(*shape) for shape in shapes],
        in_specs=[ANY] * 3 + [VM] * (1 + count),
        out_specs=[ANY] * 6,
        scratch_shapes=[pltpu.VMEM((8, 128), F32), pltpu.VMEM((8, rows), jnp.int32)]
        + list(GATHER_SEMS)
        + [DMA, DMA((plan.size,))]
        + [DMA] * 10,
        compiler_params=pltpu.CompilerParams(collective_id=0, has_side_effects=True),
        cost_estimate=LIGHT,
        name="start_gather",
    )(x, attn_w, gate_up_w, segments, *[gain.reshape(1, own) for gain in gains])


def dot(left, right):
    return jnp.dot(left, right, preferred_element_type=F32)


def contract_last(left, right):
    return lax.dot_general(left, right, (((1,), (1,)), ((), ())), preferred_element_type=F32)


def contract_first(left, right):
    return lax.dot_general(left, right, (((0,), (0,)), ((), ())), preferred_element_type=F32)


def chip_rows(index, chip, rows):
    return pl.multiple_of(flips(index, chip) // 2 * (2 * rows), 2 * rows)


def ffn_forward(plan, h_all, w_gate, w_up):
    tokens, width = h_all.shape
    units = w_gate.shape[1]
    moves = plan.natural(width)

    def kernel(h, wg_ref, wu_ref, gate, up, act, wg, wu, sem):
        @pl.when(pl.program_id(0) == 0)
        def _():
            pieces = [
                (src.at[pl.ds(first, rows)], dst.at[pl.ds(to, rows)])
                for src, dst in ((wg_ref, wg), (wu_ref, wu))
                for first, to, rows in moves
            ]
            Loads(*zip(*pieces), sem).wait()

        values = h[...]
        g = dot(values, wg[...])
        u = dot(values, wu[...])
        gate[...] = g.astype(BF)
        up[...] = u.astype(BF)
        act[...] = (g * jax.nn.sigmoid(g) * u).astype(BF)

    rows = 2 * STEP
    part = pl.BlockSpec((rows, units), lambda i: (i, 0))
    return pl.pallas_call(
        kernel,
        grid=(tokens // rows,),
        out_shape=[jax.ShapeDtypeStruct((tokens, units), BF)] * 3,
        in_specs=[pl.BlockSpec((rows, width), lambda i: (i, 0)), ANY, ANY],
        out_specs=[part] * 3,
        scratch_shapes=[like(w_gate), like(w_up), DMA((2 * len(moves),))],
        compiler_params=pltpu.CompilerParams(vmem_limit_bytes=60 * 2**20),
        cost_estimate=LIGHT,
        name="ffn_forward",
    )(h_all, w_gate, w_up)


def ffn_backward(plan, d, h_all, w_down, gate, up, act):
    rows, width = d.shape
    tokens = rows * plan.size
    units = gate.shape[1]
    at_dp = width // plan.dp
    tile = 256
    two = 2 * rows

    def kernel(d_ref, *refs):
        ins, refs = refs[:5], refs[5:]
        outs, (h_all, wd, gate, up, act) = refs[:4], refs[4:9]
        d_all, gu_turned, act_turned, gu_sum, down_sum, out, g_gate, g_up, g_down = refs[9:18]
        sems, load_sems, store_sems, out_sems = refs[18:25], refs[25], refs[26], refs[27]
        dp, seq, index = plan.here()
        loads = Loads(ins, (wd, gate, up, act, h_all), load_sems)
        greet([plan.across(dp, seq, bit) for bit in (1, 2, 4, 8)])
        begin, finish = gather_steps(plan, d_ref, d_all, dp, seq, index, sems)
        begin()
        stores = []
        pair = []

        def products(first, last):
            chips = [pl.ds(chip_rows(index, chip, rows), two) for chip in pair]

            @pl.loop(0, width // tile)
            def _(i):
                columns = pl.ds(pl.multiple_of(i * tile, tile), tile)
                block = dot(
                    gu_turned[...],
                    jnp.concatenate([h_all[chip, columns] for chip in chips], axis=0),
                )
                if not first:
                    block = gu_sum[:, columns] + block
                if last:
                    block = block.T.astype(BF)
                    row = i * tile
                    row = plan.place(row // at_dp) * at_dp + row % at_dp
                    to = pl.ds(pl.multiple_of(row, tile), tile)
                    g_gate[to, :] = block[:, :units]
                    g_up[to, :] = block[:, units:]
                else:
                    gu_sum[:, columns] = block

            @pl.loop(0, width // tile)
            def _(i):
                columns = pl.ds(pl.multiple_of(i * tile, tile), tile)
                block = dot(
                    act_turned[...],
                    jnp.concatenate([d_all[chip, columns] for chip in chips], axis=0),
                )
                if not first:
                    block = down_sum[:, columns] + block
                if last:
                    g_down[:, columns] = block.astype(BF)
                else:
                    down_sum[:, columns] = block

        def use(chip):
            if chip == 0:
                loads.wait()
            some = pl.ds(chip_rows(index, chip, rows), two)
            columns = pl.ds(len(pair) * two, two)
            grad = contract_last(d_all[some, :], wd[...])
            g = gate[some, :].astype(F32)
            u = up[some, :].astype(F32)
            sigma = jax.nn.sigmoid(g)
            grad_gate = (grad * u * sigma * (1.0 + g * (1.0 - sigma))).astype(BF)
            grad_up = (grad * (g * sigma)).astype(BF)
            out[some, pl.ds(0, units)] = grad_gate
            out[some, pl.ds(units, units)] = grad_up
            store = pltpu.make_async_copy(out.at[some], outs[0].at[some], store_sems.at[chip // 2])
            store.start()
            stores.append(store)
            gu_turned[pl.ds(0, units), columns] = grad_gate.T
            gu_turned[pl.ds(units, units), columns] = grad_up.T
            act_turned[:, columns] = act[some, :].T
            pair.append(chip)
            if len(pair) == 2:
                products(len(stores) == 2, len(stores) == 8)
                pair.clear()

        finish(use)
        for i, src in enumerate((g_gate, g_up, g_down)):
            store = pltpu.make_async_copy(src, outs[1 + i], out_sems.at[i])
            store.start()
            stores.append(store)
        for store in stores:
            store.wait()

    return pl.pallas_call(
        kernel,
        out_shape=[
            jax.ShapeDtypeStruct((tokens, 2 * units), BF),
            jax.ShapeDtypeStruct((width, units), BF),
            jax.ShapeDtypeStruct((width, units), BF),
            jax.ShapeDtypeStruct((units, width), BF),
        ],
        in_specs=[VM] + [ANY] * 5,
        out_specs=[ANY] * 4,
        scratch_shapes=[
            pltpu.VMEM(shape, BF)
            for shape in (h_all.shape, (units, width), gate.shape, up.shape, act.shape, h_all.shape)
        ]
        + [
            pltpu.VMEM((2 * units, 2 * two), BF),
            pltpu.VMEM((units, 2 * two), BF),
            pltpu.VMEM((2 * units, width), F32),
            pltpu.VMEM((units, width), F32),
            pltpu.VMEM((tokens, 2 * units), BF),
            pltpu.VMEM((width, units), BF),
            pltpu.VMEM((width, units), BF),
            pltpu.VMEM((units, width), BF),
        ]
        + list(GATHER_SEMS)
        + [DMA((5,)), DMA((8,)), DMA((3,))],
        compiler_params=pltpu.CompilerParams(
            collective_id=10, has_side_effects=True, vmem_limit_bytes=62 * 2**20
        ),
        cost_estimate=LIGHT,
        name="ffn_backward",
    )(d, w_down, gate, up, act, h_all)


def row_sums(values):
    ones = jnp.ones((8, values.shape[1]), F32)
    sums = lax.dot_general(
        ones,
        values,
        (((1,), (1,)), ((), ())),
        precision=lax.Precision.HIGHEST,
        preferred_element_type=F32,
    )
    return sums[:1]


def spread_sums(rows):
    ones = jnp.ones((rows.shape[0], HEAD), F32)
    return lax.dot_general(
        rows,
        ones,
        (((0,), (0,)), ((), ())),
        precision=lax.Precision.HIGHEST,
        preferred_element_type=F32,
    )


STEP = 256


def lay_out(docs_ref, row_ref):
    for i in range(docs_ref.shape[0]):
        rows = docs_ref.shape[2]
        row_ref[:, i * rows : (i + 1) * rows] = docs_ref[i, :1, :].astype(F32)


def my_gain(plan, gains_ref, which, head):
    own = HEAD // plan.pieces
    parts = [gains_ref[head * plan.pieces + i, which : which + 1, :own] for i in range(plan.pieces)]
    return jnp.concatenate(parts, axis=1)


def scores_of(q, k, q_docs, k_docs, start):
    scores = contract_last(q, k) * HEAD ** (-0.5)
    row = start + lax.broadcasted_iota(jnp.int32, scores.shape, 0)
    column = lax.broadcasted_iota(jnp.int32, scores.shape, 1)
    allowed = (column <= row) & (spread_sums(q_docs)[:, :1] == k_docs)
    scores = jnp.where(allowed, scores, -1e30)
    top = jnp.max(scores, axis=1, keepdims=True)
    weights = jnp.exp(scores - top)
    return weights / jnp.sum(weights, axis=1, keepdims=True)


def swap_sums(plan, dp, index, mine, held, s_sem, r_sem):
    def begin():
        def to(step, carry):
            send(mine, held.at[index], s_sem, r_sem, plan.member(dp, (index + step) % plan.size))
            return carry

        pltpu.make_async_copy(mine, held.at[index], r_sem).start()
        lax.fori_loop(1, plan.size, to, 0)

    def finish():
        wait_bytes(held, r_sem)
        wait_bytes(held.at[pl.ds(0, plan.size - 1)], s_sem)

    return begin, finish


def attend_forward(
    plan, x_all, w_qkv, gate_up_w, gains, docs, cosine, sine, blocks
):
    tokens, width = x_all.shape
    length = cosine.shape[0]
    own, both = gate_up_w.shape
    table = half_columns(plan, both // 2, blocks, 1)

    def kernel(x_ref, wq_ref, up, ga, do, cs_ref, sn_ref, uo, q, k, sums, ql, kl, vl, mixed, *rest):
        x, wq, cs, sn, sem = rest[:5]
        loads = Loads((wq_ref, cs_ref, sn_ref), (wq, cs, sn), sem)
        step_rows = [pl.ds(i * STEP, STEP) for i in range(tokens // STEP)]
        Loads(
            [x_ref.at[rows] for rows in step_rows], [x.at[rows] for rows in step_rows], rest[5]
        )
        tile_sem, rest = rest[5], rest[6:]
        gn, dr, stats, held, t_send, t_recv, u_send, u_recv = rest
        dp, seq, index = plan.here()
        greet_group(plan, dp, index)
        lay_out(do, dr)
        for which in range(2):
            gn[which : which + 1, :] = my_gain(plan, ga, which, plan.head(index))
        loads.wait()

        @pl.loop(0, tokens // STEP)
        def _(i):
            rows = pl.ds(pl.multiple_of(i * STEP, STEP), STEP)
            pltpu.make_async_copy(x_ref.at[rows], x.at[rows], tile_sem.at[i]).wait()
            block = dot(x[rows, :], wq[...])
            q[rows, :] = block[:, :HEAD]
            k[rows, :] = block[:, HEAD : 2 * HEAD]
            vl[rows, :] = block[:, 2 * HEAD :].astype(BF)
            stats[0, :, rows] = row_sums(block[:, :HEAD] * block[:, :HEAD])
            stats[1, :, rows] = row_sums(block[:, HEAD : 2 * HEAD] * block[:, HEAD : 2 * HEAD])

        begin, finish = swap_sums(plan, dp, index, stats, held, t_send, t_recv)
        begin()
        begin_u, finish_u = columns_out(plan, dp, index, up, uo, table, u_send, u_recv)
        begin_u()
        finish()
        for which in range(2):
            sums[which] = jnp.sum(held[:, which, 0, :], axis=0, keepdims=True)

        @pl.loop(0, tokens // STEP)
        def _(i):
            rows = pl.ds(pl.multiple_of(i * STEP, STEP), STEP)
            places = pl.ds(pl.multiple_of((i % (length // STEP)) * STEP, STEP), STEP)
            for which, raw, low in ((0, q, ql), (1, k, kl)):
                r = lax.rsqrt(spread_sums(sums[which, :, rows]) / width + epsilon)
                values = raw[rows, :] * r * gn[which : which + 1, :]
                turned = values * cs[places, :] + pltpu.roll(values, HEAD // 2, 1) * sn[places, :]
                low[rows, :] = turned.astype(BF)

        @pl.loop(0, tokens // length)
        def _(b):
            for j in range(length // STEP):
                start = pl.multiple_of(b * length + j * STEP, STEP)
                rows = pl.ds(start, STEP)
                keys = pl.ds(pl.multiple_of(b * length, length), (j + 1) * STEP)
                probs = scores_of(
                    ql[rows, :], kl[keys, :], dr[:, rows], dr[:, keys], j * STEP
                )
                mixed[rows, :] = dot(probs.astype(BF), vl[keys, :]).astype(BF)

        finish_u()

    per_head = (tokens, HEAD)
    shapes = (
        ((plan.size * own, both // 2 // plan.size), BF),
        (per_head, F32),
        (per_head, F32),
        ((2, 1, tokens), F32),
        (per_head, BF),
        (per_head, BF),
        (per_head, BF),
        (per_head, BF),
    )
    return pl.pallas_call(
        kernel,
        out_shape=[jax.ShapeDtypeStruct(*shape) for shape in shapes],
        in_specs=[ANY] * 3 + [VM] * 2 + [ANY] * 2,
        out_specs=[ANY] + [VM] * 7,
        scratch_shapes=[like(value) for value in (x_all, w_qkv, cosine, sine)]
        + [DMA((3,)), DMA((tokens // STEP,))]
        + [
            pltpu.VMEM((8, HEAD), F32),
            pltpu.VMEM((1, tokens), F32),
            pltpu.VMEM((2, 1, tokens), F32),
            pltpu.VMEM((plan.size, 2, 1, tokens), F32),
        ]
        + [DMA] * 4,
        compiler_params=pltpu.CompilerParams(
            collective_id=3, has_side_effects=True, vmem_limit_bytes=56 * 2**20
        ),
        cost_estimate=LIGHT,
        name="attend_forward",
    )(x_all, w_qkv, gate_up_w, gains, docs, cosine, sine)


def attend_backward(
    plan,
    b,
    w_out,
    q,
    k,
    sums,
    ql,
    kl,
    vl,
    mixed,
    gains,
    docs,
    cosine,
    sine,
    g_gate,
    blocks,
):
    rows_here, width = b.shape
    tokens = rows_here * plan.size
    own = g_gate.shape[0] // plan.size
    inner = g_gate.shape[1] * plan.size
    length = cosine.shape[0]
    scale = HEAD ** (-0.5)

    def kernel(*refs):
        b_ref, sums, ga, do, gg = refs[:5]
        wo, q, k, ql, kl, vl, mx, cs, sn = refs[30:39]
        loads = Loads(refs[5:14], refs[30:39], refs[39])
        dqkv, g_out, g_gain, gate_out = refs[14:18]
        ba, dq, dk, dv, gn, dr, stats, held, t_send, t_recv, gg_send, gg_recv = refs[18:30]
        dp, seq, index = plan.here()
        greet_group(plan, dp, index)
        begin_b, finish_b = gather_steps(plan, b_ref, ba, dp, seq, index, refs[40:])
        begin_b()
        lay_out(do, dr)
        for which in range(2):
            gn[which : which + 1, :] = my_gain(plan, ga, which, plan.head(index))
        begin_g, finish_g = columns_back(
            plan, dp, index, gg, gate_out, half_columns(plan, inner, blocks, 0), gg_send, gg_recv
        )
        dk[...] = jnp.zeros_like(dk)
        dv[...] = jnp.zeros_like(dv)

        def use(chip):
            if chip == 0:
                loads.wait()
            if chip == 8:
                begin_g(1)
            if chip == 10:
                begin_g(0)
            first = chip_rows(index, chip, rows_here)
            rows = pl.ds(first, STEP)
            start = first % length

            def block(count):
                keys = pl.ds(pl.multiple_of(first - start, STEP), count)
                grad = contract_last(ba[rows, :], wo[...]).astype(BF)
                probs = scores_of(ql[rows, :], kl[keys, :], dr[:, rows], dr[:, keys], start)
                grad_probs = contract_last(grad, vl[keys, :])
                delta = jnp.sum(probs * grad_probs, axis=1, keepdims=True)
                grad_scores = (probs * (grad_probs - delta)).astype(BF)
                dq[rows, :] = dot(grad_scores, kl[keys, :]) * scale
                dk[keys, :] += contract_first(grad_scores, ql[rows, :]) * scale
                dv[keys, :] += contract_first(probs.astype(BF), grad)

            @pl.when(start < length // 2)
            def _():
                block(length // 2)

            @pl.when(start >= length // 2)
            def _():
                block(length)

        finish_b(use)

        @pl.loop(0, tokens // STEP)
        def _(i):
            rows = pl.ds(pl.multiple_of(i * STEP, STEP), STEP)
            places = pl.ds(pl.multiple_of((i % (length // STEP)) * STEP, STEP), STEP)
            for which, raw, grad in ((0, q, dq), (1, k, dk)):
                values = grad[rows, :]
                turned = values * cs[places, :] - pltpu.roll(values, HEAD // 2, 1) * sn[places, :]
                grad[rows, :] = turned
                stats[which, :, rows] = row_sums(turned * gn[which : which + 1, :] * raw[rows, :])

        begin, finish = swap_sums(plan, dp, index, stats, held, t_send, t_recv)
        begin()
        turned_mixed = mx[...].T

        @pl.loop(0, width // 512)
        def _(i):
            columns = pl.ds(pl.multiple_of(i * 512, 512), 512)
            g_out[:, columns] = dot(turned_mixed, ba[:, columns]).astype(BF)

        g_gain[...] = jnp.zeros_like(g_gain)
        finish()

        @pl.loop(0, tokens // STEP)
        def _(i):
            rows = pl.ds(pl.multiple_of(i * STEP, STEP), STEP)
            for which, raw, grad in ((0, q, dq), (1, k, dk)):
                total = spread_sums(held[:, which, 0, rows])
                r = lax.rsqrt(spread_sums(sums[which, :, rows]) / width + epsilon)
                u = raw[rows, :]
                e = grad[rows, :]
                back = r * (gn[which : which + 1, :] * e) - u * (r * r * r * (total / width))
                dqkv[rows, pl.ds(which * HEAD, HEAD)] = back.astype(BF)
                g_gain[which : which + 1, :] += jnp.sum(e * u * r, axis=0, keepdims=True)
            dqkv[rows, pl.ds(2 * HEAD, HEAD)] = dv[rows, :].astype(BF)

        finish_g()

    per_head = (tokens, HEAD)
    shapes = (
        ((tokens, 3 * HEAD), BF),
        ((HEAD, width), BF),
        ((8, HEAD), F32),
        ((own, inner), BF),
    )
    return pl.pallas_call(
        kernel,
        out_shape=[jax.ShapeDtypeStruct(*shape) for shape in shapes],
        in_specs=[VM] * 4 + [ANY] * 10,
        out_specs=[VM] * 3 + [ANY],
        scratch_shapes=[
            pltpu.VMEM((tokens, width), BF),
            pltpu.VMEM(per_head, F32),
            pltpu.VMEM(per_head, F32),
            pltpu.VMEM(per_head, F32),
            pltpu.VMEM((8, HEAD), F32),
            pltpu.VMEM((1, tokens), F32),
            pltpu.VMEM((2, 1, tokens), F32),
            pltpu.VMEM((plan.size, 2, 1, tokens), F32),
        ]
        + [DMA] * 4
        + [like(value) for value in (w_out, q, k, ql, kl, vl, mixed, cosine, sine)]
        + [DMA((9,))]
        + list(GATHER_SEMS),
        compiler_params=pltpu.CompilerParams(
            collective_id=4, has_side_effects=True, vmem_limit_bytes=56 * 2**20
        ),
        cost_estimate=LIGHT,
        name="attend_backward",
    )(b, sums, gains, docs, g_gate, w_out, q, k, ql, kl, vl, mixed, cosine, sine)


def finish_backward(
    plan, dqkv, w_qkv, x_all, g_up, g_out, g_head, g_attn, g_ffn, before, blocks
):
    tokens, width = x_all.shape
    own = width // plan.devices
    rows = tokens // plan.size
    inner = g_up.shape[1] * plan.size
    pieces = HEAD // own
    tile = 256
    at_dp = width // plan.dp
    per_dp = at_dp // tile
    tiles = width // plan.groups // tile

    def kernel(dq_ref, wq_ref, x_ref, gu, go, gh, gat, gff, bf, ig, w_grad, up_out, ga_out, *rest):
        (dq, wq, x), load_sem = rest[:3], rest[3]
        loads = Loads((dq_ref, wq_ref, x_ref), (dq, wq, x), load_sem)
        rest = rest[4:]
        bufs, sems = rest[:6], rest[6:12]
        turned, gq, gq_far, got_x, got_q, got_o, ga = rest[12:19]
        q_s, q_r, o_s, o_r, ga_s, ga_r, gu_s, gu_r, x_s, x_r = rest[19:]
        dp, seq, index = plan.here()
        me = dp * plan.seq + seq
        group = plan.group_of(dp)
        greet_all(plan, dp, seq)

        def device_of(flat):
            return flat // plan.seq, flat % plan.seq

        def o_to(piece, carry):
            other = plan.head(index) * pieces + piece
            src = go.at[pl.ds(pl.multiple_of(piece * own, own), own)]

            @pl.when(other == me)
            def _():
                pltpu.make_async_copy(src, got_o.at[group], o_r).start()

            @pl.when(other != me)
            def _():
                send(src, got_o.at[group], o_s, o_r, device_of(other))

            return carry

        def ga_to(step, carry):
            other = (me + step) % plan.devices
            send(ga.at[other], ga_out.at[me], ga_s, ga_r, device_of(other))
            return carry

        table = half_columns(plan, inner, blocks, 0)
        begin_u, finish_u = columns_back(plan, dp, index, gu, up_out, table, gu_s, gu_r)

        def product(of_group, u):
            row = plan.dp_of(of_group, u // per_dp) * at_dp + (u % per_dp) * tile
            block = dot(turned[...], x[:, pl.ds(pl.multiple_of(row, tile), tile)])
            return block.T.astype(BF)

        def others():
            for away in range(1, plan.groups):
                to_group = (group + away) % plan.groups

                @pl.loop(0, tiles)
                def _(u, away=away, to_group=to_group):
                    gq_far[away - 1, u] = product(to_group, u)
                    send(
                        gq_far.at[away - 1, u],
                        got_x.at[away - 1, u],
                        x_s,
                        x_r.at[away - 1, u],
                        plan.in_group(to_group, index),
                    )

        def ours():
            @pl.loop(0, tiles)
            def _(u):
                gq[u] = product(group, u)

        def collect():
            @pl.loop(0, tiles)
            def _(u):
                total = gq[u].astype(F32)
                for away in range(1, plan.groups):
                    wait_bytes(got_x.at[away - 1, u], x_r.at[away - 1, u])
                    total = total + got_x[away - 1, u].astype(F32)
                gq[u] = total.astype(BF)
                owner_dp = plan.dp_of(group, u // per_dp)
                for piece in range(tile // own):
                    owner_seq = (u % per_dp) * (tile // own) + piece
                    src = gq.at[u, pl.ds(piece * own, own)]
                    mine = owner_dp * plan.seq + owner_seq == me

                    @pl.when(mine)
                    def _(src=src):
                        pltpu.make_async_copy(src, got_q.at[index], q_r).start()

                    @pl.when(jnp.logical_not(mine))
                    def _(src=src, owner_seq=owner_seq):
                        send(src, got_q.at[index], q_s, q_r, (owner_dp, owner_seq))

        def meanwhile(i):
            if i == 0:
                loads.wait(2)
                turned[...] = dq[...].T
                others()
            elif i == 1:
                ours()
            elif i == 2:
                lax.fori_loop(0, pieces, o_to, 0)
                ga[...] = jnp.zeros_like(ga)
                for other in range(plan.devices):
                    part = slice(other * own, (other + 1) * own)
                    ga[other, 2:3, :own] = gat[:, part]
                    ga[other, 3:4, :own] = gff[:, part]
                for piece in range(pieces):
                    part = slice(piece * own, (piece + 1) * own)
                    ga[plan.head(index) * pieces + piece, 0:2, :own] = gh[0:2, part]
                lax.fori_loop(1, plan.devices, ga_to, 0)
                pltpu.make_async_copy(ga.at[me], ga_out.at[me], ga_r).start()
            elif i == 3:
                collect()

        def write(here, value):
            ig[here, :] = bf[here, :] + value

        begin_u(1)
        begin_u(0)
        loads.wait(0, 1)
        scatter_steps(plan, dp, seq, index, [(dq, 0, wq)], True, write, bufs, sems, meanwhile)
        wait_bytes(got_o, o_r)
        wait_bytes(got_q, q_r)
        for part in range(3):
            for member in range(plan.size):
                total = got_q[member, :, part * HEAD : (part + 1) * HEAD].astype(F32)
                w_grad[:, pl.ds(part * width + plan.head(member) * HEAD, HEAD)] = total
        total = got_o[0].astype(F32)
        for other in range(1, plan.groups):
            total = total + got_o[other].astype(F32)
        w_grad[:, pl.ds(3 * width, width)] = total
        finish_u()
        wait_bytes(ga_out, ga_r)
        wait_bytes(ga_out.at[pl.ds(0, plan.devices - 1)], ga_s)
        wait_bytes(got_q.at[pl.ds(0, plan.size - 1)], q_s)
        wait_bytes(gq_far, x_s)

        def sent_o(piece, carry):
            @pl.when(plan.head(index) * pieces + piece != me)
            def _():
                wait_bytes(go.at[pl.ds(0, own)], o_s)

            return carry

        lax.fori_loop(0, pieces, sent_o, 0)

    shapes = (
        ((rows, width), F32),
        ((own, 4 * width), F32),
        ((own, inner), BF),
        ((plan.devices, 8, 128), F32),
    )
    return pl.pallas_call(
        kernel,
        out_shape=[jax.ShapeDtypeStruct(*shape) for shape in shapes],
        in_specs=[ANY] * 5 + [VM] * 4,
        out_specs=[VM, VM, ANY, VM],
        scratch_shapes=[like(value) for value in (dqkv, w_qkv, x_all)]
        + [DMA((3,))]
        + scatter_scratch(rows, width)
        + [
            pltpu.VMEM((3 * HEAD, tokens), BF),
            pltpu.VMEM((tiles, tile, 3 * HEAD), BF),
            pltpu.VMEM((plan.groups - 1, tiles, tile, 3 * HEAD), BF),
            pltpu.VMEM((plan.groups - 1, tiles, tile, 3 * HEAD), BF),
            pltpu.VMEM((plan.size, own, 3 * HEAD), BF),
            pltpu.VMEM((plan.groups, own, width), BF),
            pltpu.VMEM((plan.devices, 8, 128), F32),
        ]
        + [DMA] * 9
        + [DMA((plan.groups - 1, tiles))],
        compiler_params=pltpu.CompilerParams(
            collective_id=5, has_side_effects=True, vmem_limit_bytes=60 * 2**20
        ),
        cost_estimate=LIGHT,
        name="finish_backward",
    )(dqkv, w_qkv, x_all, g_up, g_out, g_head, g_attn, g_ffn, before)


def per_device(
    plan,
    hidden_in,
    segments,
    attn_weights,
    q_gain,
    k_gain,
    attn_gain,
    ffn_gain,
    gate_up_weights,
    down_weights,
    cotangent,
):
    x = hidden_in[0]
    rows, width = x.shape
    own = attn_weights.shape[0]
    inner = gate_up_weights.shape[1] // 2
    length = rows * plan.seq
    tokens = rows * plan.size
    groups = plan.groups
    dp, seq, index = plan.here()
    me = dp * plan.seq + seq
    direct = (inner // (groups * plan.size)) % 128 == 0
    blocks = groups if direct else 1

    across = [[plan.dp_of(high, low) for high in range(groups)] for low in range(plan.low)]

    def join_groups(value):
        return lax.all_gather(value, "dp", axis_index_groups=across, axis=0, tiled=True)

    def sum_groups(value):
        return lax.psum_scatter(
            value.astype(BF), "dp", axis_index_groups=across, scatter_dimension=0, tiled=True
        )

    x_all, w_qkv, gate_part, w_out, gains_all, docs = start_gather(
        plan,
        x,
        attn_weights,
        gate_up_weights,
        [q_gain, k_gain, attn_gain, ffn_gain],
        segments,
        blocks,
    )
    w_gate = join_groups(gate_part)
    positions = np.arange(length, dtype=np.float32)
    frequency = rope_base ** (-2.0 * np.arange(HEAD // 2, dtype=np.float32) / HEAD)
    angles = positions[:, None] * frequency.astype(np.float32)[None, :]
    cosine = jnp.asarray(np.concatenate([np.cos(angles)] * 2, axis=1), F32)
    sine = jnp.asarray(np.concatenate([-np.sin(angles), np.sin(angles)], axis=1), F32)

    up_part, q, k, row_sums_qk, q_low, k_low, v_low, mixed = attend_forward(
        plan,
        x_all,
        w_qkv,
        gate_up_weights,
        gains_all,
        docs,
        cosine,
        sine,
        blocks,
    )
    w_up = join_groups(up_part)
    down_weights, _ = lax.optimization_barrier((down_weights, up_part))
    if direct:
        w_down = join_groups(down_weights)
    else:
        w_all = lax.all_gather(down_weights, ("dp", "seq"), axis=0, tiled=True)
        each = inner // plan.size
        w_down = lax.dynamic_slice_in_dim(w_all, index * each, each, 0)
    branch, hidden, _, h_all = hidden_forward(plan, mixed, w_out, x, gains_all)
    branch, w_gate = lax.optimization_barrier((branch, w_gate))

    gate, up, act = ffn_forward(plan, h_all, w_gate, w_up)
    output, grad_down_in, grad_fg = output_norm(
        plan, act, w_down, hidden, cotangent[0], gains_all
    )

    gu_low, g_gate, g_up, g_down = ffn_backward(
        plan, grad_down_in, h_all, w_down, gate, up, act
    )
    g_gate = sum_groups(g_gate)
    g_up = sum_groups(g_up)
    if direct:
        grad_down = sum_groups(g_down).astype(F32)
    else:
        spread = jnp.zeros((inner, width), BF)
        spread = lax.dynamic_update_slice_in_dim(spread, g_down, index * g_down.shape[0], 0)
        grad_down = lax.psum_scatter(
            spread, ("dp", "seq"), scatter_dimension=0, tiled=True
        ).astype(F32)

    grad_hidden, grad_ag, grad_branch = hidden_backward(
        plan, gu_low, [w_gate, w_up], cotangent[0], branch, gains_all
    )
    dqkv, g_out, g_head, gate_rows = attend_backward(
        plan,
        grad_branch,
        w_out,
        q,
        k,
        row_sums_qk,
        q_low,
        k_low,
        v_low,
        mixed,
        gains_all,
        docs,
        cosine,
        sine,
        g_gate,
        blocks,
    )

    input_grad, grad_attn, up_rows, gain_rows = finish_backward(
        plan,
        dqkv,
        w_qkv,
        x_all,
        g_up,
        g_out,
        g_head,
        grad_ag,
        grad_fg,
        grad_hidden,
        blocks,
    )
    grad_gate_up = jnp.concatenate([gate_rows, up_rows], axis=1).astype(F32)
    gain_grads = jnp.sum(gain_rows, axis=0)[:4, :own]
    return (
        output[None],
        input_grad[None],
        grad_attn,
        grad_gate_up,
        grad_down,
        gain_grads[0],
        gain_grads[1],
        gain_grads[2],
        gain_grads[3],
    )


def solution(mesh):
    by_token = P("dp", "seq", None)
    by_row = P(("dp", "seq"), None)
    by_gain = P(("dp", "seq"))

    def run(hidden_in, segments, attn_weights, *rest):
        plan = Plan(mesh, hidden_in.shape[2] // HEAD)
        return jax.shard_map(
            functools.partial(per_device, plan),
            mesh=mesh,
            in_specs=(by_token, P("dp", "seq"), by_row)
            + (by_gain,) * 4
            + (by_row, by_row, by_token),
            out_specs=(by_token, by_token, by_row, by_row, by_row) + (by_gain,) * 4,
            check_vma=False,
        )(hidden_in, segments, attn_weights, *rest)

    return run
```

```python
import functools

import jax
import jax.numpy as jnp
import numpy as np
from jax import lax
from jax.experimental import pallas as pl
from jax.experimental.pallas import tpu as pltpu
from jax.sharding import PartitionSpec as P

HEAD = 128
epsilon = 1e-06
rope_base = 500000.0
MESH = pl.DeviceIdType.MESH
BF = jnp.bfloat16
F32 = jnp.float32
ANY = pl.BlockSpec(memory_space=pl.ANY)
VM = pl.BlockSpec(memory_space=pltpu.VMEM)
DMA = pltpu.SemaphoreType.DMA
LIGHT = pl.CostEstimate(flops=0, bytes_accessed=0, transcendentals=0)


class Plan:
    def __init__(self, mesh, heads):
        self.dp = mesh.shape["dp"]
        self.seq = mesh.shape["seq"]
        self.size = heads
        self.low = heads // self.seq
        self.groups = self.dp // self.low
        self.devices = self.dp * self.seq
        self.pieces = self.devices // heads
        self.chips = self.seq // 2
        self.by_chip = self.groups == 2 and self.size == self.dp * self.chips

    def group_of(self, dp):
        return dp % self.groups + (dp // self.groups) * (self.groups - 1 - 2 * (dp % self.groups))

    def dp_of(self, group, low):
        return low * self.groups + group + low * (self.groups - 1 - 2 * group)

    def flat(self, group, index):
        return self.dp_of(group, index // self.seq) * self.seq + index % self.seq

    def place(self, dp):
        return self.group_of(dp) * self.low + dp // self.groups

    def natural(self, rows):
        if self.low == 1:
            return [(0, 0, rows)]
        count = rows // self.dp
        return [(self.place(i) * count, i * count, count) for i in range(self.dp)]

    def here(self):
        dp = lax.axis_index("dp")
        seq = lax.axis_index("seq")
        return dp, seq, (dp // self.groups) * self.seq + seq

    def head(self, index):
        if self.by_chip:
            return self.dp_of(index % 2, index // self.seq) * self.chips + (index % self.seq) // 2
        return index

    def of_head(self, head):
        if self.by_chip:
            dp = head // self.chips
            low = dp // self.groups
            return low * self.seq + (head % self.chips) * 2 + self.group_of(dp)
        return head

    def in_group(self, group, index):
        return self.dp_of(group, index // self.seq), index % self.seq

    def member(self, dp, index):
        return self.in_group(self.group_of(dp), index)

    def across(self, dp, seq, bit):
        if bit < self.seq:
            return dp, flip(seq, bit)
        return 2 * self.groups - 1 - dp, seq


def flip(value, bit):
    return value + bit * (1 - 2 * ((value // bit) % 2))


def flips(value, mask):
    bit = 1
    while bit <= mask:
        if mask & bit:
            value = flip(value, bit)
        bit *= 2
    return value


def greet(devices):
    barrier = pltpu.get_barrier_semaphore()
    for device in devices:
        pl.semaphore_signal(barrier, inc=1, device_id=device, device_id_type=MESH)
    pl.semaphore_wait(barrier, len(devices))


def greet_all(plan, dp, seq):
    barrier = pltpu.get_barrier_semaphore()
    me = dp * plan.seq + seq

    def hello(step, carry):
        other = (me + step) % plan.devices
        pl.semaphore_signal(
            barrier, inc=1, device_id=(other // plan.seq, other % plan.seq), device_id_type=MESH
        )
        return carry

    lax.fori_loop(1, plan.devices, hello, 0)
    pl.semaphore_wait(barrier, plan.devices - 1)


def greet_group(plan, dp, index):
    barrier = pltpu.get_barrier_semaphore()

    def hello(step, carry):
        other = plan.member(dp, (index + step) % plan.size)
        pl.semaphore_signal(barrier, inc=1, device_id=other, device_id_type=MESH)
        return carry

    lax.fori_loop(1, plan.size, hello, 0)
    pl.semaphore_wait(barrier, plan.size - 1)


def send(src, dst, send_sem, recv_sem, device):
    copy = pltpu.make_async_remote_copy(
        src_ref=src,
        dst_ref=dst,
        send_sem=send_sem,
        recv_sem=recv_sem,
        device_id=device,
        device_id_type=MESH,
    )
    copy.start()
    return copy


def wait_bytes(ref, sem):
    pltpu.make_async_copy(ref, ref, sem).wait()


class Loads:
    def __init__(self, sources, buffers, sems):
        self.copies = [
            pltpu.make_async_copy(src, dst, sems.at[i])
            for i, (src, dst) in enumerate(zip(sources, buffers))
        ]
        for copy in self.copies:
            copy.start()

    def wait(self, *which):
        for i in which or range(len(self.copies)):
            self.copies[i].wait()


def like(value):
    return pltpu.VMEM(value.shape, value.dtype)


def halves(rows):
    return ((0, rows // 2), (rows // 2, rows - rows // 2))


ORDERS = ((2, 4), (4, 2))


def gather_steps(plan, x, out, dp, seq, index, sems):
    far_send, far_recv, near_send, near_recv, core_send, core_recv, local = sems
    rows = x.shape[0]
    parts = halves(rows)
    copies = []

    def place(mask, part=None):
        start, count = (0, rows) if part is None else parts[part]
        return out.at[pl.ds(pl.multiple_of(flips(index, mask) * rows + start, 16), count)]

    def push(src, dst, send_sem, recv_sem, bit):
        copies.append(send(src, dst, send_sem, recv_sem, plan.across(dp, seq, bit)))

    def near(mask, part, number, bit):
        push(place(mask, part), place(mask, part), near_send.at[number], near_recv.at[number], bit)

    def to_core(mask, part, number):
        push(place(mask, part), place(mask, part), core_send.at[number], core_recv.at[number], 1)

    def begin():
        pltpu.make_async_copy(x, out.at[pl.ds(index * rows, rows)], local).start()
        for part in range(2):
            start, count = parts[part]
            push(
                x.at[pl.ds(start, count)], place(0, part), far_send.at[part], far_recv.at[part], 8
            )
        for bit in (2, 4):
            push(x, place(0), near_send.at[bit // 4], near_recv.at[bit // 4], bit)
        push(x, place(0), core_send.at[0], core_recv.at[0], 1)

    def finish(use=None):
        def here(chip):
            if use is not None:
                use(chip)

        pltpu.make_async_copy(x, out.at[pl.ds(index * rows, rows)], local).wait()
        wait_bytes(place(1), core_recv.at[0])
        here(0)
        for bit, other in ORDERS:
            part = bit // 4
            wait_bytes(place(bit), near_recv.at[part])
            near(bit, part, 2 + part, other)
            to_core(bit, None, 1 + part)
        def from_far(part):
            wait_bytes(place(8, part), far_recv.at[part])
            for bit in (2, 4):
                near(8, part, 4 + 2 * part + bit // 4, bit)
            to_core(8, part, 5 + part)

        wait_bytes(place(3), core_recv.at[1])
        here(2)
        from_far(0)
        wait_bytes(place(5), core_recv.at[2])
        here(4)
        for part in range(2):
            wait_bytes(place(6, part), near_recv.at[2 + part])
            to_core(6, part, 3 + part)
        from_far(1)
        for part in range(2):
            wait_bytes(place(7, part), core_recv.at[3 + part])
        here(6)
        for part in range(2):
            wait_bytes(place(9, part), core_recv.at[5 + part])
        here(8)
        for part in range(2):
            for bit, other in ORDERS:
                wait_bytes(place(8 | bit, part), near_recv.at[4 + 2 * part + bit // 4])
                if part == bit // 4:
                    near(8 | bit, part, 8 + part, other)
                to_core(8 | bit, part, 7 + 2 * part + bit // 4)
        for bit in (2, 4):
            for part in range(2):
                wait_bytes(place(9 | bit, part), core_recv.at[7 + 2 * part + bit // 4])
            if bit == 2:
                here(10)
        for part in range(2):
            wait_bytes(place(14, part), near_recv.at[8 + part])
            to_core(14, part, 11 + part)
        here(12)
        for part in range(2):
            wait_bytes(place(15, part), core_recv.at[11 + part])
        here(14)
        for copy in copies:
            copy.wait_send()

    return begin, finish


GATHER_SEMS = (DMA((2,)), DMA((2,)), DMA((10,)), DMA((10,)), DMA((13,)), DMA((13,)), DMA)


def scatter_steps(plan, dp, seq, index, pairs, turned, write, bufs, sems, meanwhile=None):
    theirs, mine, got_core, got_first, got_second, got_far = bufs
    core_send, core_recv, send_sems, recv_sems, far_send, far_recv = sems
    rows, width = got_far.shape
    tile = 512
    piece = rows // (2 * CHUNKS)
    copies = []

    def compute(dst, plane, core, blocks):
        starts = [flips(index, core | 2 * m | 8 * plane) * rows for m in blocks]

        @pl.loop(0, width // tile)
        def _(j):
            columns = pl.ds(pl.multiple_of(j * tile, tile), tile)
            block = None
            for l_ref, offset, r_ref in pairs:
                depth = r_ref.shape[1] if turned else r_ref.shape[0]
                some = jnp.concatenate(
                    [
                        l_ref[pl.ds(pl.multiple_of(start, rows), rows), pl.ds(offset, depth)]
                        for start in starts
                    ],
                    axis=0,
                )
                if turned:
                    part = contract_last(some, r_ref[columns, :])
                else:
                    part = dot(some, r_ref[:, columns])
                block = part if block is None else block + part
            block = block.astype(BF)
            for i, m in enumerate(blocks):
                dst[plane, m, :, columns] = block[i * rows : (i + 1) * rows]

    def push(src, dst, send_sem, recv_sem, bit):
        copy = send(src, dst, send_sem, recv_sem, plan.across(dp, seq, bit))
        copies.append(copy)
        return copy

    def add(dst, src, count):
        @pl.loop(0, count // 16)
        def _(i):
            here = pl.ds(pl.multiple_of(i * 16, 16), 16)
            dst[here, :] = dst[here, :] + src[here, :]

    def to_core(plane, blocks):
        started = []
        for m in blocks:
            number = plane * 4 + m
            started.append(
                (
                    push(
                        theirs.at[plane, m],
                        got_core.at[plane, m],
                        core_send.at[number],
                        core_recv.at[number],
                        1,
                    ),
                    m,
                )
            )
        return started

    def add_core(plane, started):
        for copy, m in started:
            copy.wait_recv()
            add(mine.at[plane, m], got_core.at[plane, m], rows)

    def start_of(chunk, part):
        return (chunk * 2 + part) * piece

    def first(plane, chunk):
        started = []
        for part, (bit, other) in enumerate(ORDERS):
            here = pl.ds(start_of(chunk, part), piece)
            for k, keep in enumerate((other, 0)):
                number = (plane * CHUNKS + chunk) * 6 + part * 2 + k
                buffer = got_first.at[plane, chunk, part * 2 + k]
                copy = push(
                    mine.at[plane, (keep | bit) // 2, here],
                    buffer,
                    send_sems.at[number],
                    recv_sems.at[number],
                    bit,
                )
                started.append((copy, keep // 2, here, buffer))
        return started

    def second(plane, chunk):
        started = []
        for part, (bit, other) in enumerate(ORDERS):
            here = pl.ds(start_of(chunk, part), piece)
            number = (plane * CHUNKS + chunk) * 6 + 4 + part
            buffer = got_second.at[plane, chunk, part]
            copy = push(
                mine.at[plane, other // 2, here],
                buffer,
                send_sems.at[number],
                recv_sems.at[number],
                other,
            )
            started.append((copy, 0, here, buffer))
        return started

    def far(chunk):
        here = pl.ds(chunk * 2 * piece, 2 * piece)
        return push(
            mine.at[1, 0, here], got_far.at[here], far_send.at[chunk], far_recv.at[chunk], 8
        )

    def settle(plane, started):
        for copy, m, here, buffer in started:
            copy.wait_recv()
            add(mine.at[plane, m, here], buffer, piece)

    def hook(i):
        if meanwhile is not None:
            meanwhile(i)

    compute(theirs, 1, 1, (3, 1))
    core_a = to_core(1, (3, 1))
    compute(theirs, 1, 1, (2, 0))
    core_b = to_core(1, (2, 0))
    compute(mine, 1, 0, (3, 1, 2, 0))
    hook(0)
    add_core(1, core_a)
    add_core(1, core_b)
    one = [first(1, chunk) if chunk < 2 else None for chunk in range(CHUNKS)]
    compute(theirs, 0, 1, (3, 1, 2, 0))
    core = to_core(0, (3, 1, 2, 0))
    fars = []

    def advance(chunk):
        settle(1, one[chunk])
        one[chunk] = second(1, chunk)
        if chunk + 2 < CHUNKS:
            one[chunk + 2] = first(1, chunk + 2)

    def cross(chunk):
        settle(1, one[chunk])
        fars.append(far(chunk))

    advance(0)
    compute(mine, 0, 0, (3, 1, 2, 0))
    hook(1)
    advance(1)
    add_core(0, core)
    for chunk in range(2, CHUNKS):
        cross(chunk - 2)
        advance(chunk)
    zero = [first(0, chunk) for chunk in range(CHUNKS)]
    hook(2)
    for chunk in range(CHUNKS - 2, CHUNKS):
        cross(chunk)
    hook(3)
    for chunk in range(CHUNKS):
        settle(0, zero[chunk])
        zero[chunk] = second(0, chunk)
    hook(4)
    for chunk in range(CHUNKS):
        settle(0, zero[chunk])
        fars[chunk].wait_recv()

        @pl.loop(0, 2 * piece // 16)
        def _(i):
            here = pl.ds(pl.multiple_of(chunk * 2 * piece + i * 16, 16), 16)
            write(here, mine[0, 0, here, :].astype(F32) + got_far[here, :].astype(F32))

    for copy in copies:
        copy.wait_send()


CHUNKS = 4


def scatter_scratch(rows, width):
    block = (rows, width)
    piece = (rows // (2 * CHUNKS), width)
    return [
        pltpu.VMEM((2, 4) + block, BF),
        pltpu.VMEM((2, 4) + block, BF),
        pltpu.VMEM((2, 4) + block, BF),
        pltpu.VMEM((2, CHUNKS, 4) + piece, BF),
        pltpu.VMEM((2, CHUNKS, 2) + piece, BF),
        pltpu.VMEM(block, BF),
        DMA((8,)),
        DMA((8,)),
        DMA((12 * CHUNKS,)),
        DMA((12 * CHUNKS,)),
        DMA((CHUNKS,)),
        DMA((CHUNKS,)),
    ]


def scatter_call(
    plan,
    left,
    rights,
    turned,
    collective_id,
    name,
    gains,
    which,
    extras,
    outs,
    begin,
    write,
    gather=False,
    moves=None,
):
    rows = left.shape[0] // plan.size
    width = rights[0].shape[0] if turned else rights[0].shape[1]
    count = len(rights)
    depth = left.shape[1] // count
    moves = moves or [(0, 0, rights[0].shape[0])]

    def kernel(*refs):
        refs = list(refs)

        def take(number):
            taken = refs[:number]
            del refs[:number]
            return taken

        sources, (gains_ref,), more = take(1 + count), take(1), take(len(extras))
        results = take(len(outs))
        everyone = take(1) if gather else None
        held, (sem, gain_row) = take(1 + count), take(2)
        pieces = [(sources[0], held[0])] + [
            (src.at[pl.ds(first, rows)], dst.at[pl.ds(to, rows)])
            for src, dst in zip(sources[1:], held[1:])
            for first, to, rows in moves
        ]
        loads = Loads(*zip(*pieces), sem)
        own = width // plan.devices
        for device in range(plan.devices):
            gain_row[:, device * own : (device + 1) * own] = gains_ref[
                device, which : which + 1, :own
            ]
        more = [*more, gain_row]
        pairs = [(held[0], i * depth, held[1 + i]) for i in range(count)]
        dp, seq, index = plan.here()
        greet([plan.across(dp, seq, bit) for bit in (1, 2, 4, 8)])
        begin(results)
        loads.wait()

        def put(here, value):
            write(here, value, more, results)

        scatter_steps(plan, dp, seq, index, pairs, turned, put, refs[:6], refs[6:12])
        if gather:
            start, finish = gather_steps(
                plan, results[-1], everyone[0], dp, seq, index, refs[12:]
            )
            start()
            finish()

    shapes = [jax.ShapeDtypeStruct(*out) for out in outs]
    if gather:
        shapes.append(jax.ShapeDtypeStruct((plan.size * rows, width), outs[-1][1]))
    return pl.pallas_call(
        kernel,
        out_shape=shapes,
        in_specs=[ANY] * (1 + count) + [VM] * (1 + len(extras)),
        out_specs=[VM] * len(outs) + [ANY] * gather,
        scratch_shapes=[like(value) for value in (left, *rights)]
        + [DMA((1 + count * len(moves),)), pltpu.VMEM((1, width), F32)]
        + scatter_scratch(rows, width)
        + list(GATHER_SEMS) * gather,
        compiler_params=pltpu.CompilerParams(
            collective_id=collective_id, has_side_effects=True, vmem_limit_bytes=60 * 2**20
        ),
        cost_estimate=LIGHT,
        name=name,
    )(left, *rights, gains, *extras)


def rms(values):
    return lax.rsqrt(jnp.mean(values * values, axis=1, keepdims=True) + epsilon)


def rms_back(values, gain, grad):
    r = rms(values)
    scaled = grad * gain
    inner = jnp.mean(scaled * values, axis=1, keepdims=True)
    back = r * scaled - values * (r * r * r * inner)
    return back, jnp.sum(grad * values * r, axis=0, keepdims=True)


def hidden_forward(plan, mixed, w_out, x, gains):
    def write(here, value, extras, outs):
        x_ref, g = extras
        branch, hidden, low = outs
        branch[here, :] = value
        h = x_ref[here, :].astype(F32) + value * rms(value) * g[...]
        hidden[here, :] = h
        low[here, :] = h.astype(BF)

    outs = ((x.shape, F32), (x.shape, F32), (x.shape, BF))
    return scatter_call(
        plan,
        mixed,
        [w_out],
        False,
        2,
        "hidden_forward",
        gains,
        2,
        (x,),
        outs,
        lambda outs: None,
        write,
        gather=True,
    )


def output_norm(plan, act, w_down, hidden, grad_out, gains):
    def begin(outs):
        outs[2][...] = jnp.zeros_like(outs[2])

    def write(here, value, extras, outs):
        hidden_ref, dy, g = extras
        output, back, g_gain = outs
        output[here, :] = (hidden_ref[here, :] + value * rms(value) * g[...]).astype(BF)
        grad, part = rms_back(value, g[...], dy[here, :].astype(F32))
        back[here, :] = grad.astype(BF)
        g_gain[...] += part

    outs = ((hidden.shape, BF), (hidden.shape, BF), ((1, hidden.shape[1]), F32))
    return scatter_call(
        plan,
        act,
        [w_down],
        False,
        6,
        "output_norm",
        gains,
        3,
        (hidden, grad_out),
        outs,
        begin,
        write,
    )


def hidden_backward(plan, g_low, rights, grad_out, branch, gains):
    def begin(outs):
        outs[1][...] = jnp.zeros_like(outs[1])

    def write(here, value, extras, outs):
        dy, u, g = extras
        grad, g_gain, low = outs
        e = dy[here, :].astype(F32) + value
        grad[here, :] = e
        back, part = rms_back(u[here, :], g[...], e)
        low[here, :] = back.astype(BF)
        g_gain[...] += part

    outs = ((branch.shape, F32), ((1, branch.shape[1]), F32), (branch.shape, BF))
    return scatter_call(
        plan,
        g_low,
        rights,
        True,
        7,
        "hidden_backward",
        gains,
        2,
        (grad_out, branch),
        outs,
        begin,
        write,
        moves=plan.natural(rights[0].shape[0]),
    )


def half_columns(plan, inner, blocks, half):
    each = inner // blocks // plan.size

    def offset(block):
        if blocks > 1:
            return lambda member: half * inner + plan.flat(block, member) * each
        return lambda member: half * inner + member * each

    return [(offset(block), each, block * each) for block in range(blocks)]


def columns_out(plan, dp, index, w_ref, out_ref, table, send_sem, recv_sem):
    own = w_ref.shape[0]
    wide = out_ref.shape[1]
    rows = pl.ds(pl.multiple_of(index * own, own), own)

    def moves(other):
        for offset, each, place in table:
            yield (
                w_ref.at[:, pl.ds(pl.multiple_of(offset(other), 128), each)],
                out_ref.at[rows, pl.ds(place, each)],
            )

    def begin():
        def to(step, carry):
            other = (index + step) % plan.size
            for src, dst in moves(other):
                send(src, dst, send_sem, recv_sem, plan.member(dp, other))
            return carry

        lax.fori_loop(1, plan.size, to, 0)
        for src, dst in moves(index):
            pltpu.make_async_copy(src, dst, recv_sem).start()

    def finish():
        wait_bytes(out_ref, recv_sem)

        def sent(step, carry):
            wait_bytes(w_ref.at[:, pl.ds(0, wide)], send_sem)
            return carry

        lax.fori_loop(1, plan.size, sent, 0)

    return begin, finish


def columns_back(plan, dp, index, g_ref, out_ref, table, send_sem, recv_sem):
    own = g_ref.shape[0] // plan.size

    def moves(other):
        rows = pl.ds(pl.multiple_of(other * own, own), own)
        for offset, each, place in table:
            yield (
                g_ref.at[rows, pl.ds(place, each)],
                out_ref.at[:, pl.ds(pl.multiple_of(offset(index), 128), each)],
            )

    def begin(plane):
        first = flips(index, 8 * plane) // 8 * 8

        def to(step, carry):
            other = first + (index + step) % 8
            for src, dst in moves(other):
                send(src, dst, send_sem, recv_sem, plan.member(dp, other))
            return carry

        lax.fori_loop(1 - plane, 8, to, 0)
        if plane == 0:
            for src, dst in moves(index):
                pltpu.make_async_copy(src, dst, recv_sem).start()

    def finish():
        wait_bytes(g_ref, recv_sem)

        def sent(step, carry):
            wait_bytes(g_ref.at[pl.ds(0, own)], send_sem)
            return carry

        lax.fori_loop(1, plan.size, sent, 0)

    return begin, finish


def start_gather(plan, x, attn_w, gate_up_w, gains, segments, blocks):
    rows, width = x.shape
    own, both = gate_up_w.shape
    table = half_columns(plan, both // 2, blocks, 0)

    count = len(gains)

    def kernel(x_ref, w_ref, u_ref, s_ref, *refs):
        gain_refs, (xo, wo, uo, oo, go, do) = refs[:count], refs[count : count + 6]
        g_ref, d_ref = refs[count + 6 : count + 8]
        sems = refs[count + 8 :]
        gather_sems = sems[:7]
        w_send, w_recv, u_send, u_recv, o_send, o_recv, g_send, g_recv, d_send, d_recv = sems[7:17]
        far_send, far_recv = sems[17:]
        g_ref[...] = jnp.zeros_like(g_ref)
        for i, gain in enumerate(gain_refs):
            g_ref[i : i + 1, :own] = gain[...].astype(F32)
        d_ref[...] = jnp.broadcast_to(s_ref[...], d_ref.shape)
        dp, seq, index = plan.here()
        me = dp * plan.seq + seq
        greet_all(plan, dp, seq)
        begin, finish = gather_steps(plan, x_ref, xo, dp, seq, index, gather_sems)
        group = plan.group_of(dp)

        def columns(part, other):
            return pl.ds(pl.multiple_of(part * width + plan.head(other) * HEAD, HEAD), HEAD)

        def rows_of(member):
            return pl.ds(pl.multiple_of(plan.flat(group, member) * own, own), own)

        def w_to(step, carry):
            other = (index + step) % plan.size
            for part in range(3):
                send(
                    w_ref.at[:, columns(part, other)],
                    wo.at[rows_of(index), pl.ds(part * HEAD, HEAD)],
                    w_send,
                    w_recv.at[index],
                    plan.member(dp, other),
                )
            return carry

        lax.fori_loop(1, plan.size, w_to, 0)
        begin()
        for part in range(3):
            pltpu.make_async_copy(
                w_ref.at[:, columns(part, index)],
                wo.at[rows_of(index), pl.ds(part * HEAD, HEAD)],
                w_recv.at[index],
            ).start()

        def onward(step, carry):
            rows = wo.at[rows_of((index + plan.size - step) % plan.size)]
            wait_bytes(rows, w_recv.at[(index + plan.size - step) % plan.size])
            for away in range(1, plan.groups):
                to_group = (group + away) % plan.groups
                send(rows, rows, far_send, far_recv, plan.in_group(to_group, index))
            return carry

        lax.fori_loop(0, plan.size, onward, 0)
        feature = me * own
        keeper = plan.of_head(feature // HEAD)
        o_dst = oo.at[pl.ds(pl.multiple_of(feature % HEAD, own), own)]
        o_src = w_ref.at[:, pl.ds(3 * width, width)]

        def o_to(away, carry):
            to_group = (group + away) % plan.groups
            to_dp, to_seq = plan.in_group(to_group, keeper)
            same = to_dp * plan.seq + to_seq == me

            @pl.when(same)
            def _():
                pltpu.make_async_copy(o_src, o_dst, o_recv).start()

            @pl.when(jnp.logical_not(same))
            def _():
                send(o_src, o_dst, o_send, o_recv, (to_dp, to_seq))

            return carry

        lax.fori_loop(0, plan.groups, o_to, 0)
        begin_u, finish_u = columns_out(plan, dp, index, u_ref, uo, table, u_send, u_recv)
        begin_u()

        def g_to(step, carry):
            other = (me + step) % plan.devices
            send(g_ref, go.at[me], g_send, g_recv, (other // plan.seq, other % plan.seq))
            return carry

        lax.fori_loop(1, plan.devices, g_to, 0)
        pltpu.make_async_copy(g_ref, go.at[me], g_recv).start()

        def d_to(step, carry):
            send(d_ref, do.at[index], d_send, d_recv, plan.member(dp, (index + step) % plan.size))
            return carry

        lax.fori_loop(1, plan.size, d_to, 0)
        pltpu.make_async_copy(d_ref, do.at[index], d_recv).start()
        finish()
        finish_u()
        wait_bytes(go, g_recv)
        wait_bytes(do, d_recv)
        far = wo.at[pl.ds(0, (plan.groups - 1) * plan.size * own)]
        wait_bytes(far, far_recv)
        wait_bytes(far, far_send)

        def sent(step, carry):
            wait_bytes(g_ref, g_send)
            return carry

        lax.fori_loop(1, plan.devices, sent, 0)

        def sent_w(step, carry):
            wait_bytes(w_ref.at[:, pl.ds(0, 3 * HEAD)], w_send)
            return carry

        lax.fori_loop(1, plan.size, sent_w, 0)

        def sent_docs(step, carry):
            wait_bytes(d_ref, d_send)
            return carry

        lax.fori_loop(1, plan.size, sent_docs, 0)
        wait_bytes(oo, o_recv)

        def sent_o(away, carry):
            to_group = (group + away) % plan.groups
            to_dp, to_seq = plan.in_group(to_group, keeper)

            @pl.when(to_dp * plan.seq + to_seq != me)
            def _():
                wait_bytes(o_src, o_send)

            return carry

        lax.fori_loop(0, plan.groups, sent_o, 0)

    shapes = (
        ((plan.size * rows, width), BF),
        ((plan.devices * own, 3 * HEAD), BF),
        ((plan.size * own, both // 2 // plan.size), BF),
        ((HEAD, width), BF),
        ((plan.devices, 8, 128), F32),
        ((plan.size, 8, rows), jnp.int32),
    )
    return pl.pallas_call(
        kernel,
        out_shape=[jax.ShapeDtypeStruct(*shape) for shape in shapes],
        in_specs=[ANY] * 3 + [VM] * (1 + count),
        out_specs=[ANY] * 6,
        scratch_shapes=[pltpu.VMEM((8, 128), F32), pltpu.VMEM((8, rows), jnp.int32)]
        + list(GATHER_SEMS)
        + [DMA, DMA((plan.size,))]
        + [DMA] * 10,
        compiler_params=pltpu.CompilerParams(collective_id=0, has_side_effects=True),
        cost_estimate=LIGHT,
        name="start_gather",
    )(x, attn_w, gate_up_w, segments, *[gain.reshape(1, own) for gain in gains])


def dot(left, right):
    return jnp.dot(left, right, preferred_element_type=F32)


def contract_last(left, right):
    return lax.dot_general(left, right, (((1,), (1,)), ((), ())), preferred_element_type=F32)


def contract_first(left, right):
    return lax.dot_general(left, right, (((0,), (0,)), ((), ())), preferred_element_type=F32)


def chip_rows(index, chip, rows):
    return pl.multiple_of(flips(index, chip) // 2 * (2 * rows), 2 * rows)


def ffn_forward(plan, h_all, w_gate, w_up):
    tokens, width = h_all.shape
    units = w_gate.shape[1]
    moves = plan.natural(width)

    def kernel(h, wg_ref, wu_ref, gate, up, act, wg, wu, sem):
        @pl.when(pl.program_id(0) == 0)
        def _():
            pieces = [
                (src.at[pl.ds(first, rows)], dst.at[pl.ds(to, rows)])
                for src, dst in ((wg_ref, wg), (wu_ref, wu))
                for first, to, rows in moves
            ]
            Loads(*zip(*pieces), sem).wait()

        values = h[...]
        g = dot(values, wg[...])
        u = dot(values, wu[...])
        gate[...] = g.astype(BF)
        up[...] = u.astype(BF)
        act[...] = (g * jax.nn.sigmoid(g) * u).astype(BF)

    rows = 2 * STEP
    part = pl.BlockSpec((rows, units), lambda i: (i, 0))
    return pl.pallas_call(
        kernel,
        grid=(tokens // rows,),
        out_shape=[jax.ShapeDtypeStruct((tokens, units), BF)] * 3,
        in_specs=[pl.BlockSpec((rows, width), lambda i: (i, 0)), ANY, ANY],
        out_specs=[part] * 3,
        scratch_shapes=[like(w_gate), like(w_up), DMA((2 * len(moves),))],
        compiler_params=pltpu.CompilerParams(vmem_limit_bytes=60 * 2**20),
        cost_estimate=LIGHT,
        name="ffn_forward",
    )(h_all, w_gate, w_up)


def ffn_backward(plan, d, h_all, w_down, gate, up, act):
    rows, width = d.shape
    tokens = rows * plan.size
    units = gate.shape[1]
    at_dp = width // plan.dp
    tile = 256
    two = 2 * rows

    def kernel(d_ref, *refs):
        ins, refs = refs[:5], refs[5:]
        outs, (h_all, wd, gate, up, act) = refs[:4], refs[4:9]
        d_all, gu_turned, act_turned, gu_sum, down_sum, out, g_gate, g_up, g_down = refs[9:18]
        sems, load_sems, store_sems, out_sems = refs[18:25], refs[25], refs[26], refs[27]
        dp, seq, index = plan.here()
        loads = Loads(ins, (wd, gate, up, act, h_all), load_sems)
        greet([plan.across(dp, seq, bit) for bit in (1, 2, 4, 8)])
        begin, finish = gather_steps(plan, d_ref, d_all, dp, seq, index, sems)
        begin()
        stores = []
        pair = []

        def products(first, last):
            chips = [pl.ds(chip_rows(index, chip, rows), two) for chip in pair]

            @pl.loop(0, width // tile)
            def _(i):
                columns = pl.ds(pl.multiple_of(i * tile, tile), tile)
                block = dot(
                    gu_turned[...],
                    jnp.concatenate([h_all[chip, columns] for chip in chips], axis=0),
                )
                if not first:
                    block = gu_sum[:, columns] + block
                if last:
                    block = block.T.astype(BF)
                    row = i * tile
                    row = plan.place(row // at_dp) * at_dp + row % at_dp
                    to = pl.ds(pl.multiple_of(row, tile), tile)
                    g_gate[to, :] = block[:, :units]
                    g_up[to, :] = block[:, units:]
                else:
                    gu_sum[:, columns] = block

            @pl.loop(0, width // tile)
            def _(i):
                columns = pl.ds(pl.multiple_of(i * tile, tile), tile)
                block = dot(
                    act_turned[...],
                    jnp.concatenate([d_all[chip, columns] for chip in chips], axis=0),
                )
                if not first:
                    block = down_sum[:, columns] + block
                if last:
                    g_down[:, columns] = block.astype(BF)
                else:
                    down_sum[:, columns] = block

        def use(chip):
            if chip == 0:
                loads.wait()
            some = pl.ds(chip_rows(index, chip, rows), two)
            columns = pl.ds(len(pair) * two, two)
            grad = contract_last(d_all[some, :], wd[...])
            g = gate[some, :].astype(F32)
            u = up[some, :].astype(F32)
            sigma = jax.nn.sigmoid(g)
            grad_gate = (grad * u * sigma * (1.0 + g * (1.0 - sigma))).astype(BF)
            grad_up = (grad * (g * sigma)).astype(BF)
            out[some, pl.ds(0, units)] = grad_gate
            out[some, pl.ds(units, units)] = grad_up
            store = pltpu.make_async_copy(out.at[some], outs[0].at[some], store_sems.at[chip // 2])
            store.start()
            stores.append(store)
            gu_turned[pl.ds(0, units), columns] = grad_gate.T
            gu_turned[pl.ds(units, units), columns] = grad_up.T
            act_turned[:, columns] = act[some, :].T
            pair.append(chip)
            if len(pair) == 2:
                products(len(stores) == 2, len(stores) == 8)
                pair.clear()

        finish(use)
        for i, src in enumerate((g_gate, g_up, g_down)):
            store = pltpu.make_async_copy(src, outs[1 + i], out_sems.at[i])
            store.start()
            stores.append(store)
        for store in stores:
            store.wait()

    return pl.pallas_call(
        kernel,
        out_shape=[
            jax.ShapeDtypeStruct((tokens, 2 * units), BF),
            jax.ShapeDtypeStruct((width, units), BF),
            jax.ShapeDtypeStruct((width, units), BF),
            jax.ShapeDtypeStruct((units, width), BF),
        ],
        in_specs=[VM] + [ANY] * 5,
        out_specs=[ANY] * 4,
        scratch_shapes=[
            pltpu.VMEM(shape, BF)
            for shape in (h_all.shape, (units, width), gate.shape, up.shape, act.shape, h_all.shape)
        ]
        + [
            pltpu.VMEM((2 * units, 2 * two), BF),
            pltpu.VMEM((units, 2 * two), BF),
            pltpu.VMEM((2 * units, width), F32),
            pltpu.VMEM((units, width), F32),
            pltpu.VMEM((tokens, 2 * units), BF),
            pltpu.VMEM((width, units), BF),
            pltpu.VMEM((width, units), BF),
            pltpu.VMEM((units, width), BF),
        ]
        + list(GATHER_SEMS)
        + [DMA((5,)), DMA((8,)), DMA((3,))],
        compiler_params=pltpu.CompilerParams(
            collective_id=10, has_side_effects=True, vmem_limit_bytes=62 * 2**20
        ),
        cost_estimate=LIGHT,
        name="ffn_backward",
    )(d, w_down, gate, up, act, h_all)


def row_sums(values):
    ones = jnp.ones((8, values.shape[1]), F32)
    sums = lax.dot_general(
        ones,
        values,
        (((1,), (1,)), ((), ())),
        precision=lax.Precision.HIGHEST,
        preferred_element_type=F32,
    )
    return sums[:1]


def spread_sums(rows):
    ones = jnp.ones((rows.shape[0], HEAD), F32)
    return lax.dot_general(
        rows,
        ones,
        (((0,), (0,)), ((), ())),
        precision=lax.Precision.HIGHEST,
        preferred_element_type=F32,
    )


STEP = 256


def lay_out(docs_ref, row_ref):
    for i in range(docs_ref.shape[0]):
        rows = docs_ref.shape[2]
        row_ref[:, i * rows : (i + 1) * rows] = docs_ref[i, :1, :].astype(F32)


def my_gain(plan, gains_ref, which, head):
    own = HEAD // plan.pieces
    parts = [gains_ref[head * plan.pieces + i, which : which + 1, :own] for i in range(plan.pieces)]
    return jnp.concatenate(parts, axis=1)


def scores_of(q, k, q_docs, k_docs, start):
    scores = contract_last(q, k) * HEAD ** (-0.5)
    row = start + lax.broadcasted_iota(jnp.int32, scores.shape, 0)
    column = lax.broadcasted_iota(jnp.int32, scores.shape, 1)
    allowed = (column <= row) & (spread_sums(q_docs)[:, :1] == k_docs)
    scores = jnp.where(allowed, scores, -1e30)
    top = jnp.max(scores, axis=1, keepdims=True)
    weights = jnp.exp(scores - top)
    return weights / jnp.sum(weights, axis=1, keepdims=True)


def swap_sums(plan, dp, index, mine, held, s_sem, r_sem):
    def begin():
        def to(step, carry):
            send(mine, held.at[index], s_sem, r_sem, plan.member(dp, (index + step) % plan.size))
            return carry

        pltpu.make_async_copy(mine, held.at[index], r_sem).start()
        lax.fori_loop(1, plan.size, to, 0)

    def finish():
        wait_bytes(held, r_sem)
        wait_bytes(held.at[pl.ds(0, plan.size - 1)], s_sem)

    return begin, finish


def attend_forward(
    plan, x_all, w_qkv, gate_up_w, gains, docs, cosine, sine, blocks
):
    tokens, width = x_all.shape
    length = cosine.shape[0]
    own, both = gate_up_w.shape
    table = half_columns(plan, both // 2, blocks, 1)

    def kernel(x_ref, wq_ref, up, ga, do, cs_ref, sn_ref, uo, q, k, sums, ql, kl, vl, mixed, *rest):
        x, wq, cs, sn, sem = rest[:5]
        loads = Loads((wq_ref, cs_ref, sn_ref), (wq, cs, sn), sem)
        step_rows = [pl.ds(i * STEP, STEP) for i in range(tokens // STEP)]
        Loads(
            [x_ref.at[rows] for rows in step_rows], [x.at[rows] for rows in step_rows], rest[5]
        )
        tile_sem, rest = rest[5], rest[6:]
        gn, dr, stats, held, t_send, t_recv, u_send, u_recv = rest
        dp, seq, index = plan.here()
        greet_group(plan, dp, index)
        lay_out(do, dr)
        for which in range(2):
            gn[which : which + 1, :] = my_gain(plan, ga, which, plan.head(index))
        loads.wait()

        @pl.loop(0, tokens // STEP)
        def _(i):
            rows = pl.ds(pl.multiple_of(i * STEP, STEP), STEP)
            pltpu.make_async_copy(x_ref.at[rows], x.at[rows], tile_sem.at[i]).wait()
            block = dot(x[rows, :], wq[...])
            q[rows, :] = block[:, :HEAD]
            k[rows, :] = block[:, HEAD : 2 * HEAD]
            vl[rows, :] = block[:, 2 * HEAD :].astype(BF)
            stats[0, :, rows] = row_sums(block[:, :HEAD] * block[:, :HEAD])
            stats[1, :, rows] = row_sums(block[:, HEAD : 2 * HEAD] * block[:, HEAD : 2 * HEAD])

        begin, finish = swap_sums(plan, dp, index, stats, held, t_send, t_recv)
        begin()
        begin_u, finish_u = columns_out(plan, dp, index, up, uo, table, u_send, u_recv)
        begin_u()
        finish()
        for which in range(2):
            sums[which] = jnp.sum(held[:, which, 0, :], axis=0, keepdims=True)

        @pl.loop(0, tokens // STEP)
        def _(i):
            rows = pl.ds(pl.multiple_of(i * STEP, STEP), STEP)
            places = pl.ds(pl.multiple_of((i % (length // STEP)) * STEP, STEP), STEP)
            for which, raw, low in ((0, q, ql), (1, k, kl)):
                r = lax.rsqrt(spread_sums(sums[which, :, rows]) / width + epsilon)
                values = raw[rows, :] * r * gn[which : which + 1, :]
                turned = values * cs[places, :] + pltpu.roll(values, HEAD // 2, 1) * sn[places, :]
                low[rows, :] = turned.astype(BF)

        @pl.loop(0, tokens // length)
        def _(b):
            for j in range(length // STEP):
                start = pl.multiple_of(b * length + j * STEP, STEP)
                rows = pl.ds(start, STEP)
                keys = pl.ds(pl.multiple_of(b * length, length), (j + 1) * STEP)
                probs = scores_of(
                    ql[rows, :], kl[keys, :], dr[:, rows], dr[:, keys], j * STEP
                )
                mixed[rows, :] = dot(probs.astype(BF), vl[keys, :]).astype(BF)

        finish_u()

    per_head = (tokens, HEAD)
    shapes = (
        ((plan.size * own, both // 2 // plan.size), BF),
        (per_head, F32),
        (per_head, F32),
        ((2, 1, tokens), F32),
        (per_head, BF),
        (per_head, BF),
        (per_head, BF),
        (per_head, BF),
    )
    return pl.pallas_call(
        kernel,
        out_shape=[jax.ShapeDtypeStruct(*shape) for shape in shapes],
        in_specs=[ANY] * 3 + [VM] * 2 + [ANY] * 2,
        out_specs=[ANY] + [VM] * 7,
        scratch_shapes=[like(value) for value in (x_all, w_qkv, cosine, sine)]
        + [DMA((3,)), DMA((tokens // STEP,))]
        + [
            pltpu.VMEM((8, HEAD), F32),
            pltpu.VMEM((1, tokens), F32),
            pltpu.VMEM((2, 1, tokens), F32),
            pltpu.VMEM((plan.size, 2, 1, tokens), F32),
        ]
        + [DMA] * 4,
        compiler_params=pltpu.CompilerParams(
            collective_id=3, has_side_effects=True, vmem_limit_bytes=56 * 2**20
        ),
        cost_estimate=LIGHT,
        name="attend_forward",
    )(x_all, w_qkv, gate_up_w, gains, docs, cosine, sine)


def attend_backward(
    plan,
    b,
    w_out,
    q,
    k,
    sums,
    ql,
    kl,
    vl,
    mixed,
    gains,
    docs,
    cosine,
    sine,
    g_gate,
    blocks,
):
    rows_here, width = b.shape
    tokens = rows_here * plan.size
    own = g_gate.shape[0] // plan.size
    inner = g_gate.shape[1] * plan.size
    length = cosine.shape[0]
    scale = HEAD ** (-0.5)

    def kernel(*refs):
        b_ref, sums, ga, do, gg = refs[:5]
        wo, q, k, ql, kl, vl, mx, cs, sn = refs[30:39]
        loads = Loads(refs[5:14], refs[30:39], refs[39])
        dqkv, g_out, g_gain, gate_out = refs[14:18]
        ba, dq, dk, dv, gn, dr, stats, held, t_send, t_recv, gg_send, gg_recv = refs[18:30]
        dp, seq, index = plan.here()
        greet_group(plan, dp, index)
        begin_b, finish_b = gather_steps(plan, b_ref, ba, dp, seq, index, refs[40:])
        begin_b()
        lay_out(do, dr)
        for which in range(2):
            gn[which : which + 1, :] = my_gain(plan, ga, which, plan.head(index))
        begin_g, finish_g = columns_back(
            plan, dp, index, gg, gate_out, half_columns(plan, inner, blocks, 0), gg_send, gg_recv
        )
        dk[...] = jnp.zeros_like(dk)
        dv[...] = jnp.zeros_like(dv)

        def use(chip):
            if chip == 0:
                loads.wait()
            if chip == 8:
                begin_g(1)
            if chip == 10:
                begin_g(0)
            first = chip_rows(index, chip, rows_here)
            rows = pl.ds(first, STEP)
            start = first % length

            def block(count):
                keys = pl.ds(pl.multiple_of(first - start, STEP), count)
                grad = contract_last(ba[rows, :], wo[...]).astype(BF)
                probs = scores_of(ql[rows, :], kl[keys, :], dr[:, rows], dr[:, keys], start)
                grad_probs = contract_last(grad, vl[keys, :])
                delta = jnp.sum(probs * grad_probs, axis=1, keepdims=True)
                grad_scores = (probs * (grad_probs - delta)).astype(BF)
                dq[rows, :] = dot(grad_scores, kl[keys, :]) * scale
                dk[keys, :] += contract_first(grad_scores, ql[rows, :]) * scale
                dv[keys, :] += contract_first(probs.astype(BF), grad)

            @pl.when(start < length // 2)
            def _():
                block(length // 2)

            @pl.when(start >= length // 2)
            def _():
                block(length)

        finish_b(use)

        @pl.loop(0, tokens // STEP)
        def _(i):
            rows = pl.ds(pl.multiple_of(i * STEP, STEP), STEP)
            places = pl.ds(pl.multiple_of((i % (length // STEP)) * STEP, STEP), STEP)
            for which, raw, grad in ((0, q, dq), (1, k, dk)):
                values = grad[rows, :]
                turned = values * cs[places, :] - pltpu.roll(values, HEAD // 2, 1) * sn[places, :]
                grad[rows, :] = turned
                stats[which, :, rows] = row_sums(turned * gn[which : which + 1, :] * raw[rows, :])

        begin, finish = swap_sums(plan, dp, index, stats, held, t_send, t_recv)
        begin()
        turned_mixed = mx[...].T

        @pl.loop(0, width // 512)
        def _(i):
            columns = pl.ds(pl.multiple_of(i * 512, 512), 512)
            g_out[:, columns] = dot(turned_mixed, ba[:, columns]).astype(BF)

        g_gain[...] = jnp.zeros_like(g_gain)

        @pl.loop(0, tokens // STEP)
        def _(i):
            rows = pl.ds(pl.multiple_of(i * STEP, STEP), STEP)
            for which, raw, grad in ((0, q, dq), (1, k, dk)):
                r = lax.rsqrt(spread_sums(sums[which, :, rows]) / width + epsilon)
                u = raw[rows, :]
                e = grad[rows, :]
                g_gain[which : which + 1, :] += jnp.sum(e * u * r, axis=0, keepdims=True)
                grad[rows, :] = r * (gn[which : which + 1, :] * e)
                raw[rows, :] = u * (r * r * r) / width
            dqkv[rows, pl.ds(2 * HEAD, HEAD)] = dv[rows, :].astype(BF)

        finish()

        @pl.loop(0, tokens // STEP)
        def _(i):
            rows = pl.ds(pl.multiple_of(i * STEP, STEP), STEP)
            for which, raw, grad in ((0, q, dq), (1, k, dk)):
                back = grad[rows, :] - raw[rows, :] * spread_sums(held[:, which, 0, rows])
                dqkv[rows, pl.ds(which * HEAD, HEAD)] = back.astype(BF)

        finish_g()

    per_head = (tokens, HEAD)
    shapes = (
        ((tokens, 3 * HEAD), BF),
        ((HEAD, width), BF),
        ((8, HEAD), F32),
        ((own, inner), BF),
    )
    return pl.pallas_call(
        kernel,
        out_shape=[jax.ShapeDtypeStruct(*shape) for shape in shapes],
        in_specs=[VM] * 4 + [ANY] * 10,
        out_specs=[VM] * 3 + [ANY],
        scratch_shapes=[
            pltpu.VMEM((tokens, width), BF),
            pltpu.VMEM(per_head, F32),
            pltpu.VMEM(per_head, F32),
            pltpu.VMEM(per_head, F32),
            pltpu.VMEM((8, HEAD), F32),
            pltpu.VMEM((1, tokens), F32),
            pltpu.VMEM((2, 1, tokens), F32),
            pltpu.VMEM((plan.size, 2, 1, tokens), F32),
        ]
        + [DMA] * 4
        + [like(value) for value in (w_out, q, k, ql, kl, vl, mixed, cosine, sine)]
        + [DMA((9,))]
        + list(GATHER_SEMS),
        compiler_params=pltpu.CompilerParams(
            collective_id=4, has_side_effects=True, vmem_limit_bytes=56 * 2**20
        ),
        cost_estimate=LIGHT,
        name="attend_backward",
    )(b, sums, gains, docs, g_gate, w_out, q, k, ql, kl, vl, mixed, cosine, sine)


def finish_backward(
    plan, dqkv, w_qkv, x_all, g_up, g_out, g_head, g_attn, g_ffn, before, blocks
):
    tokens, width = x_all.shape
    own = width // plan.devices
    rows = tokens // plan.size
    inner = g_up.shape[1] * plan.size
    pieces = HEAD // own
    tile = 256
    at_dp = width // plan.dp
    per_dp = at_dp // tile
    tiles = width // plan.groups // tile

    def kernel(dq_ref, wq_ref, x_ref, gu, go, gh, gat, gff, bf, ig, w_grad, up_out, ga_out, *rest):
        (dq, wq, x), load_sem = rest[:3], rest[3]
        loads = Loads((dq_ref, wq_ref, x_ref), (dq, wq, x), load_sem)
        rest = rest[4:]
        bufs, sems = rest[:6], rest[6:12]
        turned, gq, gq_far, got_x, got_q, got_o, ga = rest[12:19]
        q_s, q_r, o_s, o_r, ga_s, ga_r, gu_s, gu_r, x_s, x_r = rest[19:]
        dp, seq, index = plan.here()
        me = dp * plan.seq + seq
        group = plan.group_of(dp)
        greet_all(plan, dp, seq)

        def device_of(flat):
            return flat // plan.seq, flat % plan.seq

        def o_to(piece, carry):
            other = plan.head(index) * pieces + piece
            src = go.at[pl.ds(pl.multiple_of(piece * own, own), own)]

            @pl.when(other == me)
            def _():
                pltpu.make_async_copy(src, got_o.at[group], o_r).start()

            @pl.when(other != me)
            def _():
                send(src, got_o.at[group], o_s, o_r, device_of(other))

            return carry

        def ga_to(step, carry):
            other = (me + step) % plan.devices
            send(ga.at[other], ga_out.at[me], ga_s, ga_r, device_of(other))
            return carry

        table = half_columns(plan, inner, blocks, 0)
        begin_u, finish_u = columns_back(plan, dp, index, gu, up_out, table, gu_s, gu_r)

        def product(of_group, u):
            row = plan.dp_of(of_group, u // per_dp) * at_dp + (u % per_dp) * tile
            block = dot(turned[...], x[:, pl.ds(pl.multiple_of(row, tile), tile)])
            return block.T.astype(BF)

        def others():
            for away in range(1, plan.groups):
                to_group = (group + away) % plan.groups

                @pl.loop(0, tiles)
                def _(u, away=away, to_group=to_group):
                    gq_far[away - 1, u] = product(to_group, u)
                    send(
                        gq_far.at[away - 1, u],
                        got_x.at[away - 1, u],
                        x_s,
                        x_r.at[away - 1, u],
                        plan.in_group(to_group, index),
                    )

        def ours():
            @pl.loop(0, tiles)
            def _(u):
                gq[u] = product(group, u)

        def collect():
            @pl.loop(0, tiles)
            def _(u):
                total = gq[u].astype(F32)
                for away in range(1, plan.groups):
                    wait_bytes(got_x.at[away - 1, u], x_r.at[away - 1, u])
                    total = total + got_x[away - 1, u].astype(F32)
                gq[u] = total.astype(BF)
                owner_dp = plan.dp_of(group, u // per_dp)
                for piece in range(tile // own):
                    owner_seq = (u % per_dp) * (tile // own) + piece
                    src = gq.at[u, pl.ds(piece * own, own)]
                    mine = owner_dp * plan.seq + owner_seq == me

                    @pl.when(mine)
                    def _(src=src):
                        pltpu.make_async_copy(src, got_q.at[index], q_r).start()

                    @pl.when(jnp.logical_not(mine))
                    def _(src=src, owner_seq=owner_seq):
                        send(src, got_q.at[index], q_s, q_r, (owner_dp, owner_seq))

        def meanwhile(i):
            if i == 0:
                loads.wait(2)
                turned[...] = dq[...].T
                others()
            elif i == 1:
                ours()
            elif i == 2:
                lax.fori_loop(0, pieces, o_to, 0)
                ga[...] = jnp.zeros_like(ga)
                for other in range(plan.devices):
                    part = slice(other * own, (other + 1) * own)
                    ga[other, 2:3, :own] = gat[:, part]
                    ga[other, 3:4, :own] = gff[:, part]
                for piece in range(pieces):
                    part = slice(piece * own, (piece + 1) * own)
                    ga[plan.head(index) * pieces + piece, 0:2, :own] = gh[0:2, part]
                lax.fori_loop(1, plan.devices, ga_to, 0)
                pltpu.make_async_copy(ga.at[me], ga_out.at[me], ga_r).start()
            elif i == 3:
                collect()

        def write(here, value):
            ig[here, :] = bf[here, :] + value

        begin_u(1)
        begin_u(0)
        loads.wait(0, 1)
        scatter_steps(plan, dp, seq, index, [(dq, 0, wq)], True, write, bufs, sems, meanwhile)
        wait_bytes(got_o, o_r)
        wait_bytes(got_q, q_r)
        for part in range(3):
            for member in range(plan.size):
                total = got_q[member, :, part * HEAD : (part + 1) * HEAD].astype(F32)
                w_grad[:, pl.ds(part * width + plan.head(member) * HEAD, HEAD)] = total
        total = got_o[0].astype(F32)
        for other in range(1, plan.groups):
            total = total + got_o[other].astype(F32)
        w_grad[:, pl.ds(3 * width, width)] = total
        finish_u()
        wait_bytes(ga_out, ga_r)
        wait_bytes(ga_out.at[pl.ds(0, plan.devices - 1)], ga_s)
        wait_bytes(got_q.at[pl.ds(0, plan.size - 1)], q_s)
        wait_bytes(gq_far, x_s)

        def sent_o(piece, carry):
            @pl.when(plan.head(index) * pieces + piece != me)
            def _():
                wait_bytes(go.at[pl.ds(0, own)], o_s)

            return carry

        lax.fori_loop(0, pieces, sent_o, 0)

    shapes = (
        ((rows, width), F32),
        ((own, 4 * width), F32),
        ((own, inner), BF),
        ((plan.devices, 8, 128), F32),
    )
    return pl.pallas_call(
        kernel,
        out_shape=[jax.ShapeDtypeStruct(*shape) for shape in shapes],
        in_specs=[ANY] * 5 + [VM] * 4,
        out_specs=[VM, VM, ANY, VM],
        scratch_shapes=[like(value) for value in (dqkv, w_qkv, x_all)]
        + [DMA((3,))]
        + scatter_scratch(rows, width)
        + [
            pltpu.VMEM((3 * HEAD, tokens), BF),
            pltpu.VMEM((tiles, tile, 3 * HEAD), BF),
            pltpu.VMEM((plan.groups - 1, tiles, tile, 3 * HEAD), BF),
            pltpu.VMEM((plan.groups - 1, tiles, tile, 3 * HEAD), BF),
            pltpu.VMEM((plan.size, own, 3 * HEAD), BF),
            pltpu.VMEM((plan.groups, own, width), BF),
            pltpu.VMEM((plan.devices, 8, 128), F32),
        ]
        + [DMA] * 9
        + [DMA((plan.groups - 1, tiles))],
        compiler_params=pltpu.CompilerParams(
            collective_id=5, has_side_effects=True, vmem_limit_bytes=60 * 2**20
        ),
        cost_estimate=LIGHT,
        name="finish_backward",
    )(dqkv, w_qkv, x_all, g_up, g_out, g_head, g_attn, g_ffn, before)


def per_device(
    plan,
    hidden_in,
    segments,
    attn_weights,
    q_gain,
    k_gain,
    attn_gain,
    ffn_gain,
    gate_up_weights,
    down_weights,
    cotangent,
):
    x = hidden_in[0]
    rows, width = x.shape
    own = attn_weights.shape[0]
    inner = gate_up_weights.shape[1] // 2
    length = rows * plan.seq
    tokens = rows * plan.size
    groups = plan.groups
    dp, seq, index = plan.here()
    me = dp * plan.seq + seq
    direct = (inner // (groups * plan.size)) % 128 == 0
    blocks = groups if direct else 1

    across = [[plan.dp_of(high, low) for high in range(groups)] for low in range(plan.low)]

    def join_groups(value):
        return lax.all_gather(value, "dp", axis_index_groups=across, axis=0, tiled=True)

    def sum_groups(value):
        return lax.psum_scatter(
            value.astype(BF), "dp", axis_index_groups=across, scatter_dimension=0, tiled=True
        )

    x_all, w_qkv, gate_part, w_out, gains_all, docs = start_gather(
        plan,
        x,
        attn_weights,
        gate_up_weights,
        [q_gain, k_gain, attn_gain, ffn_gain],
        segments,
        blocks,
    )
    w_gate = join_groups(gate_part)
    positions = np.arange(length, dtype=np.float32)
    frequency = rope_base ** (-2.0 * np.arange(HEAD // 2, dtype=np.float32) / HEAD)
    angles = positions[:, None] * frequency.astype(np.float32)[None, :]
    cosine = jnp.asarray(np.concatenate([np.cos(angles)] * 2, axis=1), F32)
    sine = jnp.asarray(np.concatenate([-np.sin(angles), np.sin(angles)], axis=1), F32)

    up_part, q, k, row_sums_qk, q_low, k_low, v_low, mixed = attend_forward(
        plan,
        x_all,
        w_qkv,
        gate_up_weights,
        gains_all,
        docs,
        cosine,
        sine,
        blocks,
    )
    w_up = join_groups(up_part)
    down_weights, _ = lax.optimization_barrier((down_weights, up_part))
    if direct:
        w_down = join_groups(down_weights)
    else:
        w_all = lax.all_gather(down_weights, ("dp", "seq"), axis=0, tiled=True)
        each = inner // plan.size
        w_down = lax.dynamic_slice_in_dim(w_all, index * each, each, 0)
    branch, hidden, _, h_all = hidden_forward(plan, mixed, w_out, x, gains_all)
    branch, w_gate = lax.optimization_barrier((branch, w_gate))

    gate, up, act = ffn_forward(plan, h_all, w_gate, w_up)
    output, grad_down_in, grad_fg = output_norm(
        plan, act, w_down, hidden, cotangent[0], gains_all
    )

    gu_low, g_gate, g_up, g_down = ffn_backward(
        plan, grad_down_in, h_all, w_down, gate, up, act
    )
    g_gate = sum_groups(g_gate)
    g_up = sum_groups(g_up)
    if direct:
        grad_down = sum_groups(g_down).astype(F32)
    else:
        spread = jnp.zeros((inner, width), BF)
        spread = lax.dynamic_update_slice_in_dim(spread, g_down, index * g_down.shape[0], 0)
        grad_down = lax.psum_scatter(
            spread, ("dp", "seq"), scatter_dimension=0, tiled=True
        ).astype(F32)

    grad_hidden, grad_ag, grad_branch = hidden_backward(
        plan, gu_low, [w_gate, w_up], cotangent[0], branch, gains_all
    )
    dqkv, g_out, g_head, gate_rows = attend_backward(
        plan,
        grad_branch,
        w_out,
        q,
        k,
        row_sums_qk,
        q_low,
        k_low,
        v_low,
        mixed,
        gains_all,
        docs,
        cosine,
        sine,
        g_gate,
        blocks,
    )

    input_grad, grad_attn, up_rows, gain_rows = finish_backward(
        plan,
        dqkv,
        w_qkv,
        x_all,
        g_up,
        g_out,
        g_head,
        grad_ag,
        grad_fg,
        grad_hidden,
        blocks,
    )
    grad_gate_up = jnp.concatenate([gate_rows, up_rows], axis=1).astype(F32)
    gain_grads = jnp.sum(gain_rows, axis=0)[:4, :own]
    return (
        output[None],
        input_grad[None],
        grad_attn,
        grad_gate_up,
        grad_down,
        gain_grads[0],
        gain_grads[1],
        gain_grads[2],
        gain_grads[3],
    )


def solution(mesh):
    by_token = P("dp", "seq", None)
    by_row = P(("dp", "seq"), None)
    by_gain = P(("dp", "seq"))

    def run(hidden_in, segments, attn_weights, *rest):
        plan = Plan(mesh, hidden_in.shape[2] // HEAD)
        return jax.shard_map(
            functools.partial(per_device, plan),
            mesh=mesh,
            in_specs=(by_token, P("dp", "seq"), by_row)
            + (by_gain,) * 4
            + (by_row, by_row, by_token),
            out_specs=(by_token, by_token, by_row, by_row, by_row) + (by_gain,) * 4,
            check_vma=False,
        )(hidden_in, segments, attn_weights, *rest)

    return run
```
